256 devices in a mesh: gy: 64 (over y, z, core), gz: 4 (over x).
Axes of the slice: x: 4, y: 4, z: 8, core: 2. Of those that a mesh axis runs over, the one named last changes fastest.
Arguments:
- velocity: float32 [3, 256, 64, 512], P(None, 'gy', 'gz'), may hold values from -24 to 24
- smag_coef: float32 [256, 64, 512], P('gy', 'gz'), may hold values from 0.3 to 3
- snap_code: int32 [128], replicated, may hold values from 0 to 191, as said below
Outputs:
- final_velocity: float32 [3, 256, 64, 512], P(None, 'gy', 'gz')
- pod_modes: float32 [112, 3, 64, 16, 128], P(None, None, 'gy', 'gz')
The draws below stay inside these ranges and needn't reach their ends.
Inputs may be any that keep to these rules, and one draw needn't show every extreme that they name: `snap_code`: the 128 entries are distinct.
All inputs are finite; a program needn't handle non-finite values.
Results may differ from the reference program's by a relative error of at most 0.0003.
Values sent between devices are 32-bit elements; how exact they have to be, the bound alone decides.
No kernel may reach another device: no remote copies, remote signals or barrier semaphores. Data moves between devices by JAX's collectives and lax.ppermute only.
A program may use at most 64 MiB of HBM per device.

```python
import math
import jax
import jax.numpy as jnp
from jax import lax

NX = 512
STEPS = 2
COLS = 128
RANK = 112
ITERS = 3
NY = 256
NZ = 64
ROWS = 393216


def draw_velocity(key, part):
    key = jax.random.fold_in(key, 11)
    key_y, key_z, key_base = jax.random.split(key, 3)
    plane_y = jax.random.uniform(key_y, (NY,), jnp.float32)
    plane_z = jax.random.uniform(key_z, (NZ,), jnp.float32)
    height = jnp.arange(NY).astype(jnp.float32) / NY
    scale_map = (3.0 ** height)[:, None] * 10.0 ** (0.4 * (plane_y[:, None] + plane_z[None, :])) / 4.0
    base = jax.random.truncated_normal(key_base, -5.0, 5.0, (3, NY, NZ, NX), jnp.float32)
    return (base * scale_map[None, :, :, None]).astype(jnp.float32)


def draw_snap_code(key, part):
    key = jax.random.fold_in(key, 23)
    key_pick, key_order = jax.random.split(key)
    total = (STEPS + 1) * 64
    middle = jax.random.permutation(key_pick, total - 2) + 1
    picked = jnp.concatenate([jnp.array([0, total - 1], jnp.int32), middle[:COLS - 2].astype(jnp.int32)])
    return jax.random.permutation(key_order, picked).astype(jnp.int32)


def levels(own_key, extent, cuts, low, largest):
    gain, own = 1.0, jax.random.fold_in(own_key, 6)
    for dim, parts in cuts:
        heights = jnp.exp(jax.random.uniform(jax.random.fold_in(own, dim), (parts,), jnp.float32, low / len(cuts), largest / len(cuts)))
        gain = gain * jnp.repeat(heights, extent[dim] // parts).reshape([-1 if axis == dim else 1 for axis in range(len(extent))])
    return gain


def setup_inputs(seed: int = 0) -> dict:
    key_of = jax.random.split(jax.random.key(seed), 4)
    velocity = draw_velocity(jax.random.fold_in(key_of[3], 71), 0)
    smag_coef = jnp.clip(jnp.exp(math.log(3.0) - 2.3025851 * jax.random.uniform(key_of[1], (NY, NZ, NX), jnp.float32) ** levels(key_of[1], (NY, NZ, NX), ((0, 64), (1, 4)), -0.2, 0.2)), 0.3, 3.0)
    snap_code = draw_snap_code(jax.random.fold_in(key_of[3], 71), 0)
    return {"velocity": velocity, "smag_coef": smag_coef, "snap_code": snap_code}


nu_limit = 0.125
ridge = 1.0
highest = lax.Precision.HIGHEST

def extend(field_data, rim_width, edge_copy):
    leading = field_data.ndim - 3
    wall_pad = [(0, 0)] * leading + [(rim_width, rim_width), (0, 0), (0, 0)]
    if edge_copy:
        walled = jnp.pad(field_data, wall_pad, mode='edge')
    else:
        walled = jnp.pad(field_data, wall_pad)
    side_pad = [(0, 0)] * leading + [(0, 0), (rim_width, rim_width), (rim_width, rim_width)]
    return jnp.pad(walled, side_pad, mode='wrap')

def advance(velocity_ext, coefficient):
    grad_y = (velocity_ext[:, 2:, 1:-1, 1:-1] - velocity_ext[:, :-2, 1:-1, 1:-1]) * 0.5
    grad_z = (velocity_ext[:, 1:-1, 2:, 1:-1] - velocity_ext[:, 1:-1, :-2, 1:-1]) * 0.5
    grad_x = (velocity_ext[:, 1:-1, 1:-1, 2:] - velocity_ext[:, 1:-1, 1:-1, :-2]) * 0.5
    grads = [[grad_x[c], grad_y[c], grad_z[c]] for c in range(3)]
    strain = jnp.zeros_like(grad_x[0])
    for c in range(3):
        for d in range(3):
            strain = strain + 0.5 * (grads[c][d] + grads[d][c]) ** 2
    strain_rate = coefficient[1:-1, 1:-1, 1:-1] * jnp.sqrt(strain)
    viscosity = nu_limit * strain_rate / (1.0 + strain_rate)
    inner_field = velocity_ext[:, 1:-1, 1:-1, 1:-1]
    centre = inner_field[:, 1:-1, 1:-1, 1:-1]
    visc_mid = viscosity[1:-1, 1:-1, 1:-1]
    inside = slice(1, -1)
    ahead = slice(2, None)
    behind = slice(None, -2)
    shifts = [(ahead, inside, inside), (behind, inside, inside), (inside, ahead, inside), (inside, behind, inside), (inside, inside, ahead), (inside, inside, behind)]
    result = centre
    for neighbour in shifts:
        face_visc = 0.5 * (visc_mid + viscosity[neighbour])
        result = result + face_visc * (inner_field[(slice(None),) + neighbour] - centre)
    return result

def decimate(field_data):
    size_y, size_z, size_x = (field_data.shape[1], field_data.shape[2], field_data.shape[3])
    blocks = field_data.reshape(3, size_y // 4, 4, size_z // 4, 4, size_x // 4, 4)
    return blocks.transpose(2, 4, 6, 0, 1, 3, 5).reshape(64, -1)

def orthonormal_basis(gram_matrix):
    basis_vectors = jnp.eye(gram_matrix.shape[0], RANK, dtype=jnp.float32)
    for sweep in range(ITERS):
        product = jnp.dot(gram_matrix, basis_vectors, precision=highest)
        inner_gram = jnp.dot(product.T, product, precision=highest)
        lower_factor = jnp.linalg.cholesky(inner_gram)
        basis_vectors = jax.scipy.linalg.solve_triangular(lower_factor, product.T, lower=True).T
    return basis_vectors

def reference(velocity, smag_coef, snap_code):
    coef_ext = extend(smag_coef, 2, True)
    state_one = advance(extend(velocity, 2, False), coef_ext)
    state_two = advance(extend(state_one, 2, False), coef_ext)
    decimated = jnp.concatenate([decimate(velocity), decimate(state_one), decimate(state_two)], axis=0)
    snapshots = jnp.take(decimated, snap_code.astype(jnp.int32), axis=0)
    gram_matrix = jnp.dot(snapshots, snapshots.T, precision=highest) / ROWS
    gram_matrix = gram_matrix + ridge * jnp.eye(gram_matrix.shape[0], dtype=jnp.float32)
    basis_vectors = orthonormal_basis(gram_matrix)
    pod_modes = jnp.dot(basis_vectors.T, snapshots, precision=highest)
    return (state_two, pod_modes.reshape(RANK, 3, NY // 4, NZ // 4, NX // 4))
```

```python
import jax
import jax.numpy as jnp
from jax import lax
from jax.sharding import PartitionSpec as P

RANK = 112
ITERS = 3


nu_limit = 0.125
ridge = 1.0
highest = lax.Precision.HIGHEST


def with_halo(cells, sides, width):
    for axis, dim in sides:
        count = lax.axis_size(axis)
        head = lax.slice_in_dim(cells, 0, width, axis=dim)
        tail = lax.slice_in_dim(cells, cells.shape[dim] - width, cells.shape[dim], axis=dim)
        cells = jnp.concatenate(
            [
                lax.ppermute(tail, axis, [(i, (i + 1) % count) for i in range(count)]),
                cells,
                lax.ppermute(head, axis, [((i + 1) % count, i) for i in range(count)]),
            ],
            axis=dim,
        )
    return cells


def advance(velocity_ext, coefficient):
    grad_y = (velocity_ext[:, 2:, 1:-1, 1:-1] - velocity_ext[:, :-2, 1:-1, 1:-1]) * 0.5
    grad_z = (velocity_ext[:, 1:-1, 2:, 1:-1] - velocity_ext[:, 1:-1, :-2, 1:-1]) * 0.5
    grad_x = (velocity_ext[:, 1:-1, 1:-1, 2:] - velocity_ext[:, 1:-1, 1:-1, :-2]) * 0.5
    grads = [[grad_x[c], grad_y[c], grad_z[c]] for c in range(3)]
    strain = jnp.zeros_like(grad_x[0])
    for c in range(3):
        for d in range(3):
            strain = strain + 0.5 * (grads[c][d] + grads[d][c]) ** 2
    strain_rate = coefficient[1:-1, 1:-1, 1:-1] * jnp.sqrt(strain)
    viscosity = nu_limit * strain_rate / (1.0 + strain_rate)
    inner_field = velocity_ext[:, 1:-1, 1:-1, 1:-1]
    centre = inner_field[:, 1:-1, 1:-1, 1:-1]
    visc_mid = viscosity[1:-1, 1:-1, 1:-1]
    inside = slice(1, -1)
    ahead = slice(2, None)
    behind = slice(None, -2)
    shifts = [
        (ahead, inside, inside),
        (behind, inside, inside),
        (inside, ahead, inside),
        (inside, behind, inside),
        (inside, inside, ahead),
        (inside, inside, behind),
    ]
    result = centre
    for neighbour in shifts:
        face_visc = 0.5 * (visc_mid + viscosity[neighbour])
        result = result + face_visc * (inner_field[(slice(None),) + neighbour] - centre)
    return result


def wall_masks(margin, rows_y):
    global_row = lax.axis_index("gy") * rows_y + jnp.arange(rows_y + 2 * margin) - margin
    return (global_row < 0, global_row >= rows_y * lax.axis_size("gy"))


def zero_walls(field_data, margin, rows_y):
    below, above = wall_masks(margin, rows_y)
    outside = jnp.logical_or(below, above)
    return jnp.where(outside[None, :, None, None], jnp.float32(0.0), field_data)


def edge_walls(coefficient, margin, rows_y):
    below, above = wall_masks(margin, rows_y)
    first_row = coefficient[margin][None]
    last_row = coefficient[margin + rows_y - 1][None]
    coefficient = jnp.where(below[:, None, None], first_row, coefficient)
    return jnp.where(above[:, None, None], last_row, coefficient)


def wrap_x(field_data, margin):
    return jnp.concatenate(
        [field_data[..., -margin:], field_data, field_data[..., :margin]], axis=-1
    )


def decimate(field_data):
    size_y, size_z, size_x = (field_data.shape[1], field_data.shape[2], field_data.shape[3])
    cell = jnp.arange(size_x, dtype=jnp.int32)
    place = (cell % 4) * (size_x // 4) + cell // 4
    sorting = (place[:, None] == cell[None, :]).astype(jnp.float32)
    in_order = jnp.dot(field_data.reshape(-1, size_x), sorting, precision=highest)
    blocks = in_order.reshape(3, size_y // 4, 4, size_z // 4, 4, 4, size_x // 4)
    return blocks.transpose(2, 4, 5, 0, 1, 3, 6).reshape(64, -1)


def orthonormal_basis(gram_matrix):
    basis_vectors = jnp.eye(gram_matrix.shape[0], RANK, dtype=jnp.float32)
    for sweep in range(ITERS):
        product = jnp.dot(gram_matrix, basis_vectors, precision=highest)
        inner_gram = jnp.dot(product.T, product, precision=highest)
        lower_factor = jnp.linalg.cholesky(inner_gram)
        basis_vectors = jax.scipy.linalg.solve_triangular(lower_factor, product.T, lower=True).T
    return basis_vectors


def device_sum(part):
    steps = [
        ("gz", lambda i: i ^ 1),
        ("gz", lambda i: 3 - i),
        ("gy", lambda i: i ^ 1),
        ("gy", lambda i: i ^ 2),
        ("gy", lambda i: i ^ 6),
        ("gy", lambda i: i ^ 14),
        ("gy", lambda i: i ^ 16),
        ("gy", lambda i: i ^ 48),
    ]
    for axis, partner in steps:
        count = lax.axis_size(axis)
        part = part + lax.ppermute(part, axis, [(i, partner(i)) for i in range(count)])
    return part


def local(velocity, smag_coef, snap_code):
    rows_y = velocity.shape[1]
    stacked = jnp.concatenate([velocity, smag_coef[None]], axis=0)
    padded = with_halo(stacked, (("gy", 1), ("gz", 2)), 2)
    velocity_ext = wrap_x(zero_walls(padded[:3], 2, rows_y), 2)
    coefficient = wrap_x(edge_walls(padded[3], 2, rows_y), 2)
    state_one = advance(velocity_ext, coefficient)
    second = with_halo(state_one, (("gy", 1), ("gz", 2)), 2)
    state_two = advance(wrap_x(zero_walls(second, 2, rows_y), 2), coefficient)
    selector = (snap_code[:, None] == jnp.arange(192, dtype=jnp.int32)[None, :]).astype(jnp.float32)
    all_rows = jnp.concatenate(
        [decimate(velocity), decimate(state_one), decimate(state_two)], axis=0
    )
    snapshots = jnp.dot(selector, all_rows, precision=highest)
    gram_total = device_sum(jnp.dot(snapshots, snapshots.T, precision=highest))
    rows_all = snapshots.shape[1] * lax.axis_size("gy") * lax.axis_size("gz")
    gram_matrix = gram_total / rows_all + ridge * jnp.eye(gram_total.shape[0], dtype=jnp.float32)
    basis_vectors = orthonormal_basis(gram_matrix)
    pod_modes = jnp.dot(basis_vectors.T, snapshots, precision=highest)
    shaped = pod_modes.reshape(
        basis_vectors.shape[1], 3, rows_y // 4, velocity.shape[2] // 4, velocity.shape[3] // 4
    )
    return (state_two, shaped)


def solution(mesh):
    placed = (P(None, "gy", "gz", None), P("gy", "gz", None), P())
    return jax.shard_map(
        local,
        mesh=mesh,
        in_specs=placed,
        out_specs=(P(None, "gy", "gz", None), P(None, None, "gy", "gz", None)),
        check_vma=False,
    )
```

```python
import functools

import jax
import jax.numpy as jnp
from jax import lax
from jax.experimental import pallas as pl
from jax.experimental.pallas import tpu as pltpu
from jax.sharding import PartitionSpec as P

RANK = 112
ITERS = 3
PANEL = 8


nu_limit = 0.125
ridge = 1.0
highest = lax.Precision.HIGHEST


def with_halo(cells, sides, width):
    for axis, dim in sides:
        count = lax.axis_size(axis)
        head = lax.slice_in_dim(cells, 0, width, axis=dim)
        tail = lax.slice_in_dim(cells, cells.shape[dim] - width, cells.shape[dim], axis=dim)
        cells = jnp.concatenate(
            [
                lax.ppermute(tail, axis, [(i, (i + 1) % count) for i in range(count)]),
                cells,
                lax.ppermute(head, axis, [((i + 1) % count, i) for i in range(count)]),
            ],
            axis=dim,
        )
    return cells


def advance(velocity_ext, coefficient):
    grad_y = (velocity_ext[:, 2:, 1:-1, 1:-1] - velocity_ext[:, :-2, 1:-1, 1:-1]) * 0.5
    grad_z = (velocity_ext[:, 1:-1, 2:, 1:-1] - velocity_ext[:, 1:-1, :-2, 1:-1]) * 0.5
    grad_x = (velocity_ext[:, 1:-1, 1:-1, 2:] - velocity_ext[:, 1:-1, 1:-1, :-2]) * 0.5
    grads = [[grad_x[c], grad_y[c], grad_z[c]] for c in range(3)]
    strain = jnp.zeros_like(grad_x[0])
    for c in range(3):
        for d in range(3):
            strain = strain + 0.5 * (grads[c][d] + grads[d][c]) ** 2
    strain_rate = coefficient[1:-1, 1:-1, 1:-1] * jnp.sqrt(strain)
    viscosity = nu_limit * strain_rate / (1.0 + strain_rate)
    inner_field = velocity_ext[:, 1:-1, 1:-1, 1:-1]
    centre = inner_field[:, 1:-1, 1:-1, 1:-1]
    visc_mid = viscosity[1:-1, 1:-1, 1:-1]
    inside = slice(1, -1)
    ahead = slice(2, None)
    behind = slice(None, -2)
    shifts = [
        (ahead, inside, inside),
        (behind, inside, inside),
        (inside, ahead, inside),
        (inside, behind, inside),
        (inside, inside, ahead),
        (inside, inside, behind),
    ]
    result = centre
    for neighbour in shifts:
        face_visc = 0.5 * (visc_mid + viscosity[neighbour])
        result = result + face_visc * (inner_field[(slice(None),) + neighbour] - centre)
    return result


def wall_masks(margin, rows_y):
    global_row = lax.axis_index("gy") * rows_y + jnp.arange(rows_y + 2 * margin) - margin
    return (global_row < 0, global_row >= rows_y * lax.axis_size("gy"))


def zero_walls(field_data, margin, rows_y):
    below, above = wall_masks(margin, rows_y)
    outside = jnp.logical_or(below, above)
    return jnp.where(outside[None, :, None, None], jnp.float32(0.0), field_data)


def edge_walls(coefficient, margin, rows_y):
    below, above = wall_masks(margin, rows_y)
    first_row = coefficient[margin][None]
    last_row = coefficient[margin + rows_y - 1][None]
    coefficient = jnp.where(below[:, None, None], first_row, coefficient)
    return jnp.where(above[:, None, None], last_row, coefficient)


def wrap_x(field_data, margin):
    return jnp.concatenate(
        [field_data[..., -margin:], field_data, field_data[..., :margin]], axis=-1
    )


def decimate(field_data):
    size_y, size_z, size_x = (field_data.shape[1], field_data.shape[2], field_data.shape[3])
    cell = jnp.arange(size_x, dtype=jnp.int32)
    place = (cell % 4) * (size_x // 4) + cell // 4
    sorting = (place[:, None] == cell[None, :]).astype(jnp.float32)
    in_order = jnp.dot(field_data.reshape(-1, size_x), sorting, precision=highest)
    blocks = in_order.reshape(3, size_y // 4, 4, size_z // 4, 4, 4, size_x // 4)
    return blocks.transpose(2, 4, 5, 0, 1, 3, 6).reshape(64, -1)


def recip(value):
    guess = pl.reciprocal(value, approx=True)
    return guess * (2.0 - value * guess)


def spread(block, lane):
    return jnp.broadcast_to(block[:, lane : lane + 1], block.shape)


def repeat(block, row):
    return jnp.broadcast_to(block[row : row + 1, :], block.shape)


def orthonormal_rows(inner, wide):
    panels = RANK // PANEL
    row_id = lax.broadcasted_iota(jnp.int32, (PANEL, inner.shape[1]), 0)
    left = [inner[PANEL * k : PANEL * (k + 1), :] for k in range(panels)]
    right = [wide[PANEL * k : PANEL * (k + 1), :] for k in range(panels)]
    rows = []
    for k in range(panels):
        follows = k + 1 < panels
        own_left, own_right = left[k], right[k]
        own_cols = [spread(own_left, PANEL * k + j) for j in range(PANEL)]
        if follows:
            next_left, next_right = left[k + 1], right[k + 1]
            next_cols = [spread(next_left, PANEL * k + j) for j in range(PANEL)]
        pivots = jnp.ones_like(own_left)
        for j in range(PANEL):
            pivot = repeat(own_cols[j], j)
            inverse = recip(pivot)
            pivots = jnp.where(row_id == j, pivot, pivots)
            own_factor = own_cols[j] * inverse
            for m in range(j + 1, PANEL):
                own_cols[m] = own_cols[m] - own_factor * repeat(own_cols[j], m)
            row_left, row_right = repeat(own_left, j), repeat(own_right, j)
            if follows:
                next_factor = next_cols[j] * inverse
                for m in range(j + 1, PANEL):
                    next_cols[m] = next_cols[m] - next_factor * repeat(own_cols[j], m)
                next_left = next_left - next_factor * row_left
                next_right = next_right - next_factor * row_right
            below = jnp.where(row_id > j, own_factor, 0.0)
            own_left = own_left - below * row_left
            own_right = own_right - below * row_right
        if follows:
            left[k + 1], right[k + 1] = next_left, next_right
        if k + 2 < panels:
            scale = recip(pivots)
            update = lax.dot_general(
                own_left[:, PANEL * (k + 2) : RANK],
                jnp.concatenate([own_left * scale, own_right * scale], axis=1),
                (((0,), (0,)), ((), ())),
                precision=highest,
                preferred_element_type=jnp.float32,
            )
            width = own_left.shape[1]
            for m in range(k + 2, panels):
                start = PANEL * (m - k - 2)
                left[m] = left[m] - update[start : start + PANEL, :width]
                right[m] = right[m] - update[start : start + PANEL, width:]
        root = lax.rsqrt(pivots)
        rows.append(own_right * (root * (1.5 - 0.5 * pivots * root * root)))
    return jnp.concatenate(rows, axis=0)


def basis_kernel(total_ref, snap_ref, out_ref, basis_ref, *, rows_all):
    cols = total_ref.shape[0]
    row_id = lax.broadcasted_iota(jnp.int32, (cols, cols), 0)
    col_id = lax.broadcasted_iota(jnp.int32, (cols, cols), 1)
    gram_matrix = total_ref[...] / rows_all + jnp.where(row_id == col_id, jnp.float32(ridge), 0.0)

    def sweep(step, carry):
        @pl.when(step == 0)
        def _():
            basis_ref[...] = gram_matrix[:RANK, :]

        @pl.when(step > 0)
        def _():
            basis_ref[...] = jnp.dot(
                basis_ref[...], gram_matrix, precision=highest, preferred_element_type=jnp.float32
            )

        wide = basis_ref[...]
        full = jnp.concatenate([wide, jnp.zeros((cols - RANK, cols), jnp.float32)], axis=0)
        inner = lax.dot_general(
            wide, full, (((1,), (1,)), ((), ())), precision=highest, preferred_element_type=jnp.float32
        )
        basis_ref[...] = orthonormal_rows(inner, wide)
        return carry

    lax.fori_loop(0, ITERS, sweep, 0)
    basis = basis_ref[...]
    blocks = out_ref.shape[0] // RANK
    for block in range(blocks):
        out_ref[pl.ds(block, RANK, stride=blocks), :] = jnp.dot(
            basis,
            snap_ref[:, 128 * block : 128 * (block + 1)],
            precision=highest,
            preferred_element_type=jnp.float32,
        )


def project(gram_total, snapshots, rows_all):
    cols, rows = snapshots.shape
    return pl.pallas_call(
        functools.partial(basis_kernel, rows_all=rows_all),
        out_shape=jax.ShapeDtypeStruct((RANK * rows // 128, 128), jnp.float32),
        in_specs=[pl.BlockSpec(memory_space=pltpu.VMEM)] * 2,
        out_specs=pl.BlockSpec(memory_space=pltpu.VMEM),
        scratch_shapes=[pltpu.VMEM((RANK, cols), jnp.float32)],
        compiler_params=pltpu.CompilerParams(vmem_limit_bytes=16 * 2**20),
        name="basis",
    )(gram_total, snapshots)


def device_sum(part):
    steps = [
        ("gz", lambda i: i ^ 1),
        ("gz", lambda i: 3 - i),
        ("gy", lambda i: i ^ 1),
        ("gy", lambda i: i ^ 2),
        ("gy", lambda i: i ^ 6),
        ("gy", lambda i: i ^ 14),
        ("gy", lambda i: i ^ 16),
        ("gy", lambda i: i ^ 48),
    ]
    for axis, partner in steps:
        count = lax.axis_size(axis)
        part = part + lax.ppermute(part, axis, [(i, partner(i)) for i in range(count)])
    return part


def local(velocity, smag_coef, snap_code):
    rows_y = velocity.shape[1]
    stacked = jnp.concatenate([velocity, smag_coef[None]], axis=0)
    padded = with_halo(stacked, (("gy", 1), ("gz", 2)), 2)
    velocity_ext = wrap_x(zero_walls(padded[:3], 2, rows_y), 2)
    coefficient = wrap_x(edge_walls(padded[3], 2, rows_y), 2)
    state_one = advance(velocity_ext, coefficient)
    second = with_halo(state_one, (("gy", 1), ("gz", 2)), 2)
    state_two = advance(wrap_x(zero_walls(second, 2, rows_y), 2), coefficient)
    selector = (snap_code[:, None] == jnp.arange(192, dtype=jnp.int32)[None, :]).astype(jnp.float32)
    all_rows = jnp.concatenate(
        [decimate(velocity), decimate(state_one), decimate(state_two)], axis=0
    )
    snapshots = jnp.dot(selector, all_rows, precision=highest)
    gram_total = device_sum(jnp.dot(snapshots, snapshots.T, precision=highest))
    rows_all = snapshots.shape[1] * lax.axis_size("gy") * lax.axis_size("gz")
    pod_modes = project(gram_total, snapshots, rows_all)
    shaped = pod_modes.reshape(
        RANK, 3, rows_y // 4, velocity.shape[2] // 4, velocity.shape[3] // 4
    )
    return (state_two, shaped)


def solution(mesh):
    placed = (P(None, "gy", "gz", None), P("gy", "gz", None), P())
    return jax.shard_map(
        local,
        mesh=mesh,
        in_specs=placed,
        out_specs=(P(None, "gy", "gz", None), P(None, None, "gy", "gz", None)),
        check_vma=False,
    )
```

```python
import functools

import jax
import jax.numpy as jnp
from jax import lax
from jax.experimental import pallas as pl
from jax.experimental.pallas import tpu as pltpu
from jax.sharding import PartitionSpec as P

RANK = 112
ITERS = 3
PANEL = 8
LANES = 128
SLOT = 16


nu_limit = 0.125
ridge = 1.0
highest = lax.Precision.HIGHEST


def recip(value):
    guess = pl.reciprocal(value, approx=True)
    return guess * (2.0 - value * guess)


def spread(block, lane):
    return jnp.broadcast_to(block[:, lane : lane + 1], block.shape)


def repeat(block, row):
    return jnp.broadcast_to(block[row : row + 1, :], block.shape)


def orthonormal_rows(inner, wide):
    panels = RANK // PANEL
    row_id = lax.broadcasted_iota(jnp.int32, (PANEL, inner.shape[1]), 0)
    left = [inner[PANEL * k : PANEL * (k + 1), :] for k in range(panels)]
    right = [wide[PANEL * k : PANEL * (k + 1), :] for k in range(panels)]
    rows = []
    for k in range(panels):
        follows = k + 1 < panels
        own_left, own_right = left[k], right[k]
        own_cols = [spread(own_left, PANEL * k + j) for j in range(PANEL)]
        if follows:
            next_left, next_right = left[k + 1], right[k + 1]
            next_cols = [spread(next_left, PANEL * k + j) for j in range(PANEL)]
        pivots = jnp.ones_like(own_left)
        for j in range(PANEL):
            pivot = repeat(own_cols[j], j)
            inverse = recip(pivot)
            pivots = jnp.where(row_id == j, pivot, pivots)
            own_factor = own_cols[j] * inverse
            for m in range(j + 1, PANEL):
                own_cols[m] = own_cols[m] - own_factor * repeat(own_cols[j], m)
            row_left, row_right = repeat(own_left, j), repeat(own_right, j)
            if follows:
                next_factor = next_cols[j] * inverse
                for m in range(j + 1, PANEL):
                    next_cols[m] = next_cols[m] - next_factor * repeat(own_cols[j], m)
                next_left = next_left - next_factor * row_left
                next_right = next_right - next_factor * row_right
            below = jnp.where(row_id > j, own_factor, 0.0)
            own_left = own_left - below * row_left
            own_right = own_right - below * row_right
        if follows:
            left[k + 1], right[k + 1] = next_left, next_right
        if k + 2 < panels:
            scale = recip(pivots)
            update = lax.dot_general(
                own_left[:, PANEL * (k + 2) : RANK],
                jnp.concatenate([own_left * scale, own_right * scale], axis=1),
                (((0,), (0,)), ((), ())),
                precision=highest,
                preferred_element_type=jnp.float32,
            )
            width = own_left.shape[1]
            for m in range(k + 2, panels):
                start = PANEL * (m - k - 2)
                left[m] = left[m] - update[start : start + PANEL, :width]
                right[m] = right[m] - update[start : start + PANEL, width:]
        root = lax.rsqrt(pivots)
        rows.append(own_right * (root * (1.5 - 0.5 * pivots * root * root)))
    return jnp.concatenate(rows, axis=0)


def basis_kernel(total_ref, snap_ref, out_ref, basis_ref, *, rows_all):
    cols = total_ref.shape[0]
    row_id = lax.broadcasted_iota(jnp.int32, (cols, cols), 0)
    col_id = lax.broadcasted_iota(jnp.int32, (cols, cols), 1)
    gram_matrix = total_ref[...] / rows_all + jnp.where(row_id == col_id, jnp.float32(ridge), 0.0)

    def sweep(step, carry):
        @pl.when(step == 0)
        def _():
            basis_ref[...] = gram_matrix[:RANK, :]

        @pl.when(step > 0)
        def _():
            basis_ref[...] = jnp.dot(
                basis_ref[...], gram_matrix, precision=highest, preferred_element_type=jnp.float32
            )

        wide = basis_ref[...]
        full = jnp.concatenate([wide, jnp.zeros((cols - RANK, cols), jnp.float32)], axis=0)
        inner = lax.dot_general(
            wide, full, (((1,), (1,)), ((), ())), precision=highest, preferred_element_type=jnp.float32
        )
        basis_ref[...] = orthonormal_rows(inner, wide)
        return carry

    lax.fori_loop(0, ITERS, sweep, 0)
    basis = basis_ref[...]
    blocks, cols = out_ref.shape[0] // RANK, basis.shape[1]
    for block in range(blocks):
        out_ref[pl.ds(block, RANK, stride=blocks), :] = jnp.dot(
            basis,
            snap_ref[pl.ds(block, cols, stride=SLOT), :],
            precision=highest,
            preferred_element_type=jnp.float32,
        )


def project(gram_total, snapshots, rows_all):
    cols = gram_total.shape[0]
    return pl.pallas_call(
        functools.partial(basis_kernel, rows_all=rows_all),
        out_shape=jax.ShapeDtypeStruct((RANK * 12, LANES), jnp.float32),
        in_specs=[pl.BlockSpec(memory_space=pltpu.VMEM)] * 2,
        out_specs=pl.BlockSpec(memory_space=pltpu.VMEM),
        scratch_shapes=[pltpu.VMEM((RANK, cols), jnp.float32)],
        compiler_params=pltpu.CompilerParams(vmem_limit_bytes=16 * 2**20),
        name="basis",
    )(gram_total, snapshots)


def exact_dot(values, one_hot):
    high = values.astype(jnp.bfloat16)
    rest = values - high.astype(jnp.float32)
    middle = rest.astype(jnp.bfloat16)
    low = (rest - middle.astype(jnp.float32)).astype(jnp.bfloat16)
    dot = functools.partial(jnp.dot, preferred_element_type=jnp.float32)
    return (dot(low, one_hot) + dot(middle, one_hot)) + dot(high, one_hot)


def sorting(size, to_sorted):
    cell = lax.broadcasted_iota(jnp.int32, (size, size), 0 if to_sorted else 1)
    spot = lax.broadcasted_iota(jnp.int32, (size, size), 1 if to_sorted else 0)
    place = (cell & 3) * (size // 4) + (cell >> 2)
    return jnp.where(place == spot, 1.0, 0.0).astype(jnp.bfloat16)


def pack_kernel(velocity_ref, coef_ref, block_ref, low_ref, high_ref):
    rows_y, rows_z, size_x = coef_ref.shape
    rows = jnp.concatenate(
        [velocity_ref[c].reshape(-1, size_x) for c in range(3)] + [coef_ref[...].reshape(-1, size_x)]
    )
    done = exact_dot(rows, sorting(size_x, True))
    for c in range(4):
        for y in range(rows_y):
            start = (c * rows_y + y) * rows_z
            for o in range(4):
                plane = done[start : start + rows_z, LANES * o : LANES * (o + 1)]
                block_ref[c, y, o] = plane
                low_ref[c, y, 4 * o : 4 * o + 4, :] = plane[:4]
                high_ref[c, y, 4 * o : 4 * o + 4, :] = plane[rows_z - 4 :]


def pack(velocity, smag_coef):
    rows_y, rows_z, size_x = smag_coef.shape
    edge = jax.ShapeDtypeStruct((4, rows_y, 16, LANES), jnp.float32)
    return pl.pallas_call(
        pack_kernel,
        out_shape=(jax.ShapeDtypeStruct((4, rows_y, 4, rows_z, LANES), jnp.float32), edge, edge),
        in_specs=[pl.BlockSpec(memory_space=pltpu.VMEM)] * 2,
        out_specs=[pl.BlockSpec(memory_space=pltpu.VMEM)] * 3,
        compiler_params=pltpu.CompilerParams(vmem_limit_bytes=24 * 2**20),
        name="pack",
    )(velocity, smag_coef)


def around_x(ref, index, o):
    ahead = ref[(*index, o + 1)] if o < 3 else pltpu.roll(ref[(*index, 0)], LANES - 1, 1)
    behind = ref[(*index, o - 1)] if o > 0 else pltpu.roll(ref[(*index, 3)], 1, 1)
    return ahead, behind


def around_z(plane):
    return pltpu.roll(plane, plane.shape[0] - 1, 0), pltpu.roll(plane, 1, 0)


def half_viscosity(cells_ref, y, o, coefficient):
    jump = []
    for c in range(3):
        x_ahead, x_behind = around_x(cells_ref, (c, y), o)
        z_ahead, z_behind = around_z(cells_ref[c, y, o])
        jump.append(
            (x_ahead - x_behind, cells_ref[c, y + 1, o] - cells_ref[c, y - 1, o], z_ahead - z_behind)
        )
    total = jump[0][0] ** 2 + jump[1][1] ** 2 + jump[2][2] ** 2
    total = total + total
    for c, d in ((0, 1), (0, 2), (1, 2)):
        total = total + (jump[c][d] + jump[d][c]) ** 2
    rate = coefficient * (0.5 * jnp.sqrt(total))
    return (0.5 * nu_limit) * rate * recip(1.0 + rate)


def stepped(cells_ref, y, visc_ref, v, o):
    here = visc_ref[v, o]
    visc = [*around_x(visc_ref, (v,), o), visc_ref[v + 1, o], visc_ref[v - 1, o], *around_z(here)]
    visc = [here + other for other in visc]
    result = []
    for c in range(3):
        centre = cells_ref[c, y, o]
        cells = [
            *around_x(cells_ref, (c, y), o),
            cells_ref[c, y + 1, o],
            cells_ref[c, y - 1, o],
            *around_z(centre),
        ]
        change = visc[0] * (cells[0] - centre)
        for n in range(1, 6):
            change = change + visc[n] * (cells[n] - centre)
        result.append(centre + change)
    return result


def steps_kernel(
    place_ref, block_ref, before_ref, after_ref, low_ref, high_ref, corner_before_ref, corner_after_ref,
    final_ref, snap_ref, gram_ref,
    cells_ref, visc_ref, one_ref, two_ref, wide_ref, all_ref,
):
    rows_y, rows_z = block_ref.shape[1], block_ref.shape[3]
    cols = gram_ref.shape[0]
    first, last = place_ref[cols] == 1, place_ref[cols + 1] == 1
    over, under = slice(rows_z, rows_z + 4), slice(rows_z + 4, rows_z + 8)
    for c in range(4):
        for y in range(rows_y):
            for o in range(4):
                rows = slice(4 * o, 4 * o + 4)
                own, above, below = rows_y + y, 2 * rows_y + y, y
                cells_ref[c, own, o, :rows_z] = block_ref[c, y, o]
                cells_ref[c, own, o, over] = high_ref[c, y, rows]
                cells_ref[c, own, o, under] = low_ref[c, y, rows]
                cells_ref[c, below, o, :rows_z] = before_ref[c, y, o]
                cells_ref[c, above, o, :rows_z] = after_ref[c, y, o]
                if y > 0:
                    cells_ref[c, below, o, over] = corner_before_ref[c, 3 + y - 1, rows]
                    cells_ref[c, below, o, under] = corner_before_ref[c, y - 1, rows]
                if y < rows_y - 1:
                    cells_ref[c, above, o, over] = corner_after_ref[c, 3 + y, rows]
                    cells_ref[c, above, o, under] = corner_after_ref[c, y, rows]

    @pl.when(first)
    def _():
        for y in range(1, rows_y):
            cells_ref[3, y] = cells_ref[3, rows_y]

    @pl.when(last)
    def _():
        for y in range(rows_y - 1):
            cells_ref[3, 2 * rows_y + y] = cells_ref[3, 2 * rows_y - 1]

    def visc_one(y, carry):
        for o in range(4):
            visc_ref[y, o] = half_viscosity(cells_ref, y, o, cells_ref[3, y, o])
        return carry

    lax.fori_loop(1, 3 * rows_y - 1, visc_one, 0)

    def step_one(y, carry):
        outside = jnp.logical_or(
            jnp.logical_and(first, y < rows_y), jnp.logical_and(last, y >= 2 * rows_y)
        )
        for o in range(4):
            for c, cells in enumerate(stepped(cells_ref, y, visc_ref, y, o)):
                one_ref[c, y, o] = jnp.where(outside, 0.0, cells)
        return carry

    lax.fori_loop(2, 3 * rows_y - 2, step_one, 0)

    def visc_two(y, carry):
        for o in range(4):
            visc_ref[y, o] = half_viscosity(one_ref, y, o, cells_ref[3, y, o])
        return carry

    lax.fori_loop(rows_y - 1, 2 * rows_y + 1, visc_two, 0)

    for y in range(rows_y):
        for o in range(4):
            for c, cells in enumerate(stepped(one_ref, rows_y + y, visc_ref, rows_y + y, o)):
                two_ref[c, y, o] = cells[:rows_z]
                start = (c * rows_y + y) * rows_z
                wide_ref[start : start + rows_z, LANES * o : LANES * (o + 1)] = cells[:rows_z]
    final_ref[...] = exact_dot(wide_ref[...], sorting(4 * LANES, False)).reshape(final_ref.shape)

    for state, (ref, shift) in enumerate(((block_ref, 0), (one_ref, rows_y), (two_ref, 0))):
        for y in range(rows_y):
            for z in range(4):
                for o in range(4):
                    start = SLOT * (64 * state + 16 * y + 4 * z + o)
                    for c in range(3):
                        piece = ref[c, shift + y, o, pl.ds(z, rows_z // 4, stride=4), :]
                        all_ref[start + 4 * c : start + 4 * c + 4, :] = piece

    def choose(column, carry):
        source = pl.multiple_of(place_ref[column] * SLOT, SLOT)
        target = pl.multiple_of(column * SLOT, SLOT)
        snap_ref[pl.ds(target, SLOT), :] = all_ref[pl.ds(source, SLOT), :]
        return carry

    lax.fori_loop(0, cols, choose, 0, unroll=8)
    gram = jnp.zeros((cols, cols), jnp.float32)
    for block in range(0, 12, 2):
        part = jnp.concatenate(
            [snap_ref[pl.ds(block + i, cols, stride=SLOT), :] for i in range(2)], axis=1
        )
        gram = gram + lax.dot_general(
            part, part, (((1,), (1,)), ((), ())), precision=highest, preferred_element_type=jnp.float32
        )
    gram_ref[...] = gram


def both_steps(place, block, *halo):
    _, rows_y, _, rows_z, _ = block.shape
    cols = place.shape[0] - 2
    f32 = lambda *shape: jax.ShapeDtypeStruct(shape, jnp.float32)
    scratch = lambda *shape: pltpu.VMEM(shape, jnp.float32)
    depth = rows_z + 8
    return pl.pallas_call(
        steps_kernel,
        out_shape=(
            f32(3, rows_y, rows_z, 4 * LANES),
            f32(SLOT * cols, LANES),
            f32(cols, cols),
        ),
        in_specs=[pl.BlockSpec(memory_space=pltpu.SMEM)]
        + [pl.BlockSpec(memory_space=pltpu.VMEM)] * (1 + len(halo)),
        out_specs=[pl.BlockSpec(memory_space=pltpu.VMEM)] * 3,
        scratch_shapes=[
            scratch(4, 3 * rows_y, 4, depth, LANES),
            scratch(3 * rows_y, 4, depth, LANES),
            scratch(3, 3 * rows_y, 4, depth, LANES),
            scratch(3, rows_y, 4, rows_z, LANES),
            scratch(3 * rows_y * rows_z, 4 * LANES),
            scratch(SLOT * 192, LANES),
        ],
        compiler_params=pltpu.CompilerParams(vmem_limit_bytes=32 * 2**20),
        name="steps",
    )(place, block, *halo)


def device_sum(part):
    steps = [
        ("gz", lambda i: i ^ 1),
        ("gz", lambda i: 3 - i),
        ("gy", lambda i: i ^ 1),
        ("gy", lambda i: i ^ 2),
        ("gy", lambda i: i ^ 6),
        ("gy", lambda i: i ^ 14),
        ("gy", lambda i: i ^ 16),
        ("gy", lambda i: i ^ 48),
    ]
    for axis, partner in steps:
        count = lax.axis_size(axis)
        part = part + lax.ppermute(part, axis, [(i, partner(i)) for i in range(count)])
    return part


def local(velocity, smag_coef, snap_code):
    block, low, high = pack(velocity, smag_coef)
    count_y, count_z = lax.axis_size("gy"), lax.axis_size("gz")

    def along_z(part, step):
        return lax.ppermute(part, "gz", [(i, (i + step) % count_z) for i in range(count_z)])

    def along_y(part, step):
        pairs = [(i, i + step) for i in range(count_y) if 0 <= i + step < count_y]
        return lax.ppermute(part, "gy", pairs)

    from_low, from_high = along_z(high, 1), along_z(low, -1)
    before, after = along_y(block, 1), along_y(block, -1)
    corner_before = along_y(jnp.concatenate([from_low[:, 1:], from_high[:, 1:]], axis=1), 1)
    corner_after = along_y(jnp.concatenate([from_low[:, :-1], from_high[:, :-1]], axis=1), -1)
    row = lax.axis_index("gy")
    walls = jnp.stack([row == 0, row == count_y - 1]).astype(jnp.int32)
    final, snapshots, gram = both_steps(
        jnp.concatenate([snap_code, walls]),
        block, before, after, from_low, from_high, corner_before, corner_after,
    )
    rows_y, rows_z = velocity.shape[1], velocity.shape[2]
    rows_all = 12 * LANES * count_y * count_z
    pod_modes = project(device_sum(gram), snapshots, rows_all)
    return (final, pod_modes.reshape(RANK, 3, rows_y // 4, rows_z // 4, LANES))


def solution(mesh):
    placed = (P(None, "gy", "gz", None), P("gy", "gz", None), P())
    return jax.shard_map(
        local,
        mesh=mesh,
        in_specs=placed,
        out_specs=(P(None, "gy", "gz", None), P(None, None, "gy", "gz", None)),
        check_vma=False,
    )
```

```python
import functools

import jax
import jax.numpy as jnp
from jax import lax
from jax.experimental import pallas as pl
from jax.experimental.pallas import tpu as pltpu
from jax.sharding import PartitionSpec as P

RANK = 112
ITERS = 3
PANEL = 8
LANES = 128
SLOT = 16


nu_limit = 0.125
ridge = 1.0
highest = lax.Precision.HIGHEST


def recip(value):
    guess = pl.reciprocal(value, approx=True)
    return guess * (2.0 - value * guess)


def spread(block, lane):
    return jnp.broadcast_to(block[:, lane : lane + 1], block.shape)


def repeat(block, row):
    return jnp.broadcast_to(block[row : row + 1, :], block.shape)


def orthonormal_rows(inner, wide):
    panels = RANK // PANEL
    row_id = lax.broadcasted_iota(jnp.int32, (PANEL, inner.shape[1]), 0)
    left = [inner[PANEL * k : PANEL * (k + 1), :] for k in range(panels)]
    right = [wide[PANEL * k : PANEL * (k + 1), :] for k in range(panels)]
    rows = []
    for k in range(panels):
        follows = k + 1 < panels
        own_left, own_right = left[k], right[k]
        own_cols = [spread(own_left, PANEL * k + j) for j in range(PANEL)]
        if follows:
            next_left, next_right = left[k + 1], right[k + 1]
            next_cols = [spread(next_left, PANEL * k + j) for j in range(PANEL)]
        pivots = jnp.ones_like(own_left)
        for j in range(PANEL):
            pivot = repeat(own_cols[j], j)
            inverse = recip(pivot)
            pivots = jnp.where(row_id == j, pivot, pivots)
            own_factor = own_cols[j] * inverse
            for m in range(j + 1, PANEL):
                own_cols[m] = own_cols[m] - own_factor * repeat(own_cols[j], m)
            row_left, row_right = repeat(own_left, j), repeat(own_right, j)
            if follows:
                next_factor = next_cols[j] * inverse
                for m in range(j + 1, PANEL):
                    next_cols[m] = next_cols[m] - next_factor * repeat(own_cols[j], m)
                next_left = next_left - next_factor * row_left
                next_right = next_right - next_factor * row_right
            below = jnp.where(row_id > j, own_factor, 0.0)
            own_left = own_left - below * row_left
            own_right = own_right - below * row_right
        if follows:
            left[k + 1], right[k + 1] = next_left, next_right
        if k + 2 < panels:
            scale = recip(pivots)
            update = lax.dot_general(
                own_left[:, PANEL * (k + 2) : RANK],
                jnp.concatenate([own_left * scale, own_right * scale], axis=1),
                (((0,), (0,)), ((), ())),
                precision=highest,
                preferred_element_type=jnp.float32,
            )
            width = own_left.shape[1]
            for m in range(k + 2, panels):
                start = PANEL * (m - k - 2)
                left[m] = left[m] - update[start : start + PANEL, :width]
                right[m] = right[m] - update[start : start + PANEL, width:]
        root = lax.rsqrt(pivots)
        rows.append(own_right * (root * (1.5 - 0.5 * pivots * root * root)))
    return jnp.concatenate(rows, axis=0)


def basis_kernel(total_ref, snap_ref, out_ref, basis_ref, *, rows_all):
    cols = total_ref.shape[1]
    row_id, col_id = ids((cols, cols))
    identity = jnp.where(row_id == col_id, jnp.float32(ridge), 0.0)
    gram_matrix = unfolded(total_ref[...]) / rows_all + identity

    def sweep(step, carry):
        @pl.when(step == 0)
        def _():
            basis_ref[...] = gram_matrix[:RANK, :]

        @pl.when(step > 0)
        def _():
            basis_ref[...] = jnp.dot(
                basis_ref[...], gram_matrix, precision=highest, preferred_element_type=jnp.float32
            )

        wide = basis_ref[...]
        full = jnp.concatenate([wide, jnp.zeros((cols - RANK, cols), jnp.float32)], axis=0)
        inner = lax.dot_general(
            wide, full, (((1,), (1,)), ((), ())), precision=highest, preferred_element_type=jnp.float32
        )
        basis_ref[...] = orthonormal_rows(inner, wide)
        return carry

    lax.fori_loop(0, ITERS, sweep, 0)
    basis = basis_ref[...]
    blocks, cols = out_ref.shape[0] // RANK, basis.shape[1]
    for block in range(blocks):
        out_ref[pl.ds(block, RANK, stride=blocks), :] = jnp.dot(
            basis,
            snap_ref[pl.ds(block, cols, stride=SLOT), :],
            precision=highest,
            preferred_element_type=jnp.float32,
        )


def project(gram_total, snapshots, rows_all):
    cols = gram_total.shape[1]
    return pl.pallas_call(
        functools.partial(basis_kernel, rows_all=rows_all),
        out_shape=jax.ShapeDtypeStruct((RANK * 12, LANES), jnp.float32),
        in_specs=[pl.BlockSpec(memory_space=pltpu.VMEM)] * 2,
        out_specs=pl.BlockSpec(memory_space=pltpu.VMEM),
        scratch_shapes=[pltpu.VMEM((RANK, cols), jnp.float32)],
        compiler_params=pltpu.CompilerParams(vmem_limit_bytes=16 * 2**20),
        name="basis",
    )(gram_total, snapshots)


def exact_dot(values, one_hot):
    high = values.astype(jnp.bfloat16)
    rest = values - high.astype(jnp.float32)
    middle = rest.astype(jnp.bfloat16)
    low = (rest - middle.astype(jnp.float32)).astype(jnp.bfloat16)
    dot = functools.partial(jnp.dot, preferred_element_type=jnp.float32)
    return (dot(low, one_hot) + dot(middle, one_hot)) + dot(high, one_hot)


def sorting(size, to_sorted):
    cell = lax.broadcasted_iota(jnp.int32, (size, size), 0 if to_sorted else 1)
    spot = lax.broadcasted_iota(jnp.int32, (size, size), 1 if to_sorted else 0)
    place = (cell & 3) * (size // 4) + (cell >> 2)
    return jnp.where(place == spot, 1.0, 0.0).astype(jnp.bfloat16)


def pack_kernel(velocity_ref, coef_ref, block_ref, low_ref, high_ref):
    rows_y, rows_z, size_x = coef_ref.shape
    rows = jnp.concatenate(
        [velocity_ref[c].reshape(-1, size_x) for c in range(3)] + [coef_ref[...].reshape(-1, size_x)]
    )
    done = exact_dot(rows, sorting(size_x, True))
    for c in range(4):
        for y in range(rows_y):
            start = (c * rows_y + y) * rows_z
            for o in range(4):
                plane = done[start : start + rows_z, LANES * o : LANES * (o + 1)]
                block_ref[c, y, o] = plane
                low_ref[c, y, 4 * o : 4 * o + 4, :] = plane[:4]
                high_ref[c, y, 4 * o : 4 * o + 4, :] = plane[rows_z - 4 :]


def pack(velocity, smag_coef):
    rows_y, rows_z, size_x = smag_coef.shape
    edge = jax.ShapeDtypeStruct((4, rows_y, 16, LANES), jnp.float32)
    return pl.pallas_call(
        pack_kernel,
        out_shape=(jax.ShapeDtypeStruct((4, rows_y, 4, rows_z, LANES), jnp.float32), edge, edge),
        in_specs=[pl.BlockSpec(memory_space=pltpu.VMEM)] * 2,
        out_specs=[pl.BlockSpec(memory_space=pltpu.VMEM)] * 3,
        compiler_params=pltpu.CompilerParams(vmem_limit_bytes=24 * 2**20),
        name="pack",
    )(velocity, smag_coef)


def around_x(ref, index, o):
    ahead = ref[(*index, o + 1)] if o < 3 else pltpu.roll(ref[(*index, 0)], LANES - 1, 1)
    behind = ref[(*index, o - 1)] if o > 0 else pltpu.roll(ref[(*index, 3)], 1, 1)
    return ahead, behind


def around_z(plane):
    return pltpu.roll(plane, plane.shape[0] - 1, 0), pltpu.roll(plane, 1, 0)


def half_viscosity(cells_ref, y, o, coefficient):
    jump = []
    for c in range(3):
        x_ahead, x_behind = around_x(cells_ref, (c, y), o)
        z_ahead, z_behind = around_z(cells_ref[c, y, o])
        jump.append(
            (x_ahead - x_behind, cells_ref[c, y + 1, o] - cells_ref[c, y - 1, o], z_ahead - z_behind)
        )
    total = jump[0][0] ** 2 + jump[1][1] ** 2 + jump[2][2] ** 2
    total = total + total
    for c, d in ((0, 1), (0, 2), (1, 2)):
        total = total + (jump[c][d] + jump[d][c]) ** 2
    rate = coefficient * (0.5 * jnp.sqrt(total))
    return (0.5 * nu_limit) * rate * recip(1.0 + rate)


def stepped(cells_ref, y, visc_ref, v, o):
    here = visc_ref[v, o]
    visc = [*around_x(visc_ref, (v,), o), visc_ref[v + 1, o], visc_ref[v - 1, o], *around_z(here)]
    visc = [here + other for other in visc]
    result = []
    for c in range(3):
        centre = cells_ref[c, y, o]
        cells = [
            *around_x(cells_ref, (c, y), o),
            cells_ref[c, y + 1, o],
            cells_ref[c, y - 1, o],
            *around_z(centre),
        ]
        change = visc[0] * (cells[0] - centre)
        for n in range(1, 6):
            change = change + visc[n] * (cells[n] - centre)
        result.append(centre + change)
    return result


def ids(shape):
    return lax.broadcasted_iota(jnp.int32, shape, 0), lax.broadcasted_iota(jnp.int32, shape, 1)


def folded(gram):
    half = gram.shape[0] // 2
    row, lane = ids((half, 2 * half))
    corner = pltpu.roll(gram[half:], half, 1)
    square = jnp.where(lane < row, corner, gram[:half])
    diagonal = jnp.sum(jnp.where(lane == row, corner, 0.0), axis=0, keepdims=True)
    return jnp.concatenate([square, jnp.broadcast_to(diagonal, (8, 2 * half))], axis=0)


def unfolded(parts):
    half = parts.shape[1] // 2
    row, lane = ids((half, 2 * half))
    square = parts[:half]
    upper = jnp.where(lane > row, square, 0.0)
    lower = pltpu.roll(jnp.where(lane < row, square, 0.0), half, 1)
    one_side = jnp.concatenate([upper, lower], axis=0)
    below = pltpu.roll(jnp.broadcast_to(parts[half : half + 1], square.shape), half, 1)
    diagonal = jnp.concatenate(
        [jnp.where(lane == row, square, 0.0), jnp.where(lane == row + half, below, 0.0)], axis=0
    )
    return one_side + one_side.T + diagonal


def steps_kernel(
    place_ref, block_ref, before_ref, after_ref, low_ref, high_ref, corner_before_ref, corner_after_ref,
    final_ref, snap_ref, gram_ref,
    cells_ref, visc_ref, one_ref, two_ref, wide_ref, all_ref,
):
    rows_y, rows_z = block_ref.shape[1], block_ref.shape[3]
    cols = gram_ref.shape[1]
    first, last = place_ref[cols] == 1, place_ref[cols + 1] == 1
    over, under = slice(rows_z, rows_z + 4), slice(rows_z + 4, rows_z + 8)
    for c in range(4):
        for y in range(rows_y):
            for o in range(4):
                rows = slice(4 * o, 4 * o + 4)
                own, above, below = rows_y + y, 2 * rows_y + y, y
                cells_ref[c, own, o, :rows_z] = block_ref[c, y, o]
                cells_ref[c, own, o, over] = high_ref[c, y, rows]
                cells_ref[c, own, o, under] = low_ref[c, y, rows]
                cells_ref[c, below, o, :rows_z] = jnp.where(first, 0.0, before_ref[c, y, o])
                cells_ref[c, above, o, :rows_z] = jnp.where(last, 0.0, after_ref[c, y, o])
                if y > 0:
                    halo = jnp.where(first, 0.0, corner_before_ref[c, 3 + y - 1, rows])
                    cells_ref[c, below, o, over] = halo
                    halo = jnp.where(first, 0.0, corner_before_ref[c, y - 1, rows])
                    cells_ref[c, below, o, under] = halo
                if y < rows_y - 1:
                    halo = jnp.where(last, 0.0, corner_after_ref[c, 3 + y, rows])
                    cells_ref[c, above, o, over] = halo
                    halo = jnp.where(last, 0.0, corner_after_ref[c, y, rows])
                    cells_ref[c, above, o, under] = halo

    @pl.when(first)
    def _():
        for y in range(1, rows_y):
            cells_ref[3, y] = cells_ref[3, rows_y]

    @pl.when(last)
    def _():
        for y in range(rows_y - 1):
            cells_ref[3, 2 * rows_y + y] = cells_ref[3, 2 * rows_y - 1]

    def visc_one(y, carry):
        for o in range(4):
            visc_ref[y, o] = half_viscosity(cells_ref, y, o, cells_ref[3, y, o])
        return carry

    lax.fori_loop(1, 3 * rows_y - 1, visc_one, 0)

    def step_one(y, carry):
        outside = jnp.logical_or(
            jnp.logical_and(first, y < rows_y), jnp.logical_and(last, y >= 2 * rows_y)
        )
        for o in range(4):
            for c, cells in enumerate(stepped(cells_ref, y, visc_ref, y, o)):
                one_ref[c, y, o] = jnp.where(outside, 0.0, cells)
        return carry

    lax.fori_loop(2, 3 * rows_y - 2, step_one, 0)

    def visc_two(y, carry):
        for o in range(4):
            visc_ref[y, o] = half_viscosity(one_ref, y, o, cells_ref[3, y, o])
        return carry

    lax.fori_loop(rows_y - 1, 2 * rows_y + 1, visc_two, 0)

    for y in range(rows_y):
        for o in range(4):
            for c, cells in enumerate(stepped(one_ref, rows_y + y, visc_ref, rows_y + y, o)):
                two_ref[c, y, o] = cells[:rows_z]
                start = (c * rows_y + y) * rows_z
                wide_ref[start : start + rows_z, LANES * o : LANES * (o + 1)] = cells[:rows_z]
    final_ref[...] = exact_dot(wide_ref[...], sorting(4 * LANES, False)).reshape(final_ref.shape)

    for state, (ref, shift) in enumerate(((block_ref, 0), (one_ref, rows_y), (two_ref, 0))):
        for y in range(rows_y):
            for z in range(4):
                for o in range(4):
                    start = SLOT * (64 * state + 16 * y + 4 * z + o)
                    for c in range(3):
                        piece = ref[c, shift + y, o, pl.ds(z, rows_z // 4, stride=4), :]
                        all_ref[start + 4 * c : start + 4 * c + 4, :] = piece

    def choose(column, carry):
        source = pl.multiple_of(place_ref[column] * SLOT, SLOT)
        target = pl.multiple_of(column * SLOT, SLOT)
        snap_ref[pl.ds(target, SLOT), :] = all_ref[pl.ds(source, SLOT), :]
        return carry

    lax.fori_loop(0, cols, choose, 0, unroll=8)
    gram = jnp.zeros((cols, cols), jnp.float32)
    for block in range(0, 12, 2):
        part = jnp.concatenate(
            [snap_ref[pl.ds(block + i, cols, stride=SLOT), :] for i in range(2)], axis=1
        )
        gram = gram + lax.dot_general(
            part, part, (((1,), (1,)), ((), ())), precision=highest, preferred_element_type=jnp.float32
        )
    gram_ref[...] = folded(gram)


def both_steps(place, block, *halo):
    _, rows_y, _, rows_z, _ = block.shape
    cols = place.shape[0] - 2
    f32 = lambda *shape: jax.ShapeDtypeStruct(shape, jnp.float32)
    scratch = lambda *shape: pltpu.VMEM(shape, jnp.float32)
    depth = rows_z + 8
    return pl.pallas_call(
        steps_kernel,
        out_shape=(
            f32(3, rows_y, rows_z, 4 * LANES),
            f32(SLOT * cols, LANES),
            f32(cols // 2 + 8, cols),
        ),
        in_specs=[pl.BlockSpec(memory_space=pltpu.SMEM)]
        + [pl.BlockSpec(memory_space=pltpu.VMEM)] * (1 + len(halo)),
        out_specs=[pl.BlockSpec(memory_space=pltpu.VMEM)] * 3,
        scratch_shapes=[
            scratch(4, 3 * rows_y, 4, depth, LANES),
            scratch(3 * rows_y, 4, depth, LANES),
            scratch(3, 3 * rows_y, 4, depth, LANES),
            scratch(3, rows_y, 4, rows_z, LANES),
            scratch(3 * rows_y * rows_z, 4 * LANES),
            scratch(SLOT * 192, LANES),
        ],
        compiler_params=pltpu.CompilerParams(vmem_limit_bytes=32 * 2**20),
        name="steps",
    )(place, block, *halo)


def device_sum(part):
    steps = [("gy", 1), ("gz", 1), ("gy", 16), ("gy", 2), ("gz", 3), ("gy", 48), ("gy", 6), ("gy", 14)]
    for axis, flip in steps:
        count = lax.axis_size(axis)
        part = part + lax.ppermute(part, axis, [(i, i ^ flip) for i in range(count)])
    return part


def local(velocity, smag_coef, snap_code):
    block, low, high = pack(velocity, smag_coef)
    count_y, count_z = lax.axis_size("gy"), lax.axis_size("gz")

    def along_z(part, step):
        return lax.ppermute(part, "gz", [(i, (i + step) % count_z) for i in range(count_z)])

    def along_y(part, step):
        return lax.ppermute(part, "gy", [(i, (i + step) % count_y) for i in range(count_y)])

    from_low, from_high = along_z(high, 1), along_z(low, -1)
    before, after = along_y(block, 1), along_y(block, -1)
    corner_before = along_y(jnp.concatenate([from_low[:, 1:], from_high[:, 1:]], axis=1), 1)
    corner_after = along_y(jnp.concatenate([from_low[:, :-1], from_high[:, :-1]], axis=1), -1)
    row = lax.axis_index("gy")
    walls = jnp.stack([row == 0, row == count_y - 1]).astype(jnp.int32)
    final, snapshots, gram = both_steps(
        jnp.concatenate([snap_code, walls]),
        block, before, after, from_low, from_high, corner_before, corner_after,
    )
    rows_y, rows_z = velocity.shape[1], velocity.shape[2]
    rows_all = 12 * LANES * count_y * count_z
    pod_modes = project(device_sum(gram), snapshots, rows_all)
    return (final, pod_modes.reshape(RANK, 3, rows_y // 4, rows_z // 4, LANES))


def solution(mesh):
    placed = (P(None, "gy", "gz", None), P("gy", "gz", None), P())
    return jax.shard_map(
        local,
        mesh=mesh,
        in_specs=placed,
        out_specs=(P(None, "gy", "gz", None), P(None, None, "gy", "gz", None)),
        check_vma=False,
    )
```

```python
import functools

import jax
import jax.numpy as jnp
from jax import lax
from jax.experimental import pallas as pl
from jax.experimental.pallas import tpu as pltpu
from jax.sharding import PartitionSpec as P

RANK = 112
ITERS = 3
PANEL = 8
LANES = 128
SLOT = 16


nu_limit = 0.125
ridge = 1.0
highest = lax.Precision.HIGHEST


def recip(value):
    return pltpu.reciprocal(value, approx=True)


def spread(block, lane):
    return jnp.broadcast_to(block[:, lane : lane + 1], block.shape)


def repeat(block, row):
    return jnp.broadcast_to(block[row : row + 1, :], block.shape)


def parts_of(value):
    high = value.astype(jnp.bfloat16).astype(jnp.float32)
    rest = value - high
    middle = rest.astype(jnp.bfloat16).astype(jnp.float32)
    return high, middle, rest - middle


def outer_sum(left, right):
    lh, lm, ll = parts_of(left)
    rh, rm, rl = parts_of(right)
    stacked_left = jnp.concatenate([lh, lh, lh, lm, lm, ll]).astype(jnp.bfloat16)
    stacked_right = jnp.concatenate([rh, rm, rl, rh, rm, rh]).astype(jnp.bfloat16)
    return lax.dot_general(
        stacked_left, stacked_right, (((0,), (0,)), ((), ())), preferred_element_type=jnp.float32
    )


def eliminate(cols, blocks, others):
    row_id = lax.broadcasted_iota(jnp.int32, blocks[0].shape, 0)
    pivots, inverses = jnp.ones_like(blocks[0]), jnp.ones_like(blocks[0])
    for j in range(0, PANEL, 2):
        first, cross = repeat(cols[j], j), repeat(cols[j], j + 1)
        corner = repeat(cols[j + 1], j + 1)
        first_inverse = recip(first)
        second_inverse = first * recip(first * corner - cross * cross)
        second = corner - cross * (cross * first_inverse)
        for i, pivot, inverse in ((j, first, first_inverse), (j + 1, second, second_inverse)):
            pivots = jnp.where(row_id == i, pivot, pivots)
            inverses = jnp.where(row_id == i, inverse, inverses)
        one = cols[j] * first_inverse
        cols[j + 1] = cols[j + 1] - one * cross
        two = cols[j + 1] * second_inverse
        for other in others:
            below = other["below"]
            other_one = below[j] * first_inverse
            below[j + 1] = below[j + 1] - other_one * cross
            other_two = below[j + 1] * second_inverse
            for m in range(j + 2, PANEL):
                a, b = repeat(cols[j], m), repeat(cols[j + 1], m)
                below[m] = (below[m] - other_one * a) - other_two * b
            for m in range(PANEL):
                a, b = repeat(below[j], m), repeat(below[j + 1], m)
                other["cols"][m] = (other["cols"][m] - other_one * a) - other_two * b
            for n, block in enumerate(blocks):
                other["blocks"][n] = other["blocks"][n] - other_one * repeat(block, j)
            other["two"] = other_two
        for m in range(j + 2, PANEL):
            a, b = repeat(cols[j], m), repeat(cols[j + 1], m)
            cols[m] = (cols[m] - one * a) - two * b
        one = jnp.where(row_id > j, one, 0.0)
        two = jnp.where(row_id > j + 1, two, 0.0)
        for n in range(len(blocks)):
            blocks[n] = blocks[n] - one * repeat(blocks[n], j)
            row = repeat(blocks[n], j + 1)
            blocks[n] = blocks[n] - two * row
            for other in others:
                other["blocks"][n] = other["blocks"][n] - other["two"] * row
    return pivots, inverses


def orthonormal_rows(inner, wide):
    width = inner.shape[1]
    both = jnp.concatenate([inner, wide], axis=1)
    matrix = [both[PANEL * k : PANEL * (k + 1)] for k in range(RANK // PANEL)]
    rows = []
    for k in range(0, len(matrix), 2):
        upper = [matrix[k][:, :width], matrix[k][:, width:]]
        lower = [matrix[k + 1][:, :width], matrix[k + 1][:, width:]]
        cols = [spread(upper[0], PANEL * k + j) for j in range(PANEL)]
        other = {
            "below": [spread(lower[0], PANEL * k + j) for j in range(PANEL)],
            "cols": [spread(lower[0], PANEL * (k + 1) + j) for j in range(PANEL)],
            "blocks": lower,
        }
        upper_pivots, upper_inverses = eliminate(cols, upper, [other])
        lower_pivots, lower_inverses = eliminate(other["cols"], lower, [])
        rows += [upper[1] * lax.rsqrt(upper_pivots), lower[1] * lax.rsqrt(lower_pivots)]
        if k + 2 < len(matrix):
            scaled = jnp.concatenate(
                [
                    jnp.concatenate([block * upper_inverses for block in upper], axis=1),
                    jnp.concatenate([block * lower_inverses for block in lower], axis=1),
                ]
            )
            update = outer_sum(jnp.concatenate([upper[0], lower[0]]), scaled)
            for m in range(k + 2, len(matrix)):
                matrix[m] = matrix[m] - update[PANEL * m : PANEL * (m + 1)]
    return jnp.concatenate(rows, axis=0)


def basis_kernel(total_ref, snap_ref, out_ref, basis_ref, *, rows_all):
    cols = total_ref.shape[1]
    row_id, col_id = ids((cols, cols))
    identity = jnp.where(row_id == col_id, jnp.float32(ridge), 0.0)
    gram_matrix = unfolded(total_ref[...]) / rows_all + identity

    def sweep(step, carry):
        @pl.when(step == 0)
        def _():
            basis_ref[...] = gram_matrix[:RANK, :]

        @pl.when(step > 0)
        def _():
            basis_ref[...] = jnp.dot(
                basis_ref[...], gram_matrix, precision=highest, preferred_element_type=jnp.float32
            )

        wide = basis_ref[...]
        full = jnp.concatenate([wide, jnp.zeros((cols - RANK, cols), jnp.float32)], axis=0)
        inner = lax.dot_general(
            wide, full, (((1,), (1,)), ((), ())), precision=highest, preferred_element_type=jnp.float32
        )
        basis_ref[...] = orthonormal_rows(inner, wide)
        return carry

    lax.fori_loop(0, ITERS, sweep, 0)
    basis = basis_ref[...]
    blocks, cols = out_ref.shape[0] // RANK, basis.shape[1]
    for block in range(blocks):
        out_ref[pl.ds(block, RANK, stride=blocks), :] = jnp.dot(
            basis,
            snap_ref[pl.ds(block, cols, stride=SLOT), :],
            precision=highest,
            preferred_element_type=jnp.float32,
        )


def project(gram_total, snapshots, rows_all):
    cols = gram_total.shape[1]
    return pl.pallas_call(
        functools.partial(basis_kernel, rows_all=rows_all),
        out_shape=jax.ShapeDtypeStruct((RANK * 12, LANES), jnp.float32),
        in_specs=[pl.BlockSpec(memory_space=pltpu.VMEM)] * 2,
        out_specs=pl.BlockSpec(memory_space=pltpu.VMEM),
        scratch_shapes=[pltpu.VMEM((RANK, cols), jnp.float32)],
        compiler_params=pltpu.CompilerParams(vmem_limit_bytes=16 * 2**20),
        name="basis",
    )(gram_total, snapshots)


def exact_dot(values, one_hot):
    high, middle, low = (part.astype(jnp.bfloat16) for part in parts_of(values))
    dot = functools.partial(jnp.dot, preferred_element_type=jnp.float32)
    return (dot(low, one_hot) + dot(middle, one_hot)) + dot(high, one_hot)


def sorting(size, to_sorted):
    cell = lax.broadcasted_iota(jnp.int32, (size, size), 0 if to_sorted else 1)
    spot = lax.broadcasted_iota(jnp.int32, (size, size), 1 if to_sorted else 0)
    place = (cell & 3) * (size // 4) + (cell >> 2)
    return jnp.where(place == spot, 1.0, 0.0).astype(jnp.bfloat16)


def edges_kernel(velocity_ref, coef_ref, low_ref, high_ref, arrived):
    layers, rows_z = low_ref.shape[2], coef_ref.shape[1]
    copies = []
    for n, (edge_ref, start) in enumerate(((low_ref, 0), (high_ref, rows_z - layers))):
        rows = pl.ds(start, layers)
        copies += [
            pltpu.make_async_copy(velocity_ref.at[:, :, rows], edge_ref.at[:3], arrived.at[2 * n]),
            pltpu.make_async_copy(coef_ref.at[:, rows], edge_ref.at[3], arrived.at[2 * n + 1]),
        ]
    for copy in copies:
        copy.start()
    for copy in copies:
        copy.wait()


def edges(velocity, smag_coef):
    rows_y, _, size_x = smag_coef.shape
    edge = jax.ShapeDtypeStruct((4, rows_y, 4, size_x), jnp.float32)
    return pl.pallas_call(
        edges_kernel,
        out_shape=(edge, edge),
        in_specs=[pl.BlockSpec(memory_space=pltpu.HBM)] * 2,
        out_specs=[pl.BlockSpec(memory_space=pltpu.VMEM)] * 2,
        scratch_shapes=[pltpu.SemaphoreType.DMA((4,))],
        compiler_params=pltpu.CompilerParams(vmem_limit_bytes=2 * 2**20),
        name="edges",
    )(*(pltpu.with_memory_space_constraint(a, pltpu.HBM) for a in (velocity, smag_coef)))


def pack_kernel(velocity_ref, coef_ref, block_ref):
    rows_y, rows_z, size_x = coef_ref.shape
    rows = [velocity_ref[c].reshape(-1, size_x) for c in range(3)] + [coef_ref[...].reshape(-1, size_x)]
    done = exact_dot(jnp.concatenate(rows), sorting(size_x, True))
    for c in range(4):
        for y in range(rows_y):
            start = (c * rows_y + y) * rows_z
            for o in range(4):
                block_ref[c, y, o] = done[start : start + rows_z, LANES * o : LANES * (o + 1)]


def pack(velocity, smag_coef):
    rows_y, rows_z, _ = smag_coef.shape
    return pl.pallas_call(
        pack_kernel,
        out_shape=jax.ShapeDtypeStruct((4, rows_y, 4, rows_z, LANES), jnp.float32),
        in_specs=[pl.BlockSpec(memory_space=pltpu.VMEM)] * 2,
        out_specs=pl.BlockSpec(memory_space=pltpu.VMEM),
        compiler_params=pltpu.CompilerParams(vmem_limit_bytes=12 * 2**20),
        name="pack",
    )(velocity, smag_coef)


def sides_kernel(low_ref, high_ref, sides_ref, up_ref, down_ref):
    rows_y, layers, size_x = low_ref.shape[1:]
    rows = jnp.concatenate([high_ref[...], low_ref[...]], axis=2).reshape(-1, size_x)
    done = exact_dot(rows, sorting(size_x, True))
    for c in range(4):
        for y in range(rows_y):
            start = 2 * layers * (c * rows_y + y)
            for o in range(4):
                part = done[start : start + 2 * layers, LANES * o : LANES * (o + 1)]
                sides_ref[c, y, o] = part
                near, far = (0, layers + 2), rows_y - 2
                for ref, away in ((up_ref, rows_y - 1 - y), (down_ref, y)):
                    if away == 0:
                        ref[c, 0, o] = part
                    elif away <= far:
                        for side, begin in enumerate(near):
                            to = 4 * (away - 1) + 2 * side
                            ref[c, 1, o, to : to + 2] = part[begin : begin + 2]


def sort_sides(low, high):
    _, rows_y, layers, _ = low.shape
    shape = lambda rows: jax.ShapeDtypeStruct((4, rows, 4, 2 * layers, LANES), jnp.float32)
    return pl.pallas_call(
        sides_kernel,
        out_shape=(shape(rows_y), shape(2), shape(2)),
        in_specs=[pl.BlockSpec(memory_space=pltpu.VMEM)] * 2,
        out_specs=[pl.BlockSpec(memory_space=pltpu.VMEM)] * 3,
        compiler_params=pltpu.CompilerParams(vmem_limit_bytes=12 * 2**20),
        cost_estimate=pl.CostEstimate(flops=2 * 10**10, bytes_accessed=10**6, transcendentals=0),
        name="sides",
    )(low, high)


def around_x(ref, index, o):
    ahead = ref[(*index, o + 1)] if o < 3 else pltpu.roll(ref[(*index, 0)], LANES - 1, 1)
    behind = ref[(*index, o - 1)] if o > 0 else pltpu.roll(ref[(*index, 3)], 1, 1)
    return ahead, behind


def around_z(plane):
    return pltpu.roll(plane, plane.shape[0] - 1, 0), pltpu.roll(plane, 1, 0)


def half_viscosity(cells_ref, y, o, coefficient):
    jump = []
    for c in range(3):
        x_ahead, x_behind = around_x(cells_ref, (c, y), o)
        z_ahead, z_behind = around_z(cells_ref[c, y, o])
        jump.append(
            (x_ahead - x_behind, cells_ref[c, y + 1, o] - cells_ref[c, y - 1, o], z_ahead - z_behind)
        )
    total = jump[0][0] ** 2 + jump[1][1] ** 2 + jump[2][2] ** 2
    total = total + total
    for c, d in ((0, 1), (0, 2), (1, 2)):
        total = total + (jump[c][d] + jump[d][c]) ** 2
    rate = coefficient * (0.5 * total * lax.rsqrt(jnp.maximum(total, 1e-37)))
    return (0.5 * nu_limit) * rate * recip(1.0 + rate)


def stepped(cells_ref, y, visc_ref, v, o):
    here = visc_ref[v, o]
    visc = [*around_x(visc_ref, (v,), o), visc_ref[v + 1, o], visc_ref[v - 1, o], *around_z(here)]
    visc = [here + other for other in visc]
    result = []
    for c in range(3):
        centre = cells_ref[c, y, o]
        cells = [
            *around_x(cells_ref, (c, y), o),
            cells_ref[c, y + 1, o],
            cells_ref[c, y - 1, o],
            *around_z(centre),
        ]
        change = visc[0] * (cells[0] - centre)
        for n in range(1, 6):
            change = change + visc[n] * (cells[n] - centre)
        result.append(centre + change)
    return result


def ids(shape):
    return lax.broadcasted_iota(jnp.int32, shape, 0), lax.broadcasted_iota(jnp.int32, shape, 1)


def folded(gram):
    half = gram.shape[0] // 2
    row, lane = ids((half, 2 * half))
    corner = pltpu.roll(gram[half:], half, 1)
    square = jnp.where(lane < row, corner, gram[:half])
    diagonal = jnp.sum(jnp.where(lane == row, corner, 0.0), axis=0, keepdims=True)
    return jnp.concatenate([square, jnp.broadcast_to(diagonal, (8, 2 * half))], axis=0)


def unfolded(parts):
    half = parts.shape[1] // 2
    row, lane = ids((half, 2 * half))
    square = parts[:half]
    upper = jnp.where(lane > row, square, 0.0)
    lower = pltpu.roll(jnp.where(lane < row, square, 0.0), half, 1)
    one_side = jnp.concatenate([upper, lower], axis=0)
    below = pltpu.roll(jnp.broadcast_to(parts[half : half + 1], square.shape), half, 1)
    diagonal = jnp.concatenate(
        [jnp.where(lane == row, square, 0.0), jnp.where(lane == row + half, below, 0.0)], axis=0
    )
    return one_side + one_side.T + diagonal


def steps_kernel(
    code_ref, block_ref, before_ref, after_ref, sides_ref, side_before_ref, side_after_ref,
    wide_ref, snap_ref, gram_ref,
    cells_ref, visc_ref, one_ref, two_ref, all_ref,
):
    _, rows_y, _, rows_z, _ = block_ref.shape
    cols = gram_ref.shape[1]
    place_y = lax.axis_index("gy")
    first, last = place_y == 0, place_y == lax.axis_size("gy") - 1
    for c in range(4):
        for y in range(rows_y):
            for o in range(4):
                cells_ref[c, rows_y + y, o, :rows_z] = block_ref[c, y, o]
                halo = jnp.where(first, 0.0, before_ref[c, y, o])
                cells_ref[c, y, o, :rows_z] = halo
                halo = jnp.where(last, 0.0, after_ref[c, y, o])
                cells_ref[c, 2 * rows_y + y, o, :rows_z] = halo
                side = (slice(rows_z, rows_z + sides_ref.shape[3]),)
                cells_ref[(c, rows_y + y, o, *side)] = sides_ref[c, y, o]
                for ref, wall, at, away in (
                    (side_before_ref, first, y, rows_y - 1 - y),
                    (side_after_ref, last, 2 * rows_y + y, y),
                ):
                    if away == 0:
                        cells_ref[(c, at, o, *side)] = jnp.where(wall, 0.0, ref[c, 0, o])
                    elif away <= rows_y - 2:
                        for n, begin in enumerate((rows_z, rows_z + sides_ref.shape[3] - 2)):
                            to = 4 * (away - 1) + 2 * n
                            halo = jnp.where(wall, 0.0, ref[c, 1, o, to : to + 2])
                            cells_ref[c, at, o, begin : begin + 2] = halo

    @pl.when(first)
    def _():
        for y in range(1, rows_y):
            cells_ref[3, y] = cells_ref[3, rows_y]

    @pl.when(last)
    def _():
        for y in range(rows_y - 1):
            cells_ref[3, 2 * rows_y + y] = cells_ref[3, 2 * rows_y - 1]

    def visc_one(y, carry):
        for o in range(4):
            visc_ref[y, o] = half_viscosity(cells_ref, y, o, cells_ref[3, y, o])
        return carry

    lax.fori_loop(1, 3 * rows_y - 1, visc_one, 0)

    def step_one(y, carry):
        outside = jnp.logical_or(
            jnp.logical_and(first, y < rows_y), jnp.logical_and(last, y >= 2 * rows_y)
        )
        for o in range(4):
            for c, cells in enumerate(stepped(cells_ref, y, visc_ref, y, o)):
                one_ref[c, y, o] = jnp.where(outside, 0.0, cells)
        return carry

    lax.fori_loop(2, 3 * rows_y - 2, step_one, 0)

    def visc_two(y, carry):
        for o in range(4):
            visc_ref[y, o] = half_viscosity(one_ref, y, o, cells_ref[3, y, o])
        return carry

    lax.fori_loop(rows_y - 1, 2 * rows_y + 1, visc_two, 0)

    for y in range(rows_y):
        for o in range(4):
            for c, cells in enumerate(stepped(one_ref, rows_y + y, visc_ref, rows_y + y, o)):
                two_ref[c, y, o] = cells[:rows_z]
                start = (c * rows_y + y) * rows_z
                wide_ref[start : start + rows_z, LANES * o : LANES * (o + 1)] = cells[:rows_z]
    for state, (ref, shift) in enumerate(((block_ref, 0), (one_ref, rows_y), (two_ref, 0))):
        for y in range(rows_y):
            for z in range(4):
                for o in range(4):
                    start = SLOT * (64 * state + 16 * y + 4 * z + o)
                    for c in range(3):
                        piece = ref[c, shift + y, o, pl.ds(z, rows_z // 4, stride=4), :]
                        all_ref[start + 4 * c : start + 4 * c + 4, :] = piece

    def choose(column, carry):
        source = pl.multiple_of(code_ref[column] * SLOT, SLOT)
        target = pl.multiple_of(column * SLOT, SLOT)
        snap_ref[pl.ds(target, SLOT), :] = all_ref[pl.ds(source, SLOT), :]
        return carry

    lax.fori_loop(0, cols, choose, 0, unroll=16)
    even, odd = jnp.zeros((cols, cols), jnp.float32), jnp.zeros((cols, cols), jnp.float32)
    across = functools.partial(
        lax.dot_general,
        dimension_numbers=(((1,), (1,)), ((), ())),
        preferred_element_type=jnp.float32,
    )
    for block in range(0, 12, 2):
        part = jnp.concatenate(
            [snap_ref[pl.ds(block + i, cols, stride=SLOT), :] for i in range(2)], axis=1
        )
        high, middle, low = (p.astype(jnp.bfloat16) for p in parts_of(part))
        odd = odd + (across(high, low) + across(high, middle))
        even = even + (across(middle, middle) + across(high, high))
    gram_ref[...] = folded(even + (odd + odd.T))


def unsort_kernel(wide_ref, final_ref):
    final_ref[...] = exact_dot(wide_ref[...], sorting(wide_ref.shape[1], False)).reshape(final_ref.shape)


def unsort(wide, shape):
    return pl.pallas_call(
        unsort_kernel,
        out_shape=jax.ShapeDtypeStruct(shape, jnp.float32),
        in_specs=[pl.BlockSpec(memory_space=pltpu.VMEM)],
        out_specs=pl.BlockSpec(memory_space=pltpu.VMEM),
        compiler_params=pltpu.CompilerParams(vmem_limit_bytes=12 * 2**20),
        cost_estimate=pl.CostEstimate(flops=4 * 10**9, bytes_accessed=10**6, transcendentals=0),
        name="unsort",
    )(wide)


def both_steps(snap_code, block, *halo):
    _, rows_y, _, rows_z, _ = block.shape
    cols = snap_code.shape[0]
    f32 = lambda *shape: jax.ShapeDtypeStruct(shape, jnp.float32)
    scratch = lambda *shape: pltpu.VMEM(shape, jnp.float32)
    depth = rows_z + 8
    return pl.pallas_call(
        steps_kernel,
        out_shape=(
            f32(3 * rows_y * rows_z, 4 * LANES),
            f32(SLOT * cols, LANES),
            f32(cols // 2 + 8, cols),
        ),
        in_specs=[pl.BlockSpec(memory_space=pltpu.SMEM)]
        + [pl.BlockSpec(memory_space=pltpu.VMEM)] * (1 + len(halo)),
        out_specs=[pl.BlockSpec(memory_space=pltpu.VMEM)] * 3,
        scratch_shapes=[
            scratch(4, 3 * rows_y, 4, depth, LANES),
            scratch(3 * rows_y, 4, depth, LANES),
            scratch(3, 3 * rows_y, 4, depth, LANES),
            scratch(3, rows_y, 4, rows_z, LANES),
            scratch(SLOT * 192, LANES),
        ],
        compiler_params=pltpu.CompilerParams(vmem_limit_bytes=32 * 2**20),
        name="steps",
    )(snap_code, block, *halo)


def device_sum(part):
    ring = 8
    swaps = (lambda z: z ^ 1, lambda z: ((z + 1) ^ 1) - 1, lambda z: 7 - z if z % 4 in (1, 2) else z ^ 3)

    def along_z(swap):
        return lambda i: i - i // 2 % ring * 2 + swap(i // 2 % ring) % ring * 2

    flip = lambda bits: lambda i: i ^ bits
    steps = [
        ("gy", flip(1)),
        ("gz", flip(1)),
        ("gy", flip(16)),
        ("gy", along_z(swaps[0])),
        ("gz", flip(3)),
        ("gy", flip(48)),
        ("gy", along_z(swaps[1])),
        ("gy", along_z(swaps[2])),
    ]
    for axis, partner in steps:
        count = lax.axis_size(axis)
        part = part + lax.ppermute(part, axis, [(i, partner(i)) for i in range(count)])
    return part


def local(velocity, smag_coef, snap_code):
    count_y, count_z = lax.axis_size("gy"), lax.axis_size("gz")

    def along_z(part, step):
        return lax.ppermute(part, "gz", [(i, (i + step) % count_z) for i in range(count_z)])

    def along_y(part, step):
        return lax.ppermute(part, "gy", [(i, (i + step) % count_y) for i in range(count_y)])

    low, high = edges(velocity, smag_coef)
    velocity, smag_coef, low, high = lax.optimization_barrier((velocity, smag_coef, low, high))
    sides, up, down = sort_sides(along_z(high, 1), along_z(low, -1))
    side_before, side_after = along_y(up, 1), along_y(down, -1)
    block = pack(velocity, smag_coef)
    before, after = along_y(block, 1), along_y(block, -1)
    wide, snapshots, gram = both_steps(
        snap_code, block, before, after, sides, side_before, side_after
    )
    rows_y, rows_z = velocity.shape[1], velocity.shape[2]
    rows_all = 12 * LANES * count_y * count_z
    pod_modes = project(device_sum(gram), snapshots, rows_all)
    return (unsort(wide, velocity.shape), pod_modes.reshape(RANK, 3, rows_y // 4, rows_z // 4, LANES))


def solution(mesh):
    placed = (P(None, "gy", "gz", None), P("gy", "gz", None), P())
    return jax.shard_map(
        local,
        mesh=mesh,
        in_specs=placed,
        out_specs=(P(None, "gy", "gz", None), P(None, None, "gy", "gz", None)),
        check_vma=False,
    )
```

```python
import functools

import jax
import jax.numpy as jnp
from jax import lax
from jax.experimental import pallas as pl
from jax.experimental.pallas import tpu as pltpu
from jax.sharding import PartitionSpec as P

RANK = 112
ITERS = 3
PANEL = 8
GROUP = 5
LANES = 128
SLOT = 16


nu_limit = 0.125
ridge = 1.0
highest = lax.Precision.HIGHEST


def recip(value):
    return pltpu.reciprocal(value, approx=True)


def spread(block, lane):
    return jnp.broadcast_to(block[:, lane : lane + 1], block.shape)


def repeat(block, row):
    return jnp.broadcast_to(block[row : row + 1, :], block.shape)


def parts_of(value):
    high = value.astype(jnp.bfloat16).astype(jnp.float32)
    rest = value - high
    middle = rest.astype(jnp.bfloat16).astype(jnp.float32)
    return high, middle, rest - middle


def outer_sum(left, right):
    lh, lm, ll = parts_of(left)
    rh, rm, rl = parts_of(right)
    stacked_left = jnp.concatenate([lh, lh, lh, lm, lm, ll]).astype(jnp.bfloat16)
    stacked_right = jnp.concatenate([rh, rm, rl, rh, rm, rh]).astype(jnp.bfloat16)
    return lax.dot_general(
        stacked_left, stacked_right, (((0,), (0,)), ((), ())), preferred_element_type=jnp.float32
    )


def eliminate(cols, blocks, others):
    row_id = lax.broadcasted_iota(jnp.int32, blocks[0].shape, 0)
    pivots, inverses = jnp.ones_like(blocks[0]), jnp.ones_like(blocks[0])
    for j in range(0, PANEL, 2):
        first, cross = repeat(cols[j], j), repeat(cols[j], j + 1)
        corner = repeat(cols[j + 1], j + 1)
        first_inverse = recip(first)
        second_inverse = first * recip(first * corner - cross * cross)
        second = corner - cross * (cross * first_inverse)
        for i, pivot, inverse in ((j, first, first_inverse), (j + 1, second, second_inverse)):
            pivots = jnp.where(row_id == i, pivot, pivots)
            inverses = jnp.where(row_id == i, inverse, inverses)
        one = cols[j] * first_inverse
        cols[j + 1] = cols[j + 1] - one * cross
        two = cols[j + 1] * second_inverse
        for other in others:
            below = other["below"]
            other_one = below[j] * first_inverse
            below[j + 1] = below[j + 1] - other_one * cross
            other_two = below[j + 1] * second_inverse
            for m in range(j + 2, PANEL):
                a, b = repeat(cols[j], m), repeat(cols[j + 1], m)
                below[m] = (below[m] - other_one * a) - other_two * b
            for m in range(len(other["cols"])):
                a, b = repeat(below[j], m), repeat(below[j + 1], m)
                other["cols"][m] = (other["cols"][m] - other_one * a) - other_two * b
            for n, block in enumerate(blocks):
                other["blocks"][n] = other["blocks"][n] - other_one * repeat(block, j)
            other["two"] = other_two
        for m in range(j + 2, PANEL):
            a, b = repeat(cols[j], m), repeat(cols[j + 1], m)
            cols[m] = (cols[m] - one * a) - two * b
        one = jnp.where(row_id > j, one, 0.0)
        two = jnp.where(row_id > j + 1, two, 0.0)
        for n in range(len(blocks)):
            blocks[n] = blocks[n] - one * repeat(blocks[n], j)
            row = repeat(blocks[n], j + 1)
            blocks[n] = blocks[n] - two * row
            for other in others:
                other["blocks"][n] = other["blocks"][n] - other["two"] * row
    return pivots, inverses


def orthonormal_rows(inner, wide):
    width = inner.shape[1]
    both = jnp.concatenate([inner, wide], axis=1)
    matrix = [both[PANEL * k : PANEL * (k + 1)] for k in range(RANK // PANEL)]
    rows = []
    for k in range(0, len(matrix), GROUP):
        group = [[part[:, :width], part[:, width:]] for part in matrix[k : k + GROUP]]
        cols = [spread(group[0][0], PANEL * k + j) for j in range(PANEL)]
        scaled = []
        for n, blocks in enumerate(group):
            at = PANEL * (k + n)
            others = []
            for later, other in enumerate(group[n + 1 :]):
                below = [spread(other[0], at + j) for j in range(PANEL)]
                ahead = [spread(other[0], at + PANEL + j) for j in range(PANEL)] if later == 0 else []
                others.append({"below": below, "cols": ahead, "blocks": other})
            pivots, inverses = eliminate(cols, blocks, others)
            rows.append(blocks[1] * lax.rsqrt(pivots))
            scaled.append(jnp.concatenate([block * inverses for block in blocks], axis=1))
            if others:
                cols = others[0]["cols"]
        if k + GROUP < len(matrix):
            update = outer_sum(
                jnp.concatenate([blocks[0] for blocks in group]), jnp.concatenate(scaled)
            )
            for m in range(k + GROUP, len(matrix)):
                matrix[m] = matrix[m] - update[PANEL * m : PANEL * (m + 1)]
    return jnp.concatenate(rows, axis=0)


def deep_left(value):
    high, middle, low = parts_of(value)
    return jnp.concatenate([high, high, high, middle, middle, low], axis=1).astype(jnp.bfloat16)


def deep_right(value, axis):
    high, middle, low = parts_of(value)
    return jnp.concatenate([high, middle, low, high, middle, high], axis=axis).astype(jnp.bfloat16)


def basis_kernel(total_ref, snap_ref, out_ref, *, rows_all):
    cols = total_ref.shape[1]
    row_id, col_id = ids((cols, cols))
    identity = jnp.where(row_id == col_id, jnp.float32(ridge), 0.0)
    gram_matrix = unfolded(total_ref[...]) / rows_all + identity

    gram_deep = deep_right(gram_matrix, 0)
    basis = gram_matrix[:RANK]
    for step in range(ITERS):
        if step > 0:
            basis = jnp.dot(deep_left(basis), gram_deep, preferred_element_type=jnp.float32)
        full = jnp.concatenate([basis, jnp.zeros((cols - RANK, cols), jnp.float32)], axis=0)
        inner = lax.dot_general(
            deep_left(basis),
            deep_right(full, 1),
            (((1,), (1,)), ((), ())),
            preferred_element_type=jnp.float32,
        )
        basis = orthonormal_rows(inner, basis)
    blocks = out_ref.shape[0] // RANK
    basis_deep = deep_left(basis)
    for block in range(0, blocks, 2):
        pair = [snap_ref[pl.ds(block + n, cols, stride=SLOT), :] for n in range(2)]
        modes = jnp.dot(
            basis_deep,
            deep_right(jnp.concatenate(pair, axis=1), 0),
            preferred_element_type=jnp.float32,
        )
        for n in range(2):
            out_ref[pl.ds(block + n, RANK, stride=blocks), :] = modes[:, LANES * n : LANES * (n + 1)]


def project(gram_total, snapshots, rows_all):
    return pl.pallas_call(
        functools.partial(basis_kernel, rows_all=rows_all),
        out_shape=jax.ShapeDtypeStruct((RANK * 12, LANES), jnp.float32),
        in_specs=[pl.BlockSpec(memory_space=pltpu.VMEM)] * 2,
        out_specs=pl.BlockSpec(memory_space=pltpu.VMEM),
        compiler_params=pltpu.CompilerParams(vmem_limit_bytes=16 * 2**20),
        name="basis",
    )(gram_total, snapshots)


def exact_dot(values, one_hot):
    high, middle, low = (part.astype(jnp.bfloat16) for part in parts_of(values))
    dot = functools.partial(jnp.dot, preferred_element_type=jnp.float32)
    return (dot(low, one_hot) + dot(middle, one_hot)) + dot(high, one_hot)


def sorting(size, to_sorted):
    cell = lax.broadcasted_iota(jnp.int32, (size, size), 0 if to_sorted else 1)
    spot = lax.broadcasted_iota(jnp.int32, (size, size), 1 if to_sorted else 0)
    place = (cell & 3) * (size // 4) + (cell >> 2)
    return jnp.where(place == spot, 1.0, 0.0).astype(jnp.bfloat16)


def edges_kernel(velocity_ref, coef_ref, low_ref, high_ref, arrived):
    layers, rows_z = low_ref.shape[2], coef_ref.shape[1]
    copies = []
    for n, (edge_ref, start) in enumerate(((low_ref, 0), (high_ref, rows_z - layers))):
        rows = pl.ds(start, layers)
        copies += [
            pltpu.make_async_copy(velocity_ref.at[:, :, rows], edge_ref.at[:3], arrived.at[2 * n]),
            pltpu.make_async_copy(coef_ref.at[:, rows], edge_ref.at[3], arrived.at[2 * n + 1]),
        ]
    for copy in copies:
        copy.start()
    for copy in copies:
        copy.wait()


def edges(velocity, smag_coef):
    rows_y, _, size_x = smag_coef.shape
    edge = jax.ShapeDtypeStruct((4, rows_y, 4, size_x), jnp.float32)
    return pl.pallas_call(
        edges_kernel,
        out_shape=(edge, edge),
        in_specs=[pl.BlockSpec(memory_space=pltpu.HBM)] * 2,
        out_specs=[pl.BlockSpec(memory_space=pltpu.VMEM)] * 2,
        scratch_shapes=[pltpu.SemaphoreType.DMA((4,))],
        compiler_params=pltpu.CompilerParams(vmem_limit_bytes=2 * 2**20),
        name="edges",
    )(*(pltpu.with_memory_space_constraint(a, pltpu.HBM) for a in (velocity, smag_coef)))


def pack_kernel(velocity_ref, coef_ref, block_ref):
    rows_y, rows_z, size_x = coef_ref.shape
    rows = [velocity_ref[c].reshape(-1, size_x) for c in range(3)] + [coef_ref[...].reshape(-1, size_x)]
    done = exact_dot(jnp.concatenate(rows), sorting(size_x, True))
    for c in range(4):
        for y in range(rows_y):
            start = (c * rows_y + y) * rows_z
            for o in range(4):
                block_ref[c, y, o] = done[start : start + rows_z, LANES * o : LANES * (o + 1)]


def pack(velocity, smag_coef):
    rows_y, rows_z, _ = smag_coef.shape
    return pl.pallas_call(
        pack_kernel,
        out_shape=jax.ShapeDtypeStruct((4, rows_y, 4, rows_z, LANES), jnp.float32),
        in_specs=[pl.BlockSpec(memory_space=pltpu.VMEM)] * 2,
        out_specs=pl.BlockSpec(memory_space=pltpu.VMEM),
        compiler_params=pltpu.CompilerParams(vmem_limit_bytes=12 * 2**20),
        name="pack",
    )(velocity, smag_coef)


def sides_kernel(low_ref, high_ref, sides_ref, chip_ref, other_ref):
    odd = lax.axis_index("gy") % 2 == 1
    rows_y, layers, size_x = low_ref.shape[1:]
    rows = jnp.concatenate([high_ref[...], low_ref[...]], axis=2).reshape(-1, size_x)
    done = exact_dot(rows, sorting(size_x, True)).reshape(4, rows_y, 2 * layers, size_x)
    for c in range(4):
        for o in range(4):
            planes = [done[c, y, :, LANES * o : LANES * (o + 1)] for y in range(rows_y)]
            for y in range(rows_y):
                sides_ref[c, y, o] = planes[y]
            for away in range(rows_y - 1):
                upper, lower = planes[rows_y - 1 - away], planes[away]
                on_chip, off_chip = jnp.where(odd, lower, upper), jnp.where(odd, upper, lower)
                for ref, plane in ((chip_ref, on_chip), (other_ref, off_chip)):
                    if away == 0:
                        ref[c, 0, o] = plane
                    else:
                        for side, begin in enumerate((0, layers + 2)):
                            to = 4 * (away - 1) + 2 * side
                            ref[c, 1, o, to : to + 2] = plane[begin : begin + 2]


def sort_sides(low, high):
    _, rows_y, layers, _ = low.shape
    shape = lambda rows: jax.ShapeDtypeStruct((4, rows, 4, 2 * layers, LANES), jnp.float32)
    return pl.pallas_call(
        sides_kernel,
        out_shape=(shape(rows_y), shape(2), shape(2)),
        in_specs=[pl.BlockSpec(memory_space=pltpu.VMEM)] * 2,
        out_specs=[pl.BlockSpec(memory_space=pltpu.VMEM)] * 3,
        compiler_params=pltpu.CompilerParams(vmem_limit_bytes=12 * 2**20),
        cost_estimate=pl.CostEstimate(flops=2 * 10**10, bytes_accessed=10**6, transcendentals=0),
        name="sides",
    )(low, high)


def around_x(ref, index, o):
    ahead = ref[(*index, o + 1)] if o < 3 else pltpu.roll(ref[(*index, 0)], LANES - 1, 1)
    behind = ref[(*index, o - 1)] if o > 0 else pltpu.roll(ref[(*index, 3)], 1, 1)
    return ahead, behind


def around_z(plane):
    return pltpu.roll(plane, plane.shape[0] - 1, 0), pltpu.roll(plane, 1, 0)


def half_viscosity(cells_ref, y, o, coefficient):
    jump = []
    for c in range(3):
        x_ahead, x_behind = around_x(cells_ref, (c, y), o)
        z_ahead, z_behind = around_z(cells_ref[c, y, o])
        jump.append(
            (x_ahead - x_behind, cells_ref[c, y + 1, o] - cells_ref[c, y - 1, o], z_ahead - z_behind)
        )
    total = jump[0][0] ** 2 + jump[1][1] ** 2 + jump[2][2] ** 2
    total = total + total
    for c, d in ((0, 1), (0, 2), (1, 2)):
        total = total + (jump[c][d] + jump[d][c]) ** 2
    rate = coefficient * (0.5 * total * lax.rsqrt(jnp.maximum(total, 1e-37)))
    return (0.5 * nu_limit) * rate * recip(1.0 + rate)


def stepped(cells_ref, y, visc_ref, v, o):
    here = visc_ref[v, o]
    visc = [*around_x(visc_ref, (v,), o), visc_ref[v + 1, o], visc_ref[v - 1, o], *around_z(here)]
    visc = [here + other for other in visc]
    result = []
    for c in range(3):
        centre = cells_ref[c, y, o]
        cells = [
            *around_x(cells_ref, (c, y), o),
            cells_ref[c, y + 1, o],
            cells_ref[c, y - 1, o],
            *around_z(centre),
        ]
        change = visc[0] * (cells[0] - centre)
        for n in range(1, 6):
            change = change + visc[n] * (cells[n] - centre)
        result.append(centre + change)
    return result


def ids(shape):
    return lax.broadcasted_iota(jnp.int32, shape, 0), lax.broadcasted_iota(jnp.int32, shape, 1)


def folded(gram):
    half = gram.shape[0] // 2
    row, lane = ids((half, 2 * half))
    corner = pltpu.roll(gram[half:], half, 1)
    square = jnp.where(lane < row, corner, gram[:half])
    diagonal = jnp.sum(jnp.where(lane == row, corner, 0.0), axis=0, keepdims=True)
    return jnp.concatenate([square, jnp.broadcast_to(diagonal, (8, 2 * half))], axis=0)


def unfolded(parts):
    half = parts.shape[1] // 2
    row, lane = ids((half, 2 * half))
    square = parts[:half]
    upper = jnp.where(lane > row, square, 0.0)
    lower = pltpu.roll(jnp.where(lane < row, square, 0.0), half, 1)
    one_side = jnp.concatenate([upper, lower], axis=0)
    below = pltpu.roll(jnp.broadcast_to(parts[half : half + 1], square.shape), half, 1)
    diagonal = jnp.concatenate(
        [jnp.where(lane == row, square, 0.0), jnp.where(lane == row + half, below, 0.0)], axis=0
    )
    return one_side + one_side.T + diagonal


def steps_kernel(
    code_ref, block_ref, chip_ref, other_ref, sides_ref, side_chip_ref, side_other_ref,
    wide_ref, snap_ref, gram_ref,
    cells_ref, visc_ref, one_ref, two_ref, all_ref,
):
    _, rows_y, _, rows_z, _ = block_ref.shape
    cols = gram_ref.shape[1]
    place_y = lax.axis_index("gy")
    first, last, odd = place_y == 0, place_y == lax.axis_size("gy") - 1, place_y % 2 == 1

    def behind(chip, other):
        return jnp.where(first, 0.0, jnp.where(odd, chip, other))

    def ahead(chip, other):
        return jnp.where(last, 0.0, jnp.where(odd, other, chip))

    for c in range(4):
        for y in range(rows_y):
            for o in range(4):
                cells_ref[c, rows_y + y, o, :rows_z] = block_ref[c, y, o]
                chip, other = chip_ref[c, y, o], other_ref[c, y, o]
                cells_ref[c, y, o, :rows_z] = behind(chip, other)
                cells_ref[c, 2 * rows_y + y, o, :rows_z] = ahead(chip, other)
                side = (slice(rows_z, rows_z + sides_ref.shape[3]),)
                cells_ref[(c, rows_y + y, o, *side)] = sides_ref[c, y, o]
                for choose, at, away in (
                    (behind, y, rows_y - 1 - y),
                    (ahead, 2 * rows_y + y, y),
                ):
                    if away == 0:
                        halo = choose(side_chip_ref[c, 0, o], side_other_ref[c, 0, o])
                        cells_ref[(c, at, o, *side)] = halo
                    elif away <= rows_y - 2:
                        for n, begin in enumerate((rows_z, rows_z + sides_ref.shape[3] - 2)):
                            part = (c, 1, o, slice(4 * (away - 1) + 2 * n, 4 * (away - 1) + 2 * n + 2))
                            halo = choose(side_chip_ref[part], side_other_ref[part])
                            cells_ref[c, at, o, begin : begin + 2] = halo

    @pl.when(first)
    def _():
        for y in range(1, rows_y):
            cells_ref[3, y] = cells_ref[3, rows_y]

    @pl.when(last)
    def _():
        for y in range(rows_y - 1):
            cells_ref[3, 2 * rows_y + y] = cells_ref[3, 2 * rows_y - 1]

    def visc_one(y, carry):
        for o in range(4):
            visc_ref[y, o] = half_viscosity(cells_ref, y, o, cells_ref[3, y, o])
        return carry

    lax.fori_loop(1, 3 * rows_y - 1, visc_one, 0)

    def step_one(y, carry):
        outside = jnp.logical_or(
            jnp.logical_and(first, y < rows_y), jnp.logical_and(last, y >= 2 * rows_y)
        )
        for o in range(4):
            for c, cells in enumerate(stepped(cells_ref, y, visc_ref, y, o)):
                one_ref[c, y, o] = jnp.where(outside, 0.0, cells)
        return carry

    lax.fori_loop(2, 3 * rows_y - 2, step_one, 0)

    def visc_two(y, carry):
        for o in range(4):
            visc_ref[y, o] = half_viscosity(one_ref, y, o, cells_ref[3, y, o])
        return carry

    lax.fori_loop(rows_y - 1, 2 * rows_y + 1, visc_two, 0)

    for y in range(rows_y):
        for o in range(4):
            for c, cells in enumerate(stepped(one_ref, rows_y + y, visc_ref, rows_y + y, o)):
                two_ref[c, y, o] = cells[:rows_z]
                start = (c * rows_y + y) * rows_z
                wide_ref[start : start + rows_z, LANES * o : LANES * (o + 1)] = cells[:rows_z]
    for state, (ref, shift) in enumerate(((block_ref, 0), (one_ref, rows_y), (two_ref, 0))):
        for y in range(rows_y):
            for z in range(4):
                for o in range(4):
                    start = SLOT * (64 * state + 16 * y + 4 * z + o)
                    for c in range(3):
                        piece = ref[c, shift + y, o, pl.ds(z, rows_z // 4, stride=4), :]
                        all_ref[start + 4 * c : start + 4 * c + 4, :] = piece

    def pick(column, carry):
        source = pl.multiple_of(code_ref[column] * SLOT, SLOT)
        target = pl.multiple_of(column * SLOT, SLOT)
        snap_ref[pl.ds(target, SLOT), :] = all_ref[pl.ds(source, SLOT), :]
        return carry

    lax.fori_loop(0, cols, pick, 0, unroll=16)
    even, odd = jnp.zeros((cols, cols), jnp.float32), jnp.zeros((cols, cols), jnp.float32)
    across = functools.partial(
        lax.dot_general,
        dimension_numbers=(((1,), (1,)), ((), ())),
        preferred_element_type=jnp.float32,
    )
    for block in range(0, 12, 2):
        part = jnp.concatenate(
            [snap_ref[pl.ds(block + i, cols, stride=SLOT), :] for i in range(2)], axis=1
        )
        high, middle, low = (p.astype(jnp.bfloat16) for p in parts_of(part))
        odd = odd + (across(high, low) + across(high, middle))
        even = even + (across(middle, middle) + across(high, high))
    gram_ref[...] = folded(even + (odd + odd.T))


def unsort_kernel(wide_ref, final_ref):
    final_ref[...] = exact_dot(wide_ref[...], sorting(wide_ref.shape[1], False)).reshape(final_ref.shape)


def unsort(wide, shape):
    return pl.pallas_call(
        unsort_kernel,
        out_shape=jax.ShapeDtypeStruct(shape, jnp.float32),
        in_specs=[pl.BlockSpec(memory_space=pltpu.VMEM)],
        out_specs=pl.BlockSpec(memory_space=pltpu.VMEM),
        compiler_params=pltpu.CompilerParams(vmem_limit_bytes=12 * 2**20),
        cost_estimate=pl.CostEstimate(flops=4 * 10**9, bytes_accessed=10**6, transcendentals=0),
        name="unsort",
    )(wide)


def both_steps(snap_code, block, *halo):
    _, rows_y, _, rows_z, _ = block.shape
    cols = snap_code.shape[0]
    f32 = lambda *shape: jax.ShapeDtypeStruct(shape, jnp.float32)
    scratch = lambda *shape: pltpu.VMEM(shape, jnp.float32)
    depth = rows_z + 8
    return pl.pallas_call(
        steps_kernel,
        out_shape=(
            f32(3 * rows_y * rows_z, 4 * LANES),
            f32(SLOT * cols, LANES),
            f32(cols // 2 + 8, cols),
        ),
        in_specs=[pl.BlockSpec(memory_space=pltpu.SMEM)]
        + [pl.BlockSpec(memory_space=pltpu.VMEM)] * (1 + len(halo)),
        out_specs=[pl.BlockSpec(memory_space=pltpu.VMEM)] * 3,
        scratch_shapes=[
            scratch(4, 3 * rows_y, 4, depth, LANES),
            scratch(3 * rows_y, 4, depth, LANES),
            scratch(3, 3 * rows_y, 4, depth, LANES),
            scratch(3, rows_y, 4, rows_z, LANES),
            scratch(SLOT * 192, LANES),
        ],
        compiler_params=pltpu.CompilerParams(vmem_limit_bytes=32 * 2**20),
        name="steps",
    )(snap_code, block, *halo)


def device_sum(part):
    ring = 8
    swaps = (lambda z: z ^ 1, lambda z: ((z + 1) ^ 1) - 1, lambda z: 7 - z if z % 4 in (1, 2) else z ^ 3)

    def along_z(swap):
        return lambda i: i - i // 2 % ring * 2 + swap(i // 2 % ring) % ring * 2

    flip = lambda bits: lambda i: i ^ bits
    steps = [
        ("gy", flip(1)),
        ("gz", flip(1)),
        ("gy", flip(16)),
        ("gy", along_z(swaps[0])),
        ("gz", flip(3)),
        ("gy", flip(48)),
        ("gy", along_z(swaps[1])),
        ("gy", along_z(swaps[2])),
    ]
    for axis, partner in steps:
        count = lax.axis_size(axis)
        part = part + lax.ppermute(part, axis, [(i, partner(i)) for i in range(count)])
    return part


def local(velocity, smag_coef, snap_code):
    count_y, count_z = lax.axis_size("gy"), lax.axis_size("gz")

    def along_z(part, step):
        return lax.ppermute(part, "gz", [(i, (i + step) % count_z) for i in range(count_z)])

    def on_chip(part):
        return lax.ppermute(part, "gy", [(i, i ^ 1) for i in range(count_y)])

    def off_chip(part):
        partners = [min(max(((i + 1) ^ 1) - 1, 0), count_y - 1) for i in range(count_y)]
        return lax.ppermute(part, "gy", list(enumerate(partners)))

    low, high = edges(velocity, smag_coef)
    velocity, smag_coef, low, high = lax.optimization_barrier((velocity, smag_coef, low, high))
    sides, side_chip, side_other = sort_sides(along_z(high, 1), along_z(low, -1))
    block = pack(velocity, smag_coef)
    wide, snapshots, gram = both_steps(
        snap_code, block, on_chip(block), off_chip(block), sides, on_chip(side_chip), off_chip(side_other)
    )
    rows_y, rows_z = velocity.shape[1], velocity.shape[2]
    rows_all = 12 * LANES * count_y * count_z
    pod_modes = project(device_sum(gram), snapshots, rows_all)
    return (unsort(wide, velocity.shape), pod_modes.reshape(RANK, 3, rows_y // 4, rows_z // 4, LANES))


def solution(mesh):
    placed = (P(None, "gy", "gz", None), P("gy", "gz", None), P())
    return jax.shard_map(
        local,
        mesh=mesh,
        in_specs=placed,
        out_specs=(P(None, "gy", "gz", None), P(None, None, "gy", "gz", None)),
        check_vma=False,
    )
```

```python
import functools

import jax
import jax.numpy as jnp
from jax import lax
from jax.experimental import pallas as pl
from jax.experimental.pallas import tpu as pltpu
from jax.sharding import PartitionSpec as P

RANK = 112
ITERS = 3
PANEL = 8
GROUP = 5
LANES = 128
SLOT = 16


nu_limit = 0.125
ridge = 1.0
highest = lax.Precision.HIGHEST


def recip(value):
    return pltpu.reciprocal(value, approx=True)


def spread(block, lane):
    return jnp.broadcast_to(block[:, lane : lane + 1], block.shape)


def repeat(block, row):
    return jnp.broadcast_to(block[row : row + 1, :], block.shape)


def parts_of(value):
    high = value.astype(jnp.bfloat16).astype(jnp.float32)
    rest = value - high
    middle = rest.astype(jnp.bfloat16).astype(jnp.float32)
    return high, middle, rest - middle


def outer_sum(left, right):
    lh, lm, ll = parts_of(left)
    rh, rm, rl = parts_of(right)
    stacked_left = jnp.concatenate([lh, lh, lh, lm, lm, ll]).astype(jnp.bfloat16)
    stacked_right = jnp.concatenate([rh, rm, rl, rh, rm, rh]).astype(jnp.bfloat16)
    return lax.dot_general(
        stacked_left, stacked_right, (((0,), (0,)), ((), ())), preferred_element_type=jnp.float32
    )


def eliminate(cols, blocks, others):
    row_id = lax.broadcasted_iota(jnp.int32, blocks[0].shape, 0)
    pivots, inverses = jnp.ones_like(blocks[0]), jnp.ones_like(blocks[0])
    for j in range(0, PANEL, 2):
        first, cross = repeat(cols[j], j), repeat(cols[j], j + 1)
        corner = repeat(cols[j + 1], j + 1)
        first_inverse = recip(first)
        second_inverse = first * recip(first * corner - cross * cross)
        second = corner - cross * (cross * first_inverse)
        for i, pivot, inverse in ((j, first, first_inverse), (j + 1, second, second_inverse)):
            pivots = jnp.where(row_id == i, pivot, pivots)
            inverses = jnp.where(row_id == i, inverse, inverses)
        one = cols[j] * first_inverse
        cols[j + 1] = cols[j + 1] - one * cross
        two = cols[j + 1] * second_inverse
        for other in others:
            below = other["below"]
            other_one = below[j] * first_inverse
            below[j + 1] = below[j + 1] - other_one * cross
            other_two = below[j + 1] * second_inverse
            for m in range(j + 2, PANEL):
                a, b = repeat(cols[j], m), repeat(cols[j + 1], m)
                below[m] = (below[m] - other_one * a) - other_two * b
            for m in range(len(other["cols"])):
                a, b = repeat(below[j], m), repeat(below[j + 1], m)
                other["cols"][m] = (other["cols"][m] - other_one * a) - other_two * b
            for n, block in enumerate(blocks):
                other["blocks"][n] = other["blocks"][n] - other_one * repeat(block, j)
            other["two"] = other_two
        for m in range(j + 2, PANEL):
            a, b = repeat(cols[j], m), repeat(cols[j + 1], m)
            cols[m] = (cols[m] - one * a) - two * b
        one = jnp.where(row_id > j, one, 0.0)
        two = jnp.where(row_id > j + 1, two, 0.0)
        for n in range(len(blocks)):
            blocks[n] = blocks[n] - one * repeat(blocks[n], j)
            row = repeat(blocks[n], j + 1)
            blocks[n] = blocks[n] - two * row
            for other in others:
                other["blocks"][n] = other["blocks"][n] - other["two"] * row
    return pivots, inverses


def orthonormal_rows(inner, wide):
    width = inner.shape[1]
    both = jnp.concatenate([inner, wide], axis=1)
    matrix = [both[PANEL * k : PANEL * (k + 1)] for k in range(RANK // PANEL)]
    rows = []
    for k in range(0, len(matrix), GROUP):
        group = [[part[:, :width], part[:, width:]] for part in matrix[k : k + GROUP]]
        cols = [spread(group[0][0], PANEL * k + j) for j in range(PANEL)]
        scaled = []
        for n, blocks in enumerate(group):
            at = PANEL * (k + n)
            others = []
            for later, other in enumerate(group[n + 1 :]):
                below = [spread(other[0], at + j) for j in range(PANEL)]
                ahead = [spread(other[0], at + PANEL + j) for j in range(PANEL)] if later == 0 else []
                others.append({"below": below, "cols": ahead, "blocks": other})
            pivots, inverses = eliminate(cols, blocks, others)
            rows.append(blocks[1] * lax.rsqrt(pivots))
            scaled.append(jnp.concatenate([block * inverses for block in blocks], axis=1))
            if others:
                cols = others[0]["cols"]
        if k + GROUP < len(matrix):
            update = outer_sum(
                jnp.concatenate([blocks[0] for blocks in group]), jnp.concatenate(scaled)
            )
            for m in range(k + GROUP, len(matrix)):
                matrix[m] = matrix[m] - update[PANEL * m : PANEL * (m + 1)]
    return jnp.concatenate(rows, axis=0)


def deep_left(value):
    high, middle, low = parts_of(value)
    return jnp.concatenate([high, high, high, middle, middle, low], axis=1).astype(jnp.bfloat16)


def deep_right(value, axis):
    high, middle, low = parts_of(value)
    return jnp.concatenate([high, middle, low, high, middle, high], axis=axis).astype(jnp.bfloat16)


def basis_kernel(total_ref, snap_ref, out_ref, *, rows_all):
    cols = total_ref.shape[1]
    row_id, col_id = ids((cols, cols))
    identity = jnp.where(row_id == col_id, jnp.float32(ridge), 0.0)
    gram_matrix = unfolded(total_ref[...]) / rows_all + identity

    gram_deep = deep_right(gram_matrix, 0)
    basis = gram_matrix[:RANK]
    for step in range(ITERS):
        if step > 0:
            basis = jnp.dot(deep_left(basis), gram_deep, preferred_element_type=jnp.float32)
        full = jnp.concatenate([basis, jnp.zeros((cols - RANK, cols), jnp.float32)], axis=0)
        inner = lax.dot_general(
            deep_left(basis),
            deep_right(full, 1),
            (((1,), (1,)), ((), ())),
            preferred_element_type=jnp.float32,
        )
        basis = orthonormal_rows(inner, basis)
    blocks = out_ref.shape[0] // RANK
    basis_deep = deep_left(basis)
    for block in range(0, blocks, 2):
        pair = [snap_ref[pl.ds(block + n, cols, stride=SLOT), :] for n in range(2)]
        modes = jnp.dot(
            basis_deep,
            deep_right(jnp.concatenate(pair, axis=1), 0),
            preferred_element_type=jnp.float32,
        )
        for n in range(2):
            out_ref[pl.ds(block + n, RANK, stride=blocks), :] = modes[:, LANES * n : LANES * (n + 1)]


def project(gram_total, snapshots, rows_all):
    return pl.pallas_call(
        functools.partial(basis_kernel, rows_all=rows_all),
        out_shape=jax.ShapeDtypeStruct((RANK * 12, LANES), jnp.float32),
        in_specs=[pl.BlockSpec(memory_space=pltpu.VMEM)] * 2,
        out_specs=pl.BlockSpec(memory_space=pltpu.VMEM),
        compiler_params=pltpu.CompilerParams(vmem_limit_bytes=16 * 2**20),
        name="basis",
    )(gram_total, snapshots)


def exact_dot(values, one_hot):
    high, middle, low = (part.astype(jnp.bfloat16) for part in parts_of(values))
    dot = functools.partial(jnp.dot, preferred_element_type=jnp.float32)
    return (dot(low, one_hot) + dot(middle, one_hot)) + dot(high, one_hot)


def sorting(size, to_sorted):
    cell = lax.broadcasted_iota(jnp.int32, (size, size), 0 if to_sorted else 1)
    spot = lax.broadcasted_iota(jnp.int32, (size, size), 1 if to_sorted else 0)
    place = (cell & 3) * (size // 4) + (cell >> 2)
    return jnp.where(place == spot, 1.0, 0.0).astype(jnp.bfloat16)


def edges_kernel(velocity_ref, coef_ref, low_ref, high_ref, arrived):
    layers, rows_z = low_ref.shape[2], coef_ref.shape[1]
    copies = []
    for n, (edge_ref, start) in enumerate(((low_ref, 0), (high_ref, rows_z - layers))):
        rows = pl.ds(start, layers)
        copies += [
            pltpu.make_async_copy(velocity_ref.at[:, :, rows], edge_ref.at[:3], arrived.at[2 * n]),
            pltpu.make_async_copy(coef_ref.at[:, rows], edge_ref.at[3], arrived.at[2 * n + 1]),
        ]
    for copy in copies:
        copy.start()
    for copy in copies:
        copy.wait()


def edges(velocity, smag_coef):
    rows_y, _, size_x = smag_coef.shape
    edge = jax.ShapeDtypeStruct((4, rows_y, 4, size_x), jnp.float32)
    return pl.pallas_call(
        edges_kernel,
        out_shape=(edge, edge),
        in_specs=[pl.BlockSpec(memory_space=pltpu.HBM)] * 2,
        out_specs=[pl.BlockSpec(memory_space=pltpu.VMEM)] * 2,
        scratch_shapes=[pltpu.SemaphoreType.DMA((4,))],
        compiler_params=pltpu.CompilerParams(vmem_limit_bytes=2 * 2**20),
        name="edges",
    )(*(pltpu.with_memory_space_constraint(a, pltpu.HBM) for a in (velocity, smag_coef)))


def pack_kernel(velocity_ref, coef_ref, block_ref):
    rows_y, rows_z, size_x = coef_ref.shape
    rows = [velocity_ref[c].reshape(-1, size_x) for c in range(3)] + [coef_ref[...].reshape(-1, size_x)]
    done = exact_dot(jnp.concatenate(rows), sorting(size_x, True))
    for c in range(4):
        for y in range(rows_y):
            start = (c * rows_y + y) * rows_z
            for o in range(4):
                block_ref[c, y, o] = done[start : start + rows_z, LANES * o : LANES * (o + 1)]


def pack(velocity, smag_coef):
    rows_y, rows_z, _ = smag_coef.shape
    return pl.pallas_call(
        pack_kernel,
        out_shape=jax.ShapeDtypeStruct((4, rows_y, 4, rows_z, LANES), jnp.float32),
        in_specs=[pl.BlockSpec(memory_space=pltpu.VMEM)] * 2,
        out_specs=pl.BlockSpec(memory_space=pltpu.VMEM),
        compiler_params=pltpu.CompilerParams(vmem_limit_bytes=12 * 2**20),
        name="pack",
    )(velocity, smag_coef)


def sides_kernel(low_ref, high_ref, sides_ref, chip_ref, other_ref):
    odd = lax.axis_index("gy") % 2 == 1
    rows_y, layers, size_x = low_ref.shape[1:]
    rows = jnp.concatenate([high_ref[...], low_ref[...]], axis=2).reshape(-1, size_x)
    done = exact_dot(rows, sorting(size_x, True)).reshape(4, rows_y, 2 * layers, size_x)
    for c in range(4):
        for o in range(4):
            planes = [done[c, y, :, LANES * o : LANES * (o + 1)] for y in range(rows_y)]
            for y in range(rows_y):
                sides_ref[c, y, o] = planes[y]
            for away in range(rows_y - 1):
                upper, lower = planes[rows_y - 1 - away], planes[away]
                on_chip, off_chip = jnp.where(odd, lower, upper), jnp.where(odd, upper, lower)
                for ref, plane in ((chip_ref, on_chip), (other_ref, off_chip)):
                    if away == 0:
                        ref[c, 0, o] = plane
                    else:
                        for side, begin in enumerate((0, layers + 2)):
                            to = 4 * (away - 1) + 2 * side
                            ref[c, 1, o, to : to + 2] = plane[begin : begin + 2]


def sort_sides(low, high):
    _, rows_y, layers, _ = low.shape
    shape = lambda rows: jax.ShapeDtypeStruct((4, rows, 4, 2 * layers, LANES), jnp.float32)
    return pl.pallas_call(
        sides_kernel,
        out_shape=(shape(rows_y), shape(2), shape(2)),
        in_specs=[pl.BlockSpec(memory_space=pltpu.VMEM)] * 2,
        out_specs=[pl.BlockSpec(memory_space=pltpu.VMEM)] * 3,
        compiler_params=pltpu.CompilerParams(vmem_limit_bytes=12 * 2**20),
        cost_estimate=pl.CostEstimate(flops=2 * 10**10, bytes_accessed=10**6, transcendentals=0),
        name="sides",
    )(low, high)


def around_x(ref, index, o):
    ahead = ref[(*index, o + 1)] if o < 3 else pltpu.roll(ref[(*index, 0)], LANES - 1, 1)
    behind = ref[(*index, o - 1)] if o > 0 else pltpu.roll(ref[(*index, 3)], 1, 1)
    return ahead, behind


def around_z(plane):
    return pltpu.roll(plane, plane.shape[0] - 1, 0), pltpu.roll(plane, 1, 0)


def half_viscosity(cells_ref, y, o, coefficient):
    jump = []
    for c in range(3):
        x_ahead, x_behind = around_x(cells_ref, (c, y), o)
        z_ahead, z_behind = around_z(cells_ref[c, y, o])
        jump.append(
            (x_ahead - x_behind, cells_ref[c, y + 1, o] - cells_ref[c, y - 1, o], z_ahead - z_behind)
        )
    total = jump[0][0] ** 2 + jump[1][1] ** 2 + jump[2][2] ** 2
    total = total + total
    for c, d in ((0, 1), (0, 2), (1, 2)):
        total = total + (jump[c][d] + jump[d][c]) ** 2
    rate = coefficient * (0.5 * total * lax.rsqrt(jnp.maximum(total, 1e-37)))
    return (0.5 * nu_limit) * rate * recip(1.0 + rate)


def stepped(cells_ref, y, visc_ref, v, o):
    here = visc_ref[v, o]
    visc = [*around_x(visc_ref, (v,), o), visc_ref[v + 1, o], visc_ref[v - 1, o], *around_z(here)]
    visc = [here + other for other in visc]
    result = []
    for c in range(3):
        centre = cells_ref[c, y, o]
        cells = [
            *around_x(cells_ref, (c, y), o),
            cells_ref[c, y + 1, o],
            cells_ref[c, y - 1, o],
            *around_z(centre),
        ]
        change = visc[0] * (cells[0] - centre)
        for n in range(1, 6):
            change = change + visc[n] * (cells[n] - centre)
        result.append(centre + change)
    return result


def ids(shape):
    return lax.broadcasted_iota(jnp.int32, shape, 0), lax.broadcasted_iota(jnp.int32, shape, 1)


def folded(gram):
    half = gram.shape[0] // 2
    row, lane = ids((half, 2 * half))
    corner = pltpu.roll(gram[half:], half, 1)
    square = jnp.where(lane < row, corner, gram[:half])
    diagonal = jnp.sum(jnp.where(lane == row, corner, 0.0), axis=0, keepdims=True)
    return jnp.concatenate([square, jnp.broadcast_to(diagonal, (8, 2 * half))], axis=0)


def unfolded(parts):
    half = parts.shape[1] // 2
    row, lane = ids((half, 2 * half))
    square = parts[:half]
    upper = jnp.where(lane > row, square, 0.0)
    lower = pltpu.roll(jnp.where(lane < row, square, 0.0), half, 1)
    one_side = jnp.concatenate([upper, lower], axis=0)
    below = pltpu.roll(jnp.broadcast_to(parts[half : half + 1], square.shape), half, 1)
    diagonal = jnp.concatenate(
        [jnp.where(lane == row, square, 0.0), jnp.where(lane == row + half, below, 0.0)], axis=0
    )
    return one_side + one_side.T + diagonal


def steps_kernel(
    code_ref, block_ref, chip_ref, other_ref, sides_ref, side_chip_ref, side_other_ref,
    wide_ref, snap_ref, gram_ref,
    cells_ref, visc_ref, one_ref, two_ref, all_ref,
):
    _, rows_y, _, rows_z, _ = block_ref.shape
    cols = gram_ref.shape[1]
    place_y = lax.axis_index("gy")
    first, last, odd = place_y == 0, place_y == lax.axis_size("gy") - 1, place_y % 2 == 1

    def behind(chip, other):
        return jnp.where(first, 0.0, jnp.where(odd, chip, other))

    def ahead(chip, other):
        return jnp.where(last, 0.0, jnp.where(odd, other, chip))

    for c in range(4):
        for y in range(rows_y):
            for o in range(4):
                cells_ref[c, rows_y + y, o, :rows_z] = block_ref[c, y, o]
                chip, other = chip_ref[c, y, o], other_ref[c, y, o]
                cells_ref[c, y, o, :rows_z] = behind(chip, other)
                cells_ref[c, 2 * rows_y + y, o, :rows_z] = ahead(chip, other)
                side = (slice(rows_z, rows_z + sides_ref.shape[3]),)
                cells_ref[(c, rows_y + y, o, *side)] = sides_ref[c, y, o]
                for choose, at, away in (
                    (behind, y, rows_y - 1 - y),
                    (ahead, 2 * rows_y + y, y),
                ):
                    if away == 0:
                        halo = choose(side_chip_ref[c, 0, o], side_other_ref[c, 0, o])
                        cells_ref[(c, at, o, *side)] = halo
                    elif away <= rows_y - 2:
                        for n, begin in enumerate((rows_z, rows_z + sides_ref.shape[3] - 2)):
                            part = (c, 1, o, slice(4 * (away - 1) + 2 * n, 4 * (away - 1) + 2 * n + 2))
                            halo = choose(side_chip_ref[part], side_other_ref[part])
                            cells_ref[c, at, o, begin : begin + 2] = halo

    @pl.when(first)
    def _():
        for y in range(1, rows_y):
            cells_ref[3, y] = cells_ref[3, rows_y]

    @pl.when(last)
    def _():
        for y in range(rows_y - 1):
            cells_ref[3, 2 * rows_y + y] = cells_ref[3, 2 * rows_y - 1]

    def visc_one(y, carry):
        for o in range(4):
            visc_ref[y, o] = half_viscosity(cells_ref, y, o, cells_ref[3, y, o])
        return carry

    lax.fori_loop(1, 3 * rows_y - 1, visc_one, 0)

    def step_one(y, carry):
        outside = jnp.logical_or(
            jnp.logical_and(first, y < rows_y), jnp.logical_and(last, y >= 2 * rows_y)
        )
        for o in range(4):
            for c, cells in enumerate(stepped(cells_ref, y, visc_ref, y, o)):
                one_ref[c, y, o] = jnp.where(outside, 0.0, cells)
        return carry

    lax.fori_loop(2, 3 * rows_y - 2, step_one, 0)

    def visc_two(y, carry):
        for o in range(4):
            visc_ref[y, o] = half_viscosity(one_ref, y, o, cells_ref[3, y, o])
        return carry

    lax.fori_loop(rows_y - 1, 2 * rows_y + 1, visc_two, 0)

    for y in range(rows_y):
        for o in range(4):
            for c, cells in enumerate(stepped(one_ref, rows_y + y, visc_ref, rows_y + y, o)):
                two_ref[c, y, o] = cells[:rows_z]
                start = (c * rows_y + y) * rows_z
                wide_ref[start : start + rows_z, LANES * o : LANES * (o + 1)] = cells[:rows_z]
    for state, (ref, shift) in enumerate(((block_ref, 0), (one_ref, rows_y), (two_ref, 0))):
        for y in range(rows_y):
            for z in range(4):
                for o in range(4):
                    start = SLOT * (64 * state + 16 * y + 4 * z + o)
                    for c in range(3):
                        piece = ref[c, shift + y, o, pl.ds(z, rows_z // 4, stride=4), :]
                        all_ref[start + 4 * c : start + 4 * c + 4, :] = piece

    def pick(column, carry):
        source = pl.multiple_of(code_ref[column] * SLOT, SLOT)
        target = pl.multiple_of(column * SLOT, SLOT)
        snap_ref[pl.ds(target, SLOT), :] = all_ref[pl.ds(source, SLOT), :]
        return carry

    lax.fori_loop(0, cols, pick, 0, unroll=16)
    even, odd = jnp.zeros((cols, cols), jnp.float32), jnp.zeros((cols, cols), jnp.float32)
    across = functools.partial(
        lax.dot_general,
        dimension_numbers=(((1,), (1,)), ((), ())),
        preferred_element_type=jnp.float32,
    )
    for block in range(0, 12, 2):
        part = jnp.concatenate(
            [snap_ref[pl.ds(block + i, cols, stride=SLOT), :] for i in range(2)], axis=1
        )
        high, middle, low = (p.astype(jnp.bfloat16) for p in parts_of(part))
        odd = odd + (across(high, low) + across(high, middle))
        even = even + (across(middle, middle) + across(high, high))
    gram_ref[...] = folded(even + (odd + odd.T))


def unsort_kernel(wide_ref, final_ref):
    final_ref[...] = exact_dot(wide_ref[...], sorting(wide_ref.shape[1], False)).reshape(final_ref.shape)


def unsort(wide, shape):
    return pl.pallas_call(
        unsort_kernel,
        out_shape=jax.ShapeDtypeStruct(shape, jnp.float32),
        in_specs=[pl.BlockSpec(memory_space=pltpu.VMEM)],
        out_specs=pl.BlockSpec(memory_space=pltpu.VMEM),
        compiler_params=pltpu.CompilerParams(vmem_limit_bytes=12 * 2**20),
        cost_estimate=pl.CostEstimate(flops=4 * 10**9, bytes_accessed=10**6, transcendentals=0),
        name="unsort",
    )(wide)


def both_steps(snap_code, block, *halo):
    _, rows_y, _, rows_z, _ = block.shape
    cols = snap_code.shape[0]
    f32 = lambda *shape: jax.ShapeDtypeStruct(shape, jnp.float32)
    scratch = lambda *shape: pltpu.VMEM(shape, jnp.float32)
    depth = rows_z + 8
    return pl.pallas_call(
        steps_kernel,
        out_shape=(
            f32(3 * rows_y * rows_z, 4 * LANES),
            f32(SLOT * cols, LANES),
            f32(cols // 2 + 8, cols),
        ),
        in_specs=[pl.BlockSpec(memory_space=pltpu.SMEM)]
        + [pl.BlockSpec(memory_space=pltpu.VMEM)] * (1 + len(halo)),
        out_specs=[pl.BlockSpec(memory_space=pltpu.VMEM)] * 3,
        scratch_shapes=[
            scratch(4, 3 * rows_y, 4, depth, LANES),
            scratch(3 * rows_y, 4, depth, LANES),
            scratch(3, 3 * rows_y, 4, depth, LANES),
            scratch(3, rows_y, 4, rows_z, LANES),
            scratch(SLOT * 192, LANES),
        ],
        compiler_params=pltpu.CompilerParams(vmem_limit_bytes=32 * 2**20),
        name="steps",
    )(snap_code, block, *halo)


def device_sum(part):
    axes = ("gy", "gz")
    size_z, size_x = 8, lax.axis_size("gz")
    moves = {
        "core": lambda x, y, z, core: (x, y, z, core ^ 1),
        "x1": lambda x, y, z, core: (x ^ 1, y, z, core),
        "x3": lambda x, y, z, core: (x ^ 3, y, z, core),
        "y1": lambda x, y, z, core: (x, y ^ 1, z, core),
        "y3": lambda x, y, z, core: (x, y ^ 3, z, core),
        "za": lambda x, y, z, core: (x, y, z ^ 1, core),
        "zb": lambda x, y, z, core: (x, y, (((z + 1) ^ 1) - 1) % size_z, core),
        "zc": lambda x, y, z, core: (x, y, size_z - 1 - z if z % 4 in (1, 2) else z ^ 3, core),
    }
    orders = (
        ("core", "x1", "za", "y1", "zb", "x3", "zc", "y3"),
        ("core", "za", "x1", "zb", "y1", "zc", "y3", "x3"),
    )

    def partner(step, device):
        row, x = divmod(device, size_x)
        core, z, y = row % 2, row // 2 % size_z, row // (2 * size_z)
        x, y, z, core = moves[orders[core][step]](x, y, z, core)
        return ((y * size_z + z) * 2 + core) * size_x + x

    count = lax.axis_size("gy") * size_x
    for step in range(len(moves)):
        pairs = [(device, partner(step, device)) for device in range(count)]
        part = part + lax.ppermute(part, axes, pairs)
    return part


def local(velocity, smag_coef, snap_code):
    count_y, count_z = lax.axis_size("gy"), lax.axis_size("gz")

    def along_z(part, step):
        return lax.ppermute(part, "gz", [(i, (i + step) % count_z) for i in range(count_z)])

    def on_chip(part):
        return lax.ppermute(part, "gy", [(i, i ^ 1) for i in range(count_y)])

    def off_chip(part):
        partners = [min(max(((i + 1) ^ 1) - 1, 0), count_y - 1) for i in range(count_y)]
        return lax.ppermute(part, "gy", list(enumerate(partners)))

    low, high = edges(velocity, smag_coef)
    velocity, smag_coef, low, high = lax.optimization_barrier((velocity, smag_coef, low, high))
    sides, side_chip, side_other = sort_sides(along_z(high, 1), along_z(low, -1))
    block = pack(velocity, smag_coef)
    wide, snapshots, gram = both_steps(
        snap_code, block, on_chip(block), off_chip(block), sides, on_chip(side_chip), off_chip(side_other)
    )
    rows_y, rows_z = velocity.shape[1], velocity.shape[2]
    rows_all = 12 * LANES * count_y * count_z
    pod_modes = project(device_sum(gram), snapshots, rows_all)
    return (unsort(wide, velocity.shape), pod_modes.reshape(RANK, 3, rows_y // 4, rows_z // 4, LANES))


def solution(mesh):
    placed = (P(None, "gy", "gz", None), P("gy", "gz", None), P())
    return jax.shard_map(
        local,
        mesh=mesh,
        in_specs=placed,
        out_specs=(P(None, "gy", "gz", None), P(None, None, "gy", "gz", None)),
        check_vma=False,
    )
```

```python
import functools

import jax
import jax.numpy as jnp
from jax import lax
from jax.experimental import pallas as pl
from jax.experimental.pallas import tpu as pltpu
from jax.sharding import PartitionSpec as P

RANK = 112
ITERS = 3
PANEL = 8
GROUP = 5
LANES = 128
SLOT = 16


nu_limit = 0.125
ridge = 1.0
highest = lax.Precision.HIGHEST


def recip(value):
    return pltpu.reciprocal(value, approx=True)


def spread(block, lane):
    return jnp.broadcast_to(block[:, lane : lane + 1], block.shape)


def repeat(block, row):
    return jnp.broadcast_to(block[row : row + 1, :], block.shape)


def parts_of(value):
    high = value.astype(jnp.bfloat16).astype(jnp.float32)
    rest = value - high
    middle = rest.astype(jnp.bfloat16).astype(jnp.float32)
    return high, middle, rest - middle


def outer_sum(left, right):
    lh, lm, ll = parts_of(left)
    rh, rm, rl = parts_of(right)
    stacked_left = jnp.concatenate([lh, lh, lh, lm, lm, ll]).astype(jnp.bfloat16)
    stacked_right = jnp.concatenate([rh, rm, rl, rh, rm, rh]).astype(jnp.bfloat16)
    return lax.dot_general(
        stacked_left, stacked_right, (((0,), (0,)), ((), ())), preferred_element_type=jnp.float32
    )


def eliminate(cols, blocks, others):
    row_id = lax.broadcasted_iota(jnp.int32, blocks[0].shape, 0)
    pivots, inverses = jnp.ones_like(blocks[0]), jnp.ones_like(blocks[0])
    for j in range(0, PANEL, 2):
        first, cross = repeat(cols[j], j), repeat(cols[j], j + 1)
        corner = repeat(cols[j + 1], j + 1)
        first_inverse = recip(first)
        second_inverse = first * recip(first * corner - cross * cross)
        second = corner - cross * (cross * first_inverse)
        for i, pivot, inverse in ((j, first, first_inverse), (j + 1, second, second_inverse)):
            pivots = jnp.where(row_id == i, pivot, pivots)
            inverses = jnp.where(row_id == i, inverse, inverses)
        one = cols[j] * first_inverse
        cols[j + 1] = cols[j + 1] - one * cross
        two = cols[j + 1] * second_inverse
        for other in others:
            below = other["below"]
            other_one = below[j] * first_inverse
            below[j + 1] = below[j + 1] - other_one * cross
            other_two = below[j + 1] * second_inverse
            for m in range(j + 2, PANEL):
                a, b = repeat(cols[j], m), repeat(cols[j + 1], m)
                below[m] = (below[m] - other_one * a) - other_two * b
            for m in range(len(other["cols"])):
                a, b = repeat(below[j], m), repeat(below[j + 1], m)
                other["cols"][m] = (other["cols"][m] - other_one * a) - other_two * b
            for n, block in enumerate(blocks):
                other["blocks"][n] = other["blocks"][n] - other_one * repeat(block, j)
            other["two"] = other_two
        for m in range(j + 2, PANEL):
            a, b = repeat(cols[j], m), repeat(cols[j + 1], m)
            cols[m] = (cols[m] - one * a) - two * b
        one = jnp.where(row_id > j, one, 0.0)
        two = jnp.where(row_id > j + 1, two, 0.0)
        for n in range(len(blocks)):
            blocks[n] = blocks[n] - one * repeat(blocks[n], j)
            row = repeat(blocks[n], j + 1)
            blocks[n] = blocks[n] - two * row
            for other in others:
                other["blocks"][n] = other["blocks"][n] - other["two"] * row
    return pivots, inverses


def orthonormal_rows(inner, wide):
    width = inner.shape[1]
    both = jnp.concatenate([inner, wide], axis=1)
    matrix = [both[PANEL * k : PANEL * (k + 1)] for k in range(RANK // PANEL)]
    rows = []
    for k in range(0, len(matrix), GROUP):
        group = [[part[:, :width], part[:, width:]] for part in matrix[k : k + GROUP]]
        cols = [spread(group[0][0], PANEL * k + j) for j in range(PANEL)]
        scaled = []
        for n, blocks in enumerate(group):
            at = PANEL * (k + n)
            others = []
            for later, other in enumerate(group[n + 1 :]):
                below = [spread(other[0], at + j) for j in range(PANEL)]
                ahead = [spread(other[0], at + PANEL + j) for j in range(PANEL)] if later == 0 else []
                others.append({"below": below, "cols": ahead, "blocks": other})
            pivots, inverses = eliminate(cols, blocks, others)
            rows.append(blocks[1] * lax.rsqrt(pivots))
            scaled.append(jnp.concatenate([block * inverses for block in blocks], axis=1))
            if others:
                cols = others[0]["cols"]
        if k + GROUP < len(matrix):
            update = outer_sum(
                jnp.concatenate([blocks[0] for blocks in group]), jnp.concatenate(scaled)
            )
            for m in range(k + GROUP, len(matrix)):
                matrix[m] = matrix[m] - update[PANEL * m : PANEL * (m + 1)]
    return jnp.concatenate(rows, axis=0)


def deep_left(value):
    high, middle, low = parts_of(value)
    return jnp.concatenate([high, high, high, middle, middle, low], axis=1).astype(jnp.bfloat16)


def deep_right(value, axis):
    high, middle, low = parts_of(value)
    return jnp.concatenate([high, middle, low, high, middle, high], axis=axis).astype(jnp.bfloat16)


def basis_kernel(total_ref, snap_ref, out_ref, *, rows_all):
    cols = total_ref.shape[1]
    row_id, col_id = ids((cols, cols))
    identity = jnp.where(row_id == col_id, jnp.float32(ridge), 0.0)
    gram_matrix = unfolded(total_ref[...]) / rows_all + identity

    gram_deep = deep_right(gram_matrix, 0)
    basis = gram_matrix[:RANK]
    for step in range(ITERS):
        if step > 0:
            basis = jnp.dot(deep_left(basis), gram_deep, preferred_element_type=jnp.float32)
        full = jnp.concatenate([basis, jnp.zeros((cols - RANK, cols), jnp.float32)], axis=0)
        inner = lax.dot_general(
            deep_left(basis),
            deep_right(full, 1),
            (((1,), (1,)), ((), ())),
            preferred_element_type=jnp.float32,
        )
        basis = orthonormal_rows(inner, basis)
    blocks = out_ref.shape[0] // RANK
    basis_deep = deep_left(basis)
    for block in range(0, blocks, 2):
        pair = [snap_ref[pl.ds(block + n, cols, stride=SLOT), :] for n in range(2)]
        modes = jnp.dot(
            basis_deep,
            deep_right(jnp.concatenate(pair, axis=1), 0),
            preferred_element_type=jnp.float32,
        )
        for n in range(2):
            out_ref[pl.ds(block + n, RANK, stride=blocks), :] = modes[:, LANES * n : LANES * (n + 1)]


def project(gram_total, snapshots, rows_all):
    return pl.pallas_call(
        functools.partial(basis_kernel, rows_all=rows_all),
        out_shape=jax.ShapeDtypeStruct((RANK * 12, LANES), jnp.float32),
        in_specs=[pl.BlockSpec(memory_space=pltpu.VMEM)] * 2,
        out_specs=pl.BlockSpec(memory_space=pltpu.VMEM),
        compiler_params=pltpu.CompilerParams(vmem_limit_bytes=16 * 2**20),
        name="basis",
    )(gram_total, snapshots)


def exact_dot(values, one_hot):
    high, middle, low = (part.astype(jnp.bfloat16) for part in parts_of(values))
    dot = functools.partial(jnp.dot, preferred_element_type=jnp.float32)
    return (dot(low, one_hot) + dot(middle, one_hot)) + dot(high, one_hot)


def sorting(size, to_sorted):
    cell = lax.broadcasted_iota(jnp.int32, (size, size), 0 if to_sorted else 1)
    spot = lax.broadcasted_iota(jnp.int32, (size, size), 1 if to_sorted else 0)
    place = (cell & 3) * (size // 4) + (cell >> 2)
    return jnp.where(place == spot, 1.0, 0.0).astype(jnp.bfloat16)


def edges_kernel(velocity_ref, coef_ref, low_ref, high_ref, arrived):
    layers, rows_z = low_ref.shape[2], coef_ref.shape[1]
    copies = []
    for n, (edge_ref, start) in enumerate(((low_ref, 0), (high_ref, rows_z - layers))):
        rows = pl.ds(start, layers)
        copies += [
            pltpu.make_async_copy(velocity_ref.at[:, :, rows], edge_ref.at[:3], arrived.at[2 * n]),
            pltpu.make_async_copy(coef_ref.at[:, rows], edge_ref.at[3], arrived.at[2 * n + 1]),
        ]
    for copy in copies:
        copy.start()
    for copy in copies:
        copy.wait()


def edges(velocity, smag_coef):
    rows_y, _, size_x = smag_coef.shape
    edge = jax.ShapeDtypeStruct((4, rows_y, 4, size_x), jnp.float32)
    return pl.pallas_call(
        edges_kernel,
        out_shape=(edge, edge),
        in_specs=[pl.BlockSpec(memory_space=pltpu.HBM)] * 2,
        out_specs=[pl.BlockSpec(memory_space=pltpu.VMEM)] * 2,
        scratch_shapes=[pltpu.SemaphoreType.DMA((4,))],
        compiler_params=pltpu.CompilerParams(vmem_limit_bytes=2 * 2**20),
        name="edges",
    )(*(pltpu.with_memory_space_constraint(a, pltpu.HBM) for a in (velocity, smag_coef)))


def pack_kernel(velocity_ref, coef_ref, block_ref):
    rows_y, rows_z, size_x = coef_ref.shape
    rows = [velocity_ref[c].reshape(-1, size_x) for c in range(3)] + [coef_ref[...].reshape(-1, size_x)]
    done = exact_dot(jnp.concatenate(rows), sorting(size_x, True))
    for c in range(4):
        for y in range(rows_y):
            start = (c * rows_y + y) * rows_z
            for o in range(4):
                block_ref[c, y, o] = done[start : start + rows_z, LANES * o : LANES * (o + 1)]


def pack(velocity, smag_coef):
    rows_y, rows_z, _ = smag_coef.shape
    return pl.pallas_call(
        pack_kernel,
        out_shape=jax.ShapeDtypeStruct((4, rows_y, 4, rows_z, LANES), jnp.float32),
        in_specs=[pl.BlockSpec(memory_space=pltpu.VMEM)] * 2,
        out_specs=pl.BlockSpec(memory_space=pltpu.VMEM),
        compiler_params=pltpu.CompilerParams(vmem_limit_bytes=12 * 2**20),
        name="pack",
    )(velocity, smag_coef)


def sides_kernel(low_ref, high_ref, sides_ref, chip_ref, other_ref):
    odd = lax.axis_index("gy") % 2 == 1
    rows_y, layers, size_x = low_ref.shape[1:]
    rows = jnp.concatenate([high_ref[...], low_ref[...]], axis=2).reshape(-1, size_x)
    done = exact_dot(rows, sorting(size_x, True)).reshape(4, rows_y, 2 * layers, size_x)
    for c in range(4):
        for o in range(4):
            planes = [done[c, y, :, LANES * o : LANES * (o + 1)] for y in range(rows_y)]
            for y in range(rows_y):
                sides_ref[c, y, o] = planes[y]
            for away in range(rows_y - 1):
                upper, lower = planes[rows_y - 1 - away], planes[away]
                on_chip, off_chip = jnp.where(odd, lower, upper), jnp.where(odd, upper, lower)
                for ref, plane in ((chip_ref, on_chip), (other_ref, off_chip)):
                    if away == 0:
                        ref[c, 0, o] = plane
                    else:
                        for side, begin in enumerate((0, layers + 2)):
                            to = 4 * (away - 1) + 2 * side
                            ref[c, 1, o, to : to + 2] = plane[begin : begin + 2]


def sort_sides(low, high):
    _, rows_y, layers, _ = low.shape
    shape = lambda rows: jax.ShapeDtypeStruct((4, rows, 4, 2 * layers, LANES), jnp.float32)
    return pl.pallas_call(
        sides_kernel,
        out_shape=(shape(rows_y), shape(2), shape(2)),
        in_specs=[pl.BlockSpec(memory_space=pltpu.VMEM)] * 2,
        out_specs=[pl.BlockSpec(memory_space=pltpu.VMEM)] * 3,
        compiler_params=pltpu.CompilerParams(vmem_limit_bytes=12 * 2**20),
        cost_estimate=pl.CostEstimate(flops=2 * 10**10, bytes_accessed=10**6, transcendentals=0),
        name="sides",
    )(low, high)


def around_x(ref, index, o):
    ahead = ref[(*index, o + 1)] if o < 3 else pltpu.roll(ref[(*index, 0)], LANES - 1, 1)
    behind = ref[(*index, o - 1)] if o > 0 else pltpu.roll(ref[(*index, 3)], 1, 1)
    return ahead, behind


def around_z(plane):
    return pltpu.roll(plane, plane.shape[0] - 1, 0), pltpu.roll(plane, 1, 0)


def half_viscosity(cells_ref, y, o, coefficient):
    jump = []
    for c in range(3):
        x_ahead, x_behind = around_x(cells_ref, (c, y), o)
        z_ahead, z_behind = around_z(cells_ref[c, y, o])
        jump.append(
            (x_ahead - x_behind, cells_ref[c, y + 1, o] - cells_ref[c, y - 1, o], z_ahead - z_behind)
        )
    total = jump[0][0] ** 2 + jump[1][1] ** 2 + jump[2][2] ** 2
    total = total + total
    for c, d in ((0, 1), (0, 2), (1, 2)):
        total = total + (jump[c][d] + jump[d][c]) ** 2
    rate = coefficient * (0.5 * total * lax.rsqrt(jnp.maximum(total, 1e-37)))
    return (0.5 * nu_limit) * rate * recip(1.0 + rate)


def stepped(cells_ref, y, visc_ref, v, o):
    here = visc_ref[v, o]
    visc = [*around_x(visc_ref, (v,), o), visc_ref[v + 1, o], visc_ref[v - 1, o], *around_z(here)]
    visc = [here + other for other in visc]
    result = []
    for c in range(3):
        centre = cells_ref[c, y, o]
        cells = [
            *around_x(cells_ref, (c, y), o),
            cells_ref[c, y + 1, o],
            cells_ref[c, y - 1, o],
            *around_z(centre),
        ]
        change = visc[0] * (cells[0] - centre)
        for n in range(1, 6):
            change = change + visc[n] * (cells[n] - centre)
        result.append(centre + change)
    return result


def ids(shape):
    return lax.broadcasted_iota(jnp.int32, shape, 0), lax.broadcasted_iota(jnp.int32, shape, 1)


def folded(gram):
    half = gram.shape[0] // 2
    row, lane = ids((half, 2 * half))
    corner = pltpu.roll(gram[half:], half, 1)
    square = jnp.where(lane < row, corner, gram[:half])
    diagonal = jnp.sum(jnp.where(lane == row, corner, 0.0), axis=0, keepdims=True)
    return jnp.concatenate([square, jnp.broadcast_to(diagonal, (8, 2 * half))], axis=0)


def unfolded(parts):
    half = parts.shape[1] // 2
    row, lane = ids((half, 2 * half))
    square = parts[:half]
    upper = jnp.where(lane > row, square, 0.0)
    lower = pltpu.roll(jnp.where(lane < row, square, 0.0), half, 1)
    one_side = jnp.concatenate([upper, lower], axis=0)
    below = pltpu.roll(jnp.broadcast_to(parts[half : half + 1], square.shape), half, 1)
    diagonal = jnp.concatenate(
        [jnp.where(lane == row, square, 0.0), jnp.where(lane == row + half, below, 0.0)], axis=0
    )
    return one_side + one_side.T + diagonal


def steps_kernel(
    code_ref, block_ref, chip_ref, other_ref, sides_ref, side_chip_ref, side_other_ref,
    wide_ref, snap_ref, gram_ref,
    cells_ref, visc_ref, one_ref, two_ref, all_ref,
):
    _, rows_y, _, rows_z, _ = block_ref.shape
    cols = gram_ref.shape[1]
    place_y = lax.axis_index("gy")
    first, last, odd = place_y == 0, place_y == lax.axis_size("gy") - 1, place_y % 2 == 1

    def behind(chip, other):
        return jnp.where(first, 0.0, jnp.where(odd, chip, other))

    def ahead(chip, other):
        return jnp.where(last, 0.0, jnp.where(odd, other, chip))

    for c in range(4):
        for y in range(rows_y):
            for o in range(4):
                cells_ref[c, rows_y + y, o, :rows_z] = block_ref[c, y, o]
                chip, other = chip_ref[c, y, o], other_ref[c, y, o]
                cells_ref[c, y, o, :rows_z] = behind(chip, other)
                cells_ref[c, 2 * rows_y + y, o, :rows_z] = ahead(chip, other)
                side = (slice(rows_z, rows_z + sides_ref.shape[3]),)
                cells_ref[(c, rows_y + y, o, *side)] = sides_ref[c, y, o]
                for choose, at, away in (
                    (behind, y, rows_y - 1 - y),
                    (ahead, 2 * rows_y + y, y),
                ):
                    if away == 0:
                        halo = choose(side_chip_ref[c, 0, o], side_other_ref[c, 0, o])
                        cells_ref[(c, at, o, *side)] = halo
                    elif away <= rows_y - 2:
                        for n, begin in enumerate((rows_z, rows_z + sides_ref.shape[3] - 2)):
                            part = (c, 1, o, slice(4 * (away - 1) + 2 * n, 4 * (away - 1) + 2 * n + 2))
                            halo = choose(side_chip_ref[part], side_other_ref[part])
                            cells_ref[c, at, o, begin : begin + 2] = halo

    @pl.when(first)
    def _():
        for y in range(1, rows_y):
            cells_ref[3, y] = cells_ref[3, rows_y]

    @pl.when(last)
    def _():
        for y in range(rows_y - 1):
            cells_ref[3, 2 * rows_y + y] = cells_ref[3, 2 * rows_y - 1]

    def visc_one(y, carry):
        for o in range(4):
            visc_ref[y, o] = half_viscosity(cells_ref, y, o, cells_ref[3, y, o])
        return carry

    lax.fori_loop(1, 3 * rows_y - 1, visc_one, 0)

    def step_one(y, carry):
        outside = jnp.logical_or(
            jnp.logical_and(first, y < rows_y), jnp.logical_and(last, y >= 2 * rows_y)
        )
        for o in range(4):
            for c, cells in enumerate(stepped(cells_ref, y, visc_ref, y, o)):
                one_ref[c, y, o] = jnp.where(outside, 0.0, cells)
        return carry

    lax.fori_loop(2, 3 * rows_y - 2, step_one, 0)

    def visc_two(y, carry):
        for o in range(4):
            visc_ref[y, o] = half_viscosity(one_ref, y, o, cells_ref[3, y, o])
        return carry

    lax.fori_loop(rows_y - 1, 2 * rows_y + 1, visc_two, 0)

    for y in range(rows_y):
        for o in range(4):
            for c, cells in enumerate(stepped(one_ref, rows_y + y, visc_ref, rows_y + y, o)):
                two_ref[c, y, o] = cells[:rows_z]
                start = (c * rows_y + y) * rows_z
                wide_ref[start : start + rows_z, LANES * o : LANES * (o + 1)] = cells[:rows_z]
    for state, (ref, shift) in enumerate(((block_ref, 0), (one_ref, rows_y), (two_ref, 0))):
        for y in range(rows_y):
            for z in range(4):
                for o in range(4):
                    start = SLOT * (64 * state + 16 * y + 4 * z + o)
                    for c in range(3):
                        piece = ref[c, shift + y, o, pl.ds(z, rows_z // 4, stride=4), :]
                        all_ref[start + 4 * c : start + 4 * c + 4, :] = piece

    def pick(column, carry):
        source = pl.multiple_of(code_ref[column] * SLOT, SLOT)
        target = pl.multiple_of(column * SLOT, SLOT)
        snap_ref[pl.ds(target, SLOT), :] = all_ref[pl.ds(source, SLOT), :]
        return carry

    lax.fori_loop(0, cols, pick, 0, unroll=16)
    even, odd = jnp.zeros((cols, cols), jnp.float32), jnp.zeros((cols, cols), jnp.float32)
    across = functools.partial(
        lax.dot_general,
        dimension_numbers=(((1,), (1,)), ((), ())),
        preferred_element_type=jnp.float32,
    )
    for block in range(0, 12, 2):
        part = jnp.concatenate(
            [snap_ref[pl.ds(block + i, cols, stride=SLOT), :] for i in range(2)], axis=1
        )
        high, middle, low = (p.astype(jnp.bfloat16) for p in parts_of(part))
        odd = odd + (across(high, low) + across(high, middle))
        even = even + (across(middle, middle) + across(high, high))
    gram_ref[...] = folded(even + (odd + odd.T))


def unsort_kernel(wide_ref, final_ref):
    final_ref[...] = exact_dot(wide_ref[...], sorting(wide_ref.shape[1], False)).reshape(final_ref.shape)


def unsort(wide, shape):
    return pl.pallas_call(
        unsort_kernel,
        out_shape=jax.ShapeDtypeStruct(shape, jnp.float32),
        in_specs=[pl.BlockSpec(memory_space=pltpu.VMEM)],
        out_specs=pl.BlockSpec(memory_space=pltpu.VMEM),
        compiler_params=pltpu.CompilerParams(vmem_limit_bytes=12 * 2**20),
        cost_estimate=pl.CostEstimate(flops=4 * 10**9, bytes_accessed=10**6, transcendentals=0),
        name="unsort",
    )(wide)


def both_steps(snap_code, block, *halo):
    _, rows_y, _, rows_z, _ = block.shape
    cols = snap_code.shape[0]
    f32 = lambda *shape: jax.ShapeDtypeStruct(shape, jnp.float32)
    scratch = lambda *shape: pltpu.VMEM(shape, jnp.float32)
    depth = rows_z + 8
    return pl.pallas_call(
        steps_kernel,
        out_shape=(
            f32(3 * rows_y * rows_z, 4 * LANES),
            f32(SLOT * cols, LANES),
            f32(cols // 2 + 8, cols),
        ),
        in_specs=[pl.BlockSpec(memory_space=pltpu.SMEM)]
        + [pl.BlockSpec(memory_space=pltpu.VMEM)] * (1 + len(halo)),
        out_specs=[pl.BlockSpec(memory_space=pltpu.VMEM)] * 3,
        scratch_shapes=[
            scratch(4, 3 * rows_y, 4, depth, LANES),
            scratch(3 * rows_y, 4, depth, LANES),
            scratch(3, 3 * rows_y, 4, depth, LANES),
            scratch(3, rows_y, 4, rows_z, LANES),
            scratch(SLOT * 192, LANES),
        ],
        compiler_params=pltpu.CompilerParams(vmem_limit_bytes=32 * 2**20),
        name="steps",
    )(snap_code, block, *halo)


def device_sum(part):
    axes = ("gy", "gz")
    size_z, size_x = 8, lax.axis_size("gz")
    rounds = (
        [lambda x, y, z, core: (x, y, z, core ^ 1)],
        [lambda x, y, z, core, bits=bits: (x ^ bits, y, z, core) for bits in (1, 2, 3)],
        [lambda x, y, z, core, bits=bits: (x, y ^ bits, z, core) for bits in (1, 2, 3)],
        [lambda x, y, z, core, bits=bits: (x, y, z ^ bits, core) for bits in (1, 2, 3)],
        [lambda x, y, z, core: (x, y, size_z - 1 - z, core)],
    )

    def partner(move, device):
        row, x = divmod(device, size_x)
        x, y, z, core = move(x, row // (2 * size_z), row // 2 % size_z, row % 2)
        return ((y * size_z + z) * 2 + core) * size_x + x

    count = lax.axis_size("gy") * size_x
    for moves in rounds:
        others = [
            lax.ppermute(part, axes, [(device, partner(move, device)) for device in range(count)])
            for move in moves
        ]
        part = part + sum(others[1:], others[0])
    return part


def local(velocity, smag_coef, snap_code):
    count_y, count_z = lax.axis_size("gy"), lax.axis_size("gz")

    def along_z(part, step):
        return lax.ppermute(part, "gz", [(i, (i + step) % count_z) for i in range(count_z)])

    def on_chip(part):
        return lax.ppermute(part, "gy", [(i, i ^ 1) for i in range(count_y)])

    def off_chip(part):
        partners = [min(max(((i + 1) ^ 1) - 1, 0), count_y - 1) for i in range(count_y)]
        return lax.ppermute(part, "gy", list(enumerate(partners)))

    low, high = edges(velocity, smag_coef)
    velocity, smag_coef, low, high = lax.optimization_barrier((velocity, smag_coef, low, high))
    sides, side_chip, side_other = sort_sides(along_z(high, 1), along_z(low, -1))
    block = pack(velocity, smag_coef)
    wide, snapshots, gram = both_steps(
        snap_code, block, on_chip(block), off_chip(block), sides, on_chip(side_chip), off_chip(side_other)
    )
    rows_y, rows_z = velocity.shape[1], velocity.shape[2]
    rows_all = 12 * LANES * count_y * count_z
    pod_modes = project(device_sum(gram), snapshots, rows_all)
    return (unsort(wide, velocity.shape), pod_modes.reshape(RANK, 3, rows_y // 4, rows_z // 4, LANES))


def solution(mesh):
    placed = (P(None, "gy", "gz", None), P("gy", "gz", None), P())
    return jax.shard_map(
        local,
        mesh=mesh,
        in_specs=placed,
        out_specs=(P(None, "gy", "gz", None), P(None, None, "gy", "gz", None)),
        check_vma=False,
    )
```

```python
import functools

import jax
import jax.numpy as jnp
from jax import lax
from jax.experimental import pallas as pl
from jax.experimental.pallas import tpu as pltpu
from jax.sharding import PartitionSpec as P

RANK = 112
ITERS = 3
PANEL = 8
GROUP = 5
LANES = 128
SLOT = 16
EDGE = 8


nu_limit = 0.125
ridge = 1.0
highest = lax.Precision.HIGHEST


def recip(value):
    return pltpu.reciprocal(value, approx=True)


def spread(block, lane):
    return jnp.broadcast_to(block[:, lane : lane + 1], block.shape)


def repeat(block, row):
    return jnp.broadcast_to(block[row : row + 1, :], block.shape)


def parts_of(value):
    high = value.astype(jnp.bfloat16).astype(jnp.float32)
    rest = value - high
    middle = rest.astype(jnp.bfloat16).astype(jnp.float32)
    return high, middle, rest - middle


def outer_sum(left, right):
    lh, lm, ll = parts_of(left)
    rh, rm, rl = parts_of(right)
    stacked_left = jnp.concatenate([lh, lh, lh, lm, lm, ll]).astype(jnp.bfloat16)
    stacked_right = jnp.concatenate([rh, rm, rl, rh, rm, rh]).astype(jnp.bfloat16)
    return lax.dot_general(
        stacked_left, stacked_right, (((0,), (0,)), ((), ())), preferred_element_type=jnp.float32
    )


def eliminate(cols, blocks, others):
    row_id = lax.broadcasted_iota(jnp.int32, blocks[0].shape, 0)
    pivots, inverses = jnp.ones_like(blocks[0]), jnp.ones_like(blocks[0])
    for j in range(0, PANEL, 2):
        first, cross = repeat(cols[j], j), repeat(cols[j], j + 1)
        corner = repeat(cols[j + 1], j + 1)
        first_inverse = recip(first)
        second_inverse = first * recip(first * corner - cross * cross)
        second = corner - cross * (cross * first_inverse)
        for i, pivot, inverse in ((j, first, first_inverse), (j + 1, second, second_inverse)):
            pivots = jnp.where(row_id == i, pivot, pivots)
            inverses = jnp.where(row_id == i, inverse, inverses)
        one = cols[j] * first_inverse
        cols[j + 1] = cols[j + 1] - one * cross
        two = cols[j + 1] * second_inverse
        for other in others:
            below = other["below"]
            other_one = below[j] * first_inverse
            below[j + 1] = below[j + 1] - other_one * cross
            other_two = below[j + 1] * second_inverse
            for m in range(j + 2, PANEL):
                a, b = repeat(cols[j], m), repeat(cols[j + 1], m)
                below[m] = (below[m] - other_one * a) - other_two * b
            for m in range(len(other["cols"])):
                a, b = repeat(below[j], m), repeat(below[j + 1], m)
                other["cols"][m] = (other["cols"][m] - other_one * a) - other_two * b
            for n, block in enumerate(blocks):
                other["blocks"][n] = other["blocks"][n] - other_one * repeat(block, j)
            other["two"] = other_two
        for m in range(j + 2, PANEL):
            a, b = repeat(cols[j], m), repeat(cols[j + 1], m)
            cols[m] = (cols[m] - one * a) - two * b
        one = jnp.where(row_id > j, one, 0.0)
        two = jnp.where(row_id > j + 1, two, 0.0)
        for n in range(len(blocks)):
            blocks[n] = blocks[n] - one * repeat(blocks[n], j)
            row = repeat(blocks[n], j + 1)
            blocks[n] = blocks[n] - two * row
            for other in others:
                other["blocks"][n] = other["blocks"][n] - other["two"] * row
    return pivots, inverses


def orthonormal_rows(inner, wide):
    width = inner.shape[1]
    both = jnp.concatenate([inner, wide], axis=1)
    matrix = [both[PANEL * k : PANEL * (k + 1)] for k in range(RANK // PANEL)]
    rows = []
    for k in range(0, len(matrix), GROUP):
        group = [[part[:, :width], part[:, width:]] for part in matrix[k : k + GROUP]]
        cols = [spread(group[0][0], PANEL * k + j) for j in range(PANEL)]
        scaled = []
        for n, blocks in enumerate(group):
            at = PANEL * (k + n)
            others = []
            for later, other in enumerate(group[n + 1 :]):
                below = [spread(other[0], at + j) for j in range(PANEL)]
                ahead = [spread(other[0], at + PANEL + j) for j in range(PANEL)] if later == 0 else []
                others.append({"below": below, "cols": ahead, "blocks": other})
            pivots, inverses = eliminate(cols, blocks, others)
            rows.append(blocks[1] * lax.rsqrt(pivots))
            scaled.append(jnp.concatenate([block * inverses for block in blocks], axis=1))
            if others:
                cols = others[0]["cols"]
        if k + GROUP < len(matrix):
            update = outer_sum(
                jnp.concatenate([blocks[0] for blocks in group]), jnp.concatenate(scaled)
            )
            for m in range(k + GROUP, len(matrix)):
                matrix[m] = matrix[m] - update[PANEL * m : PANEL * (m + 1)]
    return jnp.concatenate(rows, axis=0)


def deep_left(value):
    high, middle, low = parts_of(value)
    return jnp.concatenate([high, high, high, middle, middle, low], axis=1).astype(jnp.bfloat16)


def deep_right(value, axis):
    high, middle, low = parts_of(value)
    return jnp.concatenate([high, middle, low, high, middle, high], axis=axis).astype(jnp.bfloat16)


def basis_kernel(total_ref, snap_ref, out_ref, *, rows_all):
    cols = total_ref.shape[1]
    row_id, col_id = ids((cols, cols))
    identity = jnp.where(row_id == col_id, jnp.float32(ridge), 0.0)
    gram_matrix = unfolded(total_ref[...]) / rows_all + identity

    gram_deep = deep_right(gram_matrix, 0)
    basis = gram_matrix[:RANK]
    for step in range(ITERS):
        if step > 0:
            basis = jnp.dot(deep_left(basis), gram_deep, preferred_element_type=jnp.float32)
        full = jnp.concatenate([basis, jnp.zeros((cols - RANK, cols), jnp.float32)], axis=0)
        inner = lax.dot_general(
            deep_left(basis),
            deep_right(full, 1),
            (((1,), (1,)), ((), ())),
            preferred_element_type=jnp.float32,
        )
        basis = orthonormal_rows(inner, basis)
    blocks = out_ref.shape[0] // RANK
    basis_deep = deep_left(basis)
    for block in range(0, blocks, 2):
        pair = [snap_ref[pl.ds(block + n, cols, stride=SLOT), :] for n in range(2)]
        modes = jnp.dot(
            basis_deep,
            deep_right(jnp.concatenate(pair, axis=1), 0),
            preferred_element_type=jnp.float32,
        )
        for n in range(2):
            out_ref[pl.ds(block + n, RANK, stride=blocks), :] = modes[:, LANES * n : LANES * (n + 1)]


def project(gram_total, snapshots, rows_all):
    return pl.pallas_call(
        functools.partial(basis_kernel, rows_all=rows_all),
        out_shape=jax.ShapeDtypeStruct((RANK * 12, LANES), jnp.float32),
        in_specs=[pl.BlockSpec(memory_space=pltpu.VMEM)] * 2,
        out_specs=pl.BlockSpec(memory_space=pltpu.VMEM),
        compiler_params=pltpu.CompilerParams(vmem_limit_bytes=16 * 2**20),
        name="basis",
    )(gram_total, snapshots)


def exact_dot(values, one_hot):
    high, middle, low = (part.astype(jnp.bfloat16) for part in parts_of(values))
    dot = functools.partial(jnp.dot, preferred_element_type=jnp.float32)
    return (dot(low, one_hot) + dot(middle, one_hot)) + dot(high, one_hot)


def sorting(size, to_sorted):
    cell = lax.broadcasted_iota(jnp.int32, (size, size), 0 if to_sorted else 1)
    spot = lax.broadcasted_iota(jnp.int32, (size, size), 1 if to_sorted else 0)
    place = (cell & 3) * (size // 4) + (cell >> 2)
    return jnp.where(place == spot, 1.0, 0.0).astype(jnp.bfloat16)


def edges_kernel(velocity_ref, coef_ref, low_ref, high_ref, arrived):
    layers, rows_z = low_ref.shape[2], coef_ref.shape[1]
    copies = []
    for n, (edge_ref, start) in enumerate(((low_ref, 0), (high_ref, rows_z - layers))):
        rows = pl.ds(start, layers)
        copies += [
            pltpu.make_async_copy(velocity_ref.at[:, :, rows], edge_ref.at[:3], arrived.at[2 * n]),
            pltpu.make_async_copy(coef_ref.at[:, rows], edge_ref.at[3], arrived.at[2 * n + 1]),
        ]
    for copy in copies:
        copy.start()
    for copy in copies:
        copy.wait()


def edges(velocity, smag_coef):
    rows_y, _, size_x = smag_coef.shape
    edge = jax.ShapeDtypeStruct((4, rows_y, 4, size_x), jnp.float32)
    return pl.pallas_call(
        edges_kernel,
        out_shape=(edge, edge),
        in_specs=[pl.BlockSpec(memory_space=pltpu.HBM)] * 2,
        out_specs=[pl.BlockSpec(memory_space=pltpu.VMEM)] * 2,
        scratch_shapes=[pltpu.SemaphoreType.DMA((4,))],
        compiler_params=pltpu.CompilerParams(vmem_limit_bytes=2 * 2**20),
        name="edges",
    )(*(pltpu.with_memory_space_constraint(a, pltpu.HBM) for a in (velocity, smag_coef)))


def pack_kernel(velocity_ref, coef_ref, block_ref):
    rows_y, rows_z, size_x = coef_ref.shape
    rows = [velocity_ref[c].reshape(-1, size_x) for c in range(3)] + [coef_ref[...].reshape(-1, size_x)]
    done = exact_dot(jnp.concatenate(rows), sorting(size_x, True))
    for c in range(4):
        for y in range(rows_y):
            start = (c * rows_y + y) * rows_z
            for o in range(4):
                block_ref[c, y, o] = done[start : start + rows_z, LANES * o : LANES * (o + 1)]


def pack(velocity, smag_coef):
    rows_y, rows_z, _ = smag_coef.shape
    return pl.pallas_call(
        pack_kernel,
        out_shape=jax.ShapeDtypeStruct((4, rows_y, 4, rows_z, LANES), jnp.float32),
        in_specs=[pl.BlockSpec(memory_space=pltpu.VMEM)] * 2,
        out_specs=pl.BlockSpec(memory_space=pltpu.VMEM),
        compiler_params=pltpu.CompilerParams(vmem_limit_bytes=12 * 2**20),
        name="pack",
    )(velocity, smag_coef)


def sides_kernel(low_ref, high_ref, sides_ref, chip_ref, other_ref):
    odd = lax.axis_index("gy") % 2 == 1
    rows_y, layers, size_x = low_ref.shape[1:]
    rows = jnp.concatenate([high_ref[...], low_ref[...]], axis=2).reshape(-1, size_x)
    done = exact_dot(rows, sorting(size_x, True)).reshape(4, rows_y, 2 * layers, size_x)
    for c in range(4):
        for o in range(4):
            planes = [done[c, y, :, LANES * o : LANES * (o + 1)] for y in range(rows_y)]
            for y in range(rows_y):
                sides_ref[c, y, o] = planes[y]
            for away in range(rows_y - 1):
                upper, lower = planes[rows_y - 1 - away], planes[away]
                on_chip, off_chip = jnp.where(odd, lower, upper), jnp.where(odd, upper, lower)
                for ref, plane in ((chip_ref, on_chip), (other_ref, off_chip)):
                    if away == 0:
                        ref[c, 0, o] = plane
                    else:
                        for side, begin in enumerate((0, layers + 2)):
                            to = 4 * (away - 1) + 2 * side
                            ref[c, 1, o, to : to + 2] = plane[begin : begin + 2]


def sort_sides(low, high):
    _, rows_y, layers, _ = low.shape
    shape = lambda rows: jax.ShapeDtypeStruct((4, rows, 4, 2 * layers, LANES), jnp.float32)
    return pl.pallas_call(
        sides_kernel,
        out_shape=(shape(rows_y), shape(2), shape(2)),
        in_specs=[pl.BlockSpec(memory_space=pltpu.VMEM)] * 2,
        out_specs=[pl.BlockSpec(memory_space=pltpu.VMEM)] * 3,
        compiler_params=pltpu.CompilerParams(vmem_limit_bytes=12 * 2**20),
        cost_estimate=pl.CostEstimate(flops=2 * 10**10, bytes_accessed=10**6, transcendentals=0),
        name="sides",
    )(low, high)


def around_z(ref, index):
    return ref[(*index, slice(EDGE + 1, EDGE + 25))], ref[(*index, slice(EDGE - 1, EDGE + 23))]


def at(ref, *index):
    return ref[(*index, slice(EDGE, EDGE + 24))]


def put(ref, index, plane):
    ref[(*index, slice(EDGE, EDGE + 24))] = plane
    close(ref, index, plane)


def close(ref, index, plane):
    ref[(*index, slice(EDGE - 1, EDGE))] = plane[23:24]
    ref[(*index, slice(EDGE + 24, EDGE + 25))] = plane[:1]


def around_x(ref, index, o):
    ahead = at(ref, *index, o + 1) if o < 3 else pltpu.roll(at(ref, *index, 0), LANES - 1, 1)
    behind = at(ref, *index, o - 1) if o > 0 else pltpu.roll(at(ref, *index, 3), 1, 1)
    return ahead, behind


def half_viscosity(cells_ref, y, o, coefficient):
    jump = []
    for c in range(3):
        x_ahead, x_behind = around_x(cells_ref, (c, y), o)
        z_ahead, z_behind = around_z(cells_ref, (c, y, o))
        jump.append(
            (x_ahead - x_behind, at(cells_ref, c, y + 1, o) - at(cells_ref, c, y - 1, o), z_ahead - z_behind)
        )
    total = jump[0][0] ** 2 + jump[1][1] ** 2 + jump[2][2] ** 2
    total = total + total
    for c, d in ((0, 1), (0, 2), (1, 2)):
        total = total + (jump[c][d] + jump[d][c]) ** 2
    rate = coefficient * (0.5 * total * lax.rsqrt(jnp.maximum(total, 1e-37)))
    return (0.5 * nu_limit) * rate * recip(1.0 + rate)


def stepped(cells_ref, y, visc_ref, v, o):
    here = at(visc_ref, v, o)
    visc = [
        *around_x(visc_ref, (v,), o),
        at(visc_ref, v + 1, o),
        at(visc_ref, v - 1, o),
        *around_z(visc_ref, (v, o)),
    ]
    visc = [here + other for other in visc]
    result = []
    for c in range(3):
        centre = at(cells_ref, c, y, o)
        cells = [
            *around_x(cells_ref, (c, y), o),
            at(cells_ref, c, y + 1, o),
            at(cells_ref, c, y - 1, o),
            *around_z(cells_ref, (c, y, o)),
        ]
        change = visc[0] * (cells[0] - centre)
        for n in range(1, 6):
            change = change + visc[n] * (cells[n] - centre)
        result.append(centre + change)
    return result


def ids(shape):
    return lax.broadcasted_iota(jnp.int32, shape, 0), lax.broadcasted_iota(jnp.int32, shape, 1)


def folded(gram):
    half = gram.shape[0] // 2
    row, lane = ids((half, 2 * half))
    corner = pltpu.roll(gram[half:], half, 1)
    square = jnp.where(lane < row, corner, gram[:half])
    diagonal = jnp.sum(jnp.where(lane == row, corner, 0.0), axis=0, keepdims=True)
    return jnp.concatenate([square, jnp.broadcast_to(diagonal, (8, 2 * half))], axis=0)


def unfolded(parts):
    half = parts.shape[1] // 2
    row, lane = ids((half, 2 * half))
    square = parts[:half]
    upper = jnp.where(lane > row, square, 0.0)
    lower = pltpu.roll(jnp.where(lane < row, square, 0.0), half, 1)
    one_side = jnp.concatenate([upper, lower], axis=0)
    below = pltpu.roll(jnp.broadcast_to(parts[half : half + 1], square.shape), half, 1)
    diagonal = jnp.concatenate(
        [jnp.where(lane == row, square, 0.0), jnp.where(lane == row + half, below, 0.0)], axis=0
    )
    return one_side + one_side.T + diagonal


def steps_kernel(
    code_ref, block_ref, chip_ref, other_ref, sides_ref, side_chip_ref, side_other_ref,
    wide_ref, snap_ref, gram_ref,
    cells_ref, visc_ref, one_ref, two_ref, all_ref,
):
    _, rows_y, _, rows_z, _ = block_ref.shape
    cols = gram_ref.shape[1]
    place_y = lax.axis_index("gy")
    first, last, odd = place_y == 0, place_y == lax.axis_size("gy") - 1, place_y % 2 == 1

    def behind(chip, other):
        return jnp.where(first, 0.0, jnp.where(odd, chip, other))

    def ahead(chip, other):
        return jnp.where(last, 0.0, jnp.where(odd, other, chip))

    own_rows, layers = slice(EDGE, EDGE + rows_z), sides_ref.shape[3]
    side = slice(EDGE + rows_z, EDGE + rows_z + layers)
    for c in range(4):
        for y in range(rows_y):
            for o in range(4):
                own, below, above = (c, rows_y + y, o), (c, y, o), (c, 2 * rows_y + y, o)
                cells_ref[(*own, own_rows)] = block_ref[c, y, o]
                chip, other = chip_ref[c, y, o], other_ref[c, y, o]
                cells_ref[(*below, own_rows)] = behind(chip, other)
                cells_ref[(*above, own_rows)] = ahead(chip, other)
                cells_ref[(*own, side)] = sides_ref[c, y, o]
                for choose, place, away in ((behind, below, rows_y - 1 - y), (ahead, above, y)):
                    if away == 0:
                        halo = choose(side_chip_ref[c, 0, o], side_other_ref[c, 0, o])
                        cells_ref[(*place, side)] = halo
                    elif away <= rows_y - 2:
                        for n, begin in enumerate((rows_z, rows_z + layers - 2)):
                            part = (c, 1, o, slice(4 * (away - 1) + 2 * n, 4 * (away - 1) + 2 * n + 2))
                            halo = choose(side_chip_ref[part], side_other_ref[part])
                            cells_ref[(*place, slice(EDGE + begin, EDGE + begin + 2))] = halo
                if c < 3:
                    for place in (own, below, above):
                        close(cells_ref, place, at(cells_ref, *place))

    @pl.when(first)
    def _():
        for y in range(1, rows_y):
            cells_ref[3, y] = cells_ref[3, rows_y]

    @pl.when(last)
    def _():
        for y in range(rows_y - 1):
            cells_ref[3, 2 * rows_y + y] = cells_ref[3, 2 * rows_y - 1]

    def visc_one(y, carry):
        for o in range(4):
            put(visc_ref, (y, o), half_viscosity(cells_ref, y, o, at(cells_ref, 3, y, o)))
        return carry

    lax.fori_loop(1, 3 * rows_y - 1, visc_one, 0)

    def step_one(y, carry):
        outside = jnp.logical_or(
            jnp.logical_and(first, y < rows_y), jnp.logical_and(last, y >= 2 * rows_y)
        )
        for o in range(4):
            for c, cells in enumerate(stepped(cells_ref, y, visc_ref, y, o)):
                put(one_ref, (c, y, o), jnp.where(outside, 0.0, cells))
        return carry

    lax.fori_loop(2, 3 * rows_y - 2, step_one, 0)

    def visc_two(y, carry):
        for o in range(4):
            put(visc_ref, (y, o), half_viscosity(one_ref, y, o, at(cells_ref, 3, y, o)))
        return carry

    lax.fori_loop(rows_y - 1, 2 * rows_y + 1, visc_two, 0)

    for y in range(rows_y):
        for o in range(4):
            for c, cells in enumerate(stepped(one_ref, rows_y + y, visc_ref, rows_y + y, o)):
                two_ref[c, y, o] = cells[:rows_z]
                start = (c * rows_y + y) * rows_z
                wide_ref[start : start + rows_z, LANES * o : LANES * (o + 1)] = cells[:rows_z]
    states = ((block_ref, 0, 0), (one_ref, rows_y, EDGE), (two_ref, 0, 0))
    for state, (ref, shift, edge) in enumerate(states):
        for y in range(rows_y):
            for z in range(4):
                for o in range(4):
                    start = SLOT * (64 * state + 16 * y + 4 * z + o)
                    for c in range(3):
                        piece = ref[c, shift + y, o, pl.ds(edge + z, rows_z // 4, stride=4), :]
                        all_ref[start + 4 * c : start + 4 * c + 4, :] = piece

    def pick(column, carry):
        source = pl.multiple_of(code_ref[column] * SLOT, SLOT)
        target = pl.multiple_of(column * SLOT, SLOT)
        snap_ref[pl.ds(target, SLOT), :] = all_ref[pl.ds(source, SLOT), :]
        return carry

    lax.fori_loop(0, cols, pick, 0, unroll=16)
    even, odd = jnp.zeros((cols, cols), jnp.float32), jnp.zeros((cols, cols), jnp.float32)
    across = functools.partial(
        lax.dot_general,
        dimension_numbers=(((1,), (1,)), ((), ())),
        preferred_element_type=jnp.float32,
    )
    for block in range(0, 12, 2):
        part = jnp.concatenate(
            [snap_ref[pl.ds(block + i, cols, stride=SLOT), :] for i in range(2)], axis=1
        )
        high, middle, low = (p.astype(jnp.bfloat16) for p in parts_of(part))
        odd = odd + (across(high, low) + across(high, middle))
        even = even + (across(middle, middle) + across(high, high))
    gram_ref[...] = folded(even + (odd + odd.T))


def unsort_kernel(wide_ref, final_ref):
    final_ref[...] = exact_dot(wide_ref[...], sorting(wide_ref.shape[1], False)).reshape(final_ref.shape)


def unsort(wide, shape):
    return pl.pallas_call(
        unsort_kernel,
        out_shape=jax.ShapeDtypeStruct(shape, jnp.float32),
        in_specs=[pl.BlockSpec(memory_space=pltpu.VMEM)],
        out_specs=pl.BlockSpec(memory_space=pltpu.VMEM),
        compiler_params=pltpu.CompilerParams(vmem_limit_bytes=12 * 2**20),
        cost_estimate=pl.CostEstimate(flops=4 * 10**9, bytes_accessed=10**6, transcendentals=0),
        name="unsort",
    )(wide)


def both_steps(snap_code, block, *halo):
    _, rows_y, _, rows_z, _ = block.shape
    cols = snap_code.shape[0]
    f32 = lambda *shape: jax.ShapeDtypeStruct(shape, jnp.float32)
    scratch = lambda *shape: pltpu.VMEM(shape, jnp.float32)
    depth = EDGE + rows_z + 16
    return pl.pallas_call(
        steps_kernel,
        out_shape=(
            f32(3 * rows_y * rows_z, 4 * LANES),
            f32(SLOT * cols, LANES),
            f32(cols // 2 + 8, cols),
        ),
        in_specs=[pl.BlockSpec(memory_space=pltpu.SMEM)]
        + [pl.BlockSpec(memory_space=pltpu.VMEM)] * (1 + len(halo)),
        out_specs=[pl.BlockSpec(memory_space=pltpu.VMEM)] * 3,
        scratch_shapes=[
            scratch(4, 3 * rows_y, 4, depth, LANES),
            scratch(3 * rows_y, 4, depth, LANES),
            scratch(3, 3 * rows_y, 4, depth, LANES),
            scratch(3, rows_y, 4, rows_z, LANES),
            scratch(SLOT * 192, LANES),
        ],
        compiler_params=pltpu.CompilerParams(vmem_limit_bytes=32 * 2**20),
        name="steps",
    )(snap_code, block, *halo)


def device_sum(part):
    axes = ("gy", "gz")
    size_z, size_x = 8, lax.axis_size("gz")
    rounds = (
        [
            lambda x, y, z, core: (x, y, z, core ^ 1),
            lambda x, y, z, core: (x, y, z ^ 1, core),
            lambda x, y, z, core: (x, y, z ^ 1, core ^ 1),
        ],
        [lambda x, y, z, core, bits=bits: (x ^ bits, y, z, core) for bits in (1, 2, 3)],
        [lambda x, y, z, core, bits=bits: (x, y ^ bits, z, core) for bits in (1, 2, 3)],
        [lambda x, y, z, core, far=far: (x, y, (z + far) % size_z, core) for far in (2, -2, 4)],
    )

    def partner(move, device):
        row, x = divmod(device, size_x)
        x, y, z, core = move(x, row // (2 * size_z), row // 2 % size_z, row % 2)
        return ((y * size_z + z) * 2 + core) * size_x + x

    count = lax.axis_size("gy") * size_x
    for moves in rounds:
        others = [
            lax.ppermute(part, axes, [(device, partner(move, device)) for device in range(count)])
            for move in moves
        ]
        part = part + sum(others[1:], others[0])
    return part


def local(velocity, smag_coef, snap_code):
    count_y, count_z = lax.axis_size("gy"), lax.axis_size("gz")

    def along_z(part, step):
        return lax.ppermute(part, "gz", [(i, (i + step) % count_z) for i in range(count_z)])

    def on_chip(part):
        return lax.ppermute(part, "gy", [(i, i ^ 1) for i in range(count_y)])

    def off_chip(part):
        partners = [min(max(((i + 1) ^ 1) - 1, 0), count_y - 1) for i in range(count_y)]
        return lax.ppermute(part, "gy", list(enumerate(partners)))

    low, high = edges(velocity, smag_coef)
    velocity, smag_coef, low, high = lax.optimization_barrier((velocity, smag_coef, low, high))
    sides, side_chip, side_other = sort_sides(along_z(high, 1), along_z(low, -1))
    block = pack(velocity, smag_coef)
    wide, snapshots, gram = both_steps(
        snap_code, block, on_chip(block), off_chip(block), sides, on_chip(side_chip), off_chip(side_other)
    )
    rows_y, rows_z = velocity.shape[1], velocity.shape[2]
    rows_all = 12 * LANES * count_y * count_z
    pod_modes = project(device_sum(gram), snapshots, rows_all)
    return (unsort(wide, velocity.shape), pod_modes.reshape(RANK, 3, rows_y // 4, rows_z // 4, LANES))


def solution(mesh):
    placed = (P(None, "gy", "gz", None), P("gy", "gz", None), P())
    return jax.shard_map(
        local,
        mesh=mesh,
        in_specs=placed,
        out_specs=(P(None, "gy", "gz", None), P(None, None, "gy", "gz", None)),
        check_vma=False,
    )
```

```python
import functools

import jax
import jax.numpy as jnp
from jax import lax
from jax.experimental import pallas as pl
from jax.experimental.pallas import tpu as pltpu
from jax.sharding import PartitionSpec as P

RANK = 112
ITERS = 3
PANEL = 8
GROUP = 5
LANES = 128
SLOT = 16
EDGE = 8


nu_limit = 0.125
ridge = 1.0
highest = lax.Precision.HIGHEST


def recip(value):
    return pltpu.reciprocal(value, approx=True)


def spread(block, lane):
    return jnp.broadcast_to(block[:, lane : lane + 1], block.shape)


def repeat(block, row):
    return jnp.broadcast_to(block[row : row + 1, :], block.shape)


def parts_of(value):
    high = value.astype(jnp.bfloat16).astype(jnp.float32)
    rest = value - high
    middle = rest.astype(jnp.bfloat16).astype(jnp.float32)
    return high, middle, rest - middle


def outer_sum(left, right):
    lh, lm, ll = parts_of(left)
    rh, rm, rl = parts_of(right)
    stacked_left = jnp.concatenate([lh, lh, lh, lm, lm, ll]).astype(jnp.bfloat16)
    stacked_right = jnp.concatenate([rh, rm, rl, rh, rm, rh]).astype(jnp.bfloat16)
    return lax.dot_general(
        stacked_left, stacked_right, (((0,), (0,)), ((), ())), preferred_element_type=jnp.float32
    )


def eliminate(cols, blocks, others):
    row_id = lax.broadcasted_iota(jnp.int32, blocks[0].shape, 0)
    pivots, inverses = jnp.ones_like(blocks[0]), jnp.ones_like(blocks[0])
    for j in range(0, PANEL, 2):
        first, cross = repeat(cols[j], j), repeat(cols[j], j + 1)
        corner = repeat(cols[j + 1], j + 1)
        first_inverse = recip(first)
        second_inverse = first * recip(first * corner - cross * cross)
        second = corner - cross * (cross * first_inverse)
        for i, pivot, inverse in ((j, first, first_inverse), (j + 1, second, second_inverse)):
            pivots = jnp.where(row_id == i, pivot, pivots)
            inverses = jnp.where(row_id == i, inverse, inverses)
        one = cols[j] * first_inverse
        cols[j + 1] = cols[j + 1] - one * cross
        two = cols[j + 1] * second_inverse
        for other in others:
            below = other["below"]
            other_one = below[j] * first_inverse
            below[j + 1] = below[j + 1] - other_one * cross
            other_two = below[j + 1] * second_inverse
            for m in range(j + 2, PANEL):
                a, b = repeat(cols[j], m), repeat(cols[j + 1], m)
                below[m] = (below[m] - other_one * a) - other_two * b
            for m in range(len(other["cols"])):
                a, b = repeat(below[j], m), repeat(below[j + 1], m)
                other["cols"][m] = (other["cols"][m] - other_one * a) - other_two * b
            for n, block in enumerate(blocks):
                other["blocks"][n] = other["blocks"][n] - other_one * repeat(block, j)
            other["two"] = other_two
        for m in range(j + 2, PANEL):
            a, b = repeat(cols[j], m), repeat(cols[j + 1], m)
            cols[m] = (cols[m] - one * a) - two * b
        one = jnp.where(row_id > j, one, 0.0)
        two = jnp.where(row_id > j + 1, two, 0.0)
        for n in range(len(blocks)):
            blocks[n] = blocks[n] - one * repeat(blocks[n], j)
            row = repeat(blocks[n], j + 1)
            blocks[n] = blocks[n] - two * row
            for other in others:
                other["blocks"][n] = other["blocks"][n] - other["two"] * row
    return pivots, inverses


def orthonormal_rows(inner, wide):
    width = inner.shape[1]
    both = jnp.concatenate([inner, wide], axis=1)
    matrix = [both[PANEL * k : PANEL * (k + 1)] for k in range(RANK // PANEL)]
    rows = []
    for k in range(0, len(matrix), GROUP):
        group = [[part[:, :width], part[:, width:]] for part in matrix[k : k + GROUP]]
        cols = [spread(group[0][0], PANEL * k + j) for j in range(PANEL)]
        scaled = []
        for n, blocks in enumerate(group):
            at = PANEL * (k + n)
            others = []
            for later, other in enumerate(group[n + 1 :]):
                below = [spread(other[0], at + j) for j in range(PANEL)]
                ahead = [spread(other[0], at + PANEL + j) for j in range(PANEL)] if later == 0 else []
                others.append({"below": below, "cols": ahead, "blocks": other})
            pivots, inverses = eliminate(cols, blocks, others)
            rows.append(blocks[1] * lax.rsqrt(pivots))
            scaled.append(jnp.concatenate([block * inverses for block in blocks], axis=1))
            if others:
                cols = others[0]["cols"]
        if k + GROUP < len(matrix):
            update = outer_sum(
                jnp.concatenate([blocks[0] for blocks in group]), jnp.concatenate(scaled)
            )
            for m in range(k + GROUP, len(matrix)):
                matrix[m] = matrix[m] - update[PANEL * m : PANEL * (m + 1)]
    return jnp.concatenate(rows, axis=0)


def deep_left(value):
    high, middle, low = parts_of(value)
    return jnp.concatenate([high, high, high, middle, middle, low], axis=1).astype(jnp.bfloat16)


def deep_right(value, axis):
    high, middle, low = parts_of(value)
    return jnp.concatenate([high, middle, low, high, middle, high], axis=axis).astype(jnp.bfloat16)


def basis_kernel(total_ref, snap_ref, out_ref, *, rows_all):
    cols = total_ref.shape[1]
    row_id, col_id = ids((cols, cols))
    identity = jnp.where(row_id == col_id, jnp.float32(ridge), 0.0)
    gram_matrix = unfolded(total_ref[...]) / rows_all + identity

    gram_deep = deep_right(gram_matrix, 0)
    basis = gram_matrix[:RANK]
    for step in range(ITERS):
        if step > 0:
            basis = jnp.dot(deep_left(basis), gram_deep, preferred_element_type=jnp.float32)
        full = jnp.concatenate([basis, jnp.zeros((cols - RANK, cols), jnp.float32)], axis=0)
        inner = lax.dot_general(
            deep_left(basis),
            deep_right(full, 1),
            (((1,), (1,)), ((), ())),
            preferred_element_type=jnp.float32,
        )
        basis = orthonormal_rows(inner, basis)
    blocks = out_ref.shape[0] // RANK
    basis_deep = deep_left(basis)
    for block in range(0, blocks, 2):
        pair = [snap_ref[pl.ds(block + n, cols, stride=SLOT), :] for n in range(2)]
        modes = jnp.dot(
            basis_deep,
            deep_right(jnp.concatenate(pair, axis=1), 0),
            preferred_element_type=jnp.float32,
        )
        for n in range(2):
            out_ref[pl.ds(block + n, RANK, stride=blocks), :] = modes[:, LANES * n : LANES * (n + 1)]


def project(gram_total, snapshots, rows_all):
    return pl.pallas_call(
        functools.partial(basis_kernel, rows_all=rows_all),
        out_shape=jax.ShapeDtypeStruct((RANK * 12, LANES), jnp.float32),
        in_specs=[pl.BlockSpec(memory_space=pltpu.VMEM)] * 2,
        out_specs=pl.BlockSpec(memory_space=pltpu.VMEM),
        compiler_params=pltpu.CompilerParams(vmem_limit_bytes=16 * 2**20),
        name="basis",
    )(gram_total, snapshots)


def exact_dot(values, one_hot):
    high, middle, low = (part.astype(jnp.bfloat16) for part in parts_of(values))
    dot = functools.partial(jnp.dot, preferred_element_type=jnp.float32)
    return (dot(low, one_hot) + dot(middle, one_hot)) + dot(high, one_hot)


def sorting(size, to_sorted):
    cell = lax.broadcasted_iota(jnp.int32, (size, size), 0 if to_sorted else 1)
    spot = lax.broadcasted_iota(jnp.int32, (size, size), 1 if to_sorted else 0)
    place = (cell & 3) * (size // 4) + (cell >> 2)
    return jnp.where(place == spot, 1.0, 0.0).astype(jnp.bfloat16)


def edges_kernel(velocity_ref, coef_ref, low_ref, high_ref, far_low_ref, far_high_ref, arrived):
    layers, rows_z = low_ref.shape[2], coef_ref.shape[1]
    copies = []
    for n, (edge_ref, start) in enumerate(((low_ref, 0), (high_ref, rows_z - layers))):
        rows = pl.ds(start, layers)
        copies += [
            pltpu.make_async_copy(velocity_ref.at[:, :, rows], edge_ref.at[:3], arrived.at[2 * n]),
            pltpu.make_async_copy(coef_ref.at[:, rows], edge_ref.at[3], arrived.at[2 * n + 1]),
        ]
    for copy in copies:
        copy.start()
    for copy in copies:
        copy.wait()
    odd = lax.axis_index("gy") % 2 == 1
    rows_y = coef_ref.shape[0]
    for c in range(4):
        for away in range(rows_y - 1):
            low = jnp.where(odd, low_ref[c, rows_y - 1 - away], low_ref[c, away])
            high = jnp.where(odd, high_ref[c, rows_y - 1 - away], high_ref[c, away])
            if away == 0:
                far_low_ref[c, :layers], far_high_ref[c, :layers] = low, high
            else:
                rows = slice(layers + 2 * (away - 1), layers + 2 * away)
                far_low_ref[c, rows], far_high_ref[c, rows] = low[:2], high[2:]


def edges(velocity, smag_coef):
    rows_y, _, size_x = smag_coef.shape
    edge = jax.ShapeDtypeStruct((4, rows_y, 4, size_x), jnp.float32)
    far = jax.ShapeDtypeStruct((4, 8, size_x), jnp.float32)
    return pl.pallas_call(
        edges_kernel,
        out_shape=(edge, edge, far, far),
        in_specs=[pl.BlockSpec(memory_space=pltpu.HBM)] * 2,
        out_specs=[pl.BlockSpec(memory_space=pltpu.VMEM)] * 4,
        scratch_shapes=[pltpu.SemaphoreType.DMA((4,))],
        compiler_params=pltpu.CompilerParams(vmem_limit_bytes=2 * 2**20),
        name="edges",
    )(*(pltpu.with_memory_space_constraint(a, pltpu.HBM) for a in (velocity, smag_coef)))


def pack_kernel(velocity_ref, coef_ref, block_ref):
    rows_y, rows_z, size_x = coef_ref.shape
    rows = [velocity_ref[c].reshape(-1, size_x) for c in range(3)] + [coef_ref[...].reshape(-1, size_x)]
    done = exact_dot(jnp.concatenate(rows), sorting(size_x, True))
    for c in range(4):
        for y in range(rows_y):
            start = (c * rows_y + y) * rows_z
            for o in range(4):
                block_ref[c, y, o] = done[start : start + rows_z, LANES * o : LANES * (o + 1)]


def pack(velocity, smag_coef):
    rows_y, rows_z, _ = smag_coef.shape
    return pl.pallas_call(
        pack_kernel,
        out_shape=jax.ShapeDtypeStruct((4, rows_y, 4, rows_z, LANES), jnp.float32),
        in_specs=[pl.BlockSpec(memory_space=pltpu.VMEM)] * 2,
        out_specs=pl.BlockSpec(memory_space=pltpu.VMEM),
        compiler_params=pltpu.CompilerParams(vmem_limit_bytes=12 * 2**20),
        name="pack",
    )(velocity, smag_coef)


def sides_kernel(low_ref, high_ref, sides_ref, chip_ref):
    odd = lax.axis_index("gy") % 2 == 1
    rows_y, layers, size_x = low_ref.shape[1:]
    rows = jnp.concatenate([high_ref[...], low_ref[...]], axis=2).reshape(-1, size_x)
    done = exact_dot(rows, sorting(size_x, True)).reshape(4, rows_y, 2 * layers, size_x)
    for c in range(4):
        for o in range(4):
            planes = [done[c, y, :, LANES * o : LANES * (o + 1)] for y in range(rows_y)]
            for y in range(rows_y):
                sides_ref[c, y, o] = planes[y]
            for away in range(rows_y - 1):
                plane = jnp.where(odd, planes[away], planes[rows_y - 1 - away])
                if away == 0:
                    chip_ref[c, 0, o] = plane
                else:
                    for side, begin in enumerate((0, layers + 2)):
                        to = 4 * (away - 1) + 2 * side
                        chip_ref[c, 1, o, to : to + 2] = plane[begin : begin + 2]


def sort_sides(low, high):
    _, rows_y, layers, _ = low.shape
    shape = lambda rows: jax.ShapeDtypeStruct((4, rows, 4, 2 * layers, LANES), jnp.float32)
    return pl.pallas_call(
        sides_kernel,
        out_shape=(shape(rows_y), shape(2)),
        in_specs=[pl.BlockSpec(memory_space=pltpu.VMEM)] * 2,
        out_specs=[pl.BlockSpec(memory_space=pltpu.VMEM)] * 2,
        compiler_params=pltpu.CompilerParams(vmem_limit_bytes=12 * 2**20),
        cost_estimate=pl.CostEstimate(flops=2 * 10**10, bytes_accessed=10**6, transcendentals=0),
        name="sides",
    )(low, high)


def corners_kernel(low_ref, high_ref, other_ref):
    size_x = low_ref.shape[-1]
    low, high = low_ref[...], high_ref[...]
    near = jnp.concatenate([high[:, :4], low[:, :4]], axis=1)
    away = jnp.concatenate([high[:, 4:6], low[:, 4:6], high[:, 6:8], low[:, 6:8]], axis=1)
    rows = jnp.concatenate([near.reshape(-1, size_x), away.reshape(-1, size_x)])
    done = exact_dot(rows, sorting(size_x, True)).reshape(2, 4, 8, size_x)
    for c in range(4):
        for tile in range(2):
            for o in range(4):
                other_ref[c, tile, o] = done[tile, c, :, LANES * o : LANES * (o + 1)]


def sort_corners(low, high):
    return pl.pallas_call(
        corners_kernel,
        out_shape=jax.ShapeDtypeStruct((4, 2, 4, 8, LANES), jnp.float32),
        in_specs=[pl.BlockSpec(memory_space=pltpu.VMEM)] * 2,
        out_specs=pl.BlockSpec(memory_space=pltpu.VMEM),
        compiler_params=pltpu.CompilerParams(vmem_limit_bytes=12 * 2**20),
        cost_estimate=pl.CostEstimate(flops=15 * 10**9, bytes_accessed=10**6, transcendentals=0),
        name="corners",
    )(low, high)


def around_z(ref, index):
    return ref[(*index, slice(EDGE + 1, EDGE + 25))], ref[(*index, slice(EDGE - 1, EDGE + 23))]


def at(ref, *index):
    return ref[(*index, slice(EDGE, EDGE + 24))]


def put(ref, index, plane):
    ref[(*index, slice(EDGE, EDGE + 24))] = plane
    close(ref, index, plane)


def close(ref, index, plane):
    ref[(*index, slice(EDGE - 1, EDGE))] = plane[23:24]
    ref[(*index, slice(EDGE + 24, EDGE + 25))] = plane[:1]


def around_x(ref, index, o):
    ahead = at(ref, *index, o + 1) if o < 3 else pltpu.roll(at(ref, *index, 0), LANES - 1, 1)
    behind = at(ref, *index, o - 1) if o > 0 else pltpu.roll(at(ref, *index, 3), 1, 1)
    return ahead, behind


def half_viscosity(cells_ref, y, o, coefficient):
    jump = []
    for c in range(3):
        x_ahead, x_behind = around_x(cells_ref, (c, y), o)
        z_ahead, z_behind = around_z(cells_ref, (c, y, o))
        jump.append(
            (x_ahead - x_behind, at(cells_ref, c, y + 1, o) - at(cells_ref, c, y - 1, o), z_ahead - z_behind)
        )
    total = jump[0][0] ** 2 + jump[1][1] ** 2 + jump[2][2] ** 2
    total = total + total
    for c, d in ((0, 1), (0, 2), (1, 2)):
        total = total + (jump[c][d] + jump[d][c]) ** 2
    rate = coefficient * (0.5 * total * lax.rsqrt(jnp.maximum(total, 1e-37)))
    return (0.5 * nu_limit) * rate * recip(1.0 + rate)


def stepped(cells_ref, y, visc_ref, v, o):
    here = at(visc_ref, v, o)
    visc = [
        *around_x(visc_ref, (v,), o),
        at(visc_ref, v + 1, o),
        at(visc_ref, v - 1, o),
        *around_z(visc_ref, (v, o)),
    ]
    visc = [here + other for other in visc]
    result = []
    for c in range(3):
        centre = at(cells_ref, c, y, o)
        cells = [
            *around_x(cells_ref, (c, y), o),
            at(cells_ref, c, y + 1, o),
            at(cells_ref, c, y - 1, o),
            *around_z(cells_ref, (c, y, o)),
        ]
        change = visc[0] * (cells[0] - centre)
        for n in range(1, 6):
            change = change + visc[n] * (cells[n] - centre)
        result.append(centre + change)
    return result


def ids(shape):
    return lax.broadcasted_iota(jnp.int32, shape, 0), lax.broadcasted_iota(jnp.int32, shape, 1)


def folded(gram):
    half = gram.shape[0] // 2
    row, lane = ids((half, 2 * half))
    corner = pltpu.roll(gram[half:], half, 1)
    square = jnp.where(lane < row, corner, gram[:half])
    diagonal = jnp.sum(jnp.where(lane == row, corner, 0.0), axis=0, keepdims=True)
    return jnp.concatenate([square, jnp.broadcast_to(diagonal, (8, 2 * half))], axis=0)


def unfolded(parts):
    half = parts.shape[1] // 2
    row, lane = ids((half, 2 * half))
    square = parts[:half]
    upper = jnp.where(lane > row, square, 0.0)
    lower = pltpu.roll(jnp.where(lane < row, square, 0.0), half, 1)
    one_side = jnp.concatenate([upper, lower], axis=0)
    below = pltpu.roll(jnp.broadcast_to(parts[half : half + 1], square.shape), half, 1)
    diagonal = jnp.concatenate(
        [jnp.where(lane == row, square, 0.0), jnp.where(lane == row + half, below, 0.0)], axis=0
    )
    return one_side + one_side.T + diagonal


def steps_kernel(
    code_ref, block_ref, chip_ref, other_ref, sides_ref, side_chip_ref, side_other_ref,
    wide_ref, snap_ref, gram_ref,
    cells_ref, visc_ref, one_ref, two_ref, all_ref,
):
    _, rows_y, _, rows_z, _ = block_ref.shape
    cols = gram_ref.shape[1]
    place_y = lax.axis_index("gy")
    first, last, odd = place_y == 0, place_y == lax.axis_size("gy") - 1, place_y % 2 == 1

    def behind(chip, other):
        return jnp.where(first, 0.0, jnp.where(odd, chip, other))

    def ahead(chip, other):
        return jnp.where(last, 0.0, jnp.where(odd, other, chip))

    own_rows, layers = slice(EDGE, EDGE + rows_z), sides_ref.shape[3]
    side = slice(EDGE + rows_z, EDGE + rows_z + layers)
    for c in range(4):
        for y in range(rows_y):
            for o in range(4):
                own, below, above = (c, rows_y + y, o), (c, y, o), (c, 2 * rows_y + y, o)
                cells_ref[(*own, own_rows)] = block_ref[c, y, o]
                chip, other = chip_ref[c, y, o], other_ref[c, y, o]
                cells_ref[(*below, own_rows)] = behind(chip, other)
                cells_ref[(*above, own_rows)] = ahead(chip, other)
                cells_ref[(*own, side)] = sides_ref[c, y, o]
                for choose, place, away in ((behind, below, rows_y - 1 - y), (ahead, above, y)):
                    if away == 0:
                        halo = choose(side_chip_ref[c, 0, o], side_other_ref[c, 0, o])
                        cells_ref[(*place, side)] = halo
                    elif away <= rows_y - 2:
                        for n, begin in enumerate((rows_z, rows_z + layers - 2)):
                            part = (c, 1, o, slice(4 * (away - 1) + 2 * n, 4 * (away - 1) + 2 * n + 2))
                            halo = choose(side_chip_ref[part], side_other_ref[part])
                            cells_ref[(*place, slice(EDGE + begin, EDGE + begin + 2))] = halo
                if c < 3:
                    for place in (own, below, above):
                        close(cells_ref, place, at(cells_ref, *place))

    @pl.when(first)
    def _():
        for y in range(1, rows_y):
            cells_ref[3, y] = cells_ref[3, rows_y]

    @pl.when(last)
    def _():
        for y in range(rows_y - 1):
            cells_ref[3, 2 * rows_y + y] = cells_ref[3, 2 * rows_y - 1]

    def visc_one(y, carry):
        for o in range(4):
            put(visc_ref, (y, o), half_viscosity(cells_ref, y, o, at(cells_ref, 3, y, o)))
        return carry

    lax.fori_loop(1, 3 * rows_y - 1, visc_one, 0)

    def step_one(y, carry):
        outside = jnp.logical_or(
            jnp.logical_and(first, y < rows_y), jnp.logical_and(last, y >= 2 * rows_y)
        )
        for o in range(4):
            for c, cells in enumerate(stepped(cells_ref, y, visc_ref, y, o)):
                put(one_ref, (c, y, o), jnp.where(outside, 0.0, cells))
        return carry

    lax.fori_loop(2, 3 * rows_y - 2, step_one, 0)

    def visc_two(y, carry):
        for o in range(4):
            put(visc_ref, (y, o), half_viscosity(one_ref, y, o, at(cells_ref, 3, y, o)))
        return carry

    lax.fori_loop(rows_y - 1, 2 * rows_y + 1, visc_two, 0)

    for y in range(rows_y):
        for o in range(4):
            for c, cells in enumerate(stepped(one_ref, rows_y + y, visc_ref, rows_y + y, o)):
                two_ref[c, y, o] = cells[:rows_z]
                start = (c * rows_y + y) * rows_z
                wide_ref[start : start + rows_z, LANES * o : LANES * (o + 1)] = cells[:rows_z]
    states = ((block_ref, 0, 0), (one_ref, rows_y, EDGE), (two_ref, 0, 0))
    for state, (ref, shift, edge) in enumerate(states):
        for y in range(rows_y):
            for z in range(4):
                for o in range(4):
                    start = SLOT * (64 * state + 16 * y + 4 * z + o)
                    for c in range(3):
                        piece = ref[c, shift + y, o, pl.ds(edge + z, rows_z // 4, stride=4), :]
                        all_ref[start + 4 * c : start + 4 * c + 4, :] = piece

    def pick(column, carry):
        source = pl.multiple_of(code_ref[column] * SLOT, SLOT)
        target = pl.multiple_of(column * SLOT, SLOT)
        snap_ref[pl.ds(target, SLOT), :] = all_ref[pl.ds(source, SLOT), :]
        return carry

    lax.fori_loop(0, cols, pick, 0, unroll=16)
    even, odd = jnp.zeros((cols, cols), jnp.float32), jnp.zeros((cols, cols), jnp.float32)
    across = functools.partial(
        lax.dot_general,
        dimension_numbers=(((1,), (1,)), ((), ())),
        preferred_element_type=jnp.float32,
    )
    for block in range(0, 12, 2):
        part = jnp.concatenate(
            [snap_ref[pl.ds(block + i, cols, stride=SLOT), :] for i in range(2)], axis=1
        )
        high, middle, low = (p.astype(jnp.bfloat16) for p in parts_of(part))
        odd = odd + (across(high, low) + across(high, middle))
        even = even + (across(middle, middle) + across(high, high))
    gram_ref[...] = folded(even + (odd + odd.T))


def unsort_kernel(wide_ref, final_ref):
    final_ref[...] = exact_dot(wide_ref[...], sorting(wide_ref.shape[1], False)).reshape(final_ref.shape)


def unsort(wide, shape):
    return pl.pallas_call(
        unsort_kernel,
        out_shape=jax.ShapeDtypeStruct(shape, jnp.float32),
        in_specs=[pl.BlockSpec(memory_space=pltpu.VMEM)],
        out_specs=pl.BlockSpec(memory_space=pltpu.VMEM),
        compiler_params=pltpu.CompilerParams(vmem_limit_bytes=12 * 2**20),
        cost_estimate=pl.CostEstimate(flops=4 * 10**9, bytes_accessed=10**6, transcendentals=0),
        name="unsort",
    )(wide)


def both_steps(snap_code, block, *halo):
    _, rows_y, _, rows_z, _ = block.shape
    cols = snap_code.shape[0]
    f32 = lambda *shape: jax.ShapeDtypeStruct(shape, jnp.float32)
    scratch = lambda *shape: pltpu.VMEM(shape, jnp.float32)
    depth = EDGE + rows_z + 16
    return pl.pallas_call(
        steps_kernel,
        out_shape=(
            f32(3 * rows_y * rows_z, 4 * LANES),
            f32(SLOT * cols, LANES),
            f32(cols // 2 + 8, cols),
        ),
        in_specs=[pl.BlockSpec(memory_space=pltpu.SMEM)]
        + [pl.BlockSpec(memory_space=pltpu.VMEM)] * (1 + len(halo)),
        out_specs=[pl.BlockSpec(memory_space=pltpu.VMEM)] * 3,
        scratch_shapes=[
            scratch(4, 3 * rows_y, 4, depth, LANES),
            scratch(3 * rows_y, 4, depth, LANES),
            scratch(3, 3 * rows_y, 4, depth, LANES),
            scratch(3, rows_y, 4, rows_z, LANES),
            scratch(SLOT * 192, LANES),
        ],
        compiler_params=pltpu.CompilerParams(vmem_limit_bytes=32 * 2**20),
        name="steps",
    )(snap_code, block, *halo)


def device_sum(part):
    axes = ("gy", "gz")
    size_z, size_x = 8, lax.axis_size("gz")
    rounds = (
        [lambda x, y, z, core: (x, y, z, core ^ 1)],
        [lambda x, y, z, core, bits=bits: (x ^ bits, y, z, core) for bits in (1, 2, 3)],
        [lambda x, y, z, core, bits=bits: (x, y ^ bits, z, core) for bits in (1, 2, 3)],
        [lambda x, y, z, core, bits=bits: (x, y, z ^ bits, core) for bits in (1, 2, 3)],
        [lambda x, y, z, core: (x, y, size_z - 1 - z, core)],
    )

    def partner(move, device):
        row, x = divmod(device, size_x)
        x, y, z, core = move(x, row // (2 * size_z), row // 2 % size_z, row % 2)
        return ((y * size_z + z) * 2 + core) * size_x + x

    count = lax.axis_size("gy") * size_x
    for moves in rounds:
        others = [
            lax.ppermute(part, axes, [(device, partner(move, device)) for device in range(count)])
            for move in moves
        ]
        part = part + sum(others[1:], others[0])
    return part


def local(velocity, smag_coef, snap_code):
    count_y, count_z = lax.axis_size("gy"), lax.axis_size("gz")

    def along_z(part, step):
        return lax.ppermute(part, "gz", [(i, (i + step) % count_z) for i in range(count_z)])

    def on_chip(part):
        return lax.ppermute(part, "gy", [(i, i ^ 1) for i in range(count_y)])

    def off_chip(part, step=0):
        pairs = [
            (y * count_z + z, min(max(((y + 1) ^ 1) - 1, 0), count_y - 1) * count_z + (z + step) % count_z)
            for y in range(count_y)
            for z in range(count_z)
        ]
        return lax.ppermute(part, ("gy", "gz"), pairs)

    low, high, far_low, far_high = edges(velocity, smag_coef)
    velocity, smag_coef, low, high, far_low, far_high = lax.optimization_barrier(
        (velocity, smag_coef, low, high, far_low, far_high)
    )
    sides, side_chip = sort_sides(along_z(high, 1), along_z(low, -1))
    side_other = sort_corners(off_chip(far_high, 1), off_chip(far_low, -1))
    block = pack(velocity, smag_coef)
    wide, snapshots, gram = both_steps(
        snap_code, block, on_chip(block), off_chip(block), sides, on_chip(side_chip), side_other
    )
    rows_y, rows_z = velocity.shape[1], velocity.shape[2]
    rows_all = 12 * LANES * count_y * count_z
    pod_modes = project(device_sum(gram), snapshots, rows_all)
    return (unsort(wide, velocity.shape), pod_modes.reshape(RANK, 3, rows_y // 4, rows_z // 4, LANES))


def solution(mesh):
    placed = (P(None, "gy", "gz", None), P("gy", "gz", None), P())
    return jax.shard_map(
        local,
        mesh=mesh,
        in_specs=placed,
        out_specs=(P(None, "gy", "gz", None), P(None, None, "gy", "gz", None)),
        check_vma=False,
    )
```

```python
import functools

import jax
import jax.numpy as jnp
from jax import lax
from jax.experimental import pallas as pl
from jax.experimental.pallas import tpu as pltpu
from jax.sharding import PartitionSpec as P

RANK = 112
ITERS = 3
PANEL = 8
GROUP = 5
LANES = 128
SLOT = 16
EDGE = 8


nu_limit = 0.125
ridge = 1.0
highest = lax.Precision.HIGHEST


def recip(value):
    return pltpu.reciprocal(value, approx=True)


def spread(block, lane):
    return jnp.broadcast_to(block[:, lane : lane + 1], block.shape)


def repeat(block, row):
    return jnp.broadcast_to(block[row : row + 1, :], block.shape)


def parts_of(value):
    high = value.astype(jnp.bfloat16).astype(jnp.float32)
    rest = value - high
    middle = rest.astype(jnp.bfloat16).astype(jnp.float32)
    return high, middle, rest - middle


def outer_sum(left, right):
    lh, lm, ll = parts_of(left)
    rh, rm, rl = parts_of(right)
    stacked_left = jnp.concatenate([lh, lh, lh, lm, lm, ll]).astype(jnp.bfloat16)
    stacked_right = jnp.concatenate([rh, rm, rl, rh, rm, rh]).astype(jnp.bfloat16)
    return lax.dot_general(
        stacked_left, stacked_right, (((0,), (0,)), ((), ())), preferred_element_type=jnp.float32
    )


def eliminate(cols, blocks, others):
    row_id = lax.broadcasted_iota(jnp.int32, blocks[0].shape, 0)
    pivots, inverses = jnp.ones_like(blocks[0]), jnp.ones_like(blocks[0])
    for j in range(0, PANEL, 2):
        first, cross = repeat(cols[j], j), repeat(cols[j], j + 1)
        corner = repeat(cols[j + 1], j + 1)
        first_inverse = recip(first)
        second_inverse = first * recip(first * corner - cross * cross)
        second = corner - cross * (cross * first_inverse)
        for i, pivot, inverse in ((j, first, first_inverse), (j + 1, second, second_inverse)):
            pivots = jnp.where(row_id == i, pivot, pivots)
            inverses = jnp.where(row_id == i, inverse, inverses)
        one = cols[j] * first_inverse
        cols[j + 1] = cols[j + 1] - one * cross
        two = cols[j + 1] * second_inverse
        for other in others:
            below = other["below"]
            other_one = below[j] * first_inverse
            below[j + 1] = below[j + 1] - other_one * cross
            other_two = below[j + 1] * second_inverse
            for m in range(j + 2, PANEL):
                a, b = repeat(cols[j], m), repeat(cols[j + 1], m)
                below[m] = (below[m] - other_one * a) - other_two * b
            for m in range(len(other["cols"])):
                a, b = repeat(below[j], m), repeat(below[j + 1], m)
                other["cols"][m] = (other["cols"][m] - other_one * a) - other_two * b
            for n, block in enumerate(blocks):
                other["blocks"][n] = other["blocks"][n] - other_one * repeat(block, j)
            other["two"] = other_two
        for m in range(j + 2, PANEL):
            a, b = repeat(cols[j], m), repeat(cols[j + 1], m)
            cols[m] = (cols[m] - one * a) - two * b
        one = jnp.where(row_id > j, one, 0.0)
        two = jnp.where(row_id > j + 1, two, 0.0)
        for n in range(len(blocks)):
            blocks[n] = blocks[n] - one * repeat(blocks[n], j)
            row = repeat(blocks[n], j + 1)
            blocks[n] = blocks[n] - two * row
            for other in others:
                other["blocks"][n] = other["blocks"][n] - other["two"] * row
    return pivots, inverses


def orthonormal_rows(inner, wide):
    width = inner.shape[1]
    both = jnp.concatenate([inner, wide], axis=1)
    matrix = [both[PANEL * k : PANEL * (k + 1)] for k in range(RANK // PANEL)]
    rows = []
    for k in range(0, len(matrix), GROUP):
        group = [[part[:, :width], part[:, width:]] for part in matrix[k : k + GROUP]]
        cols = [spread(group[0][0], PANEL * k + j) for j in range(PANEL)]
        scaled = []
        for n, blocks in enumerate(group):
            at = PANEL * (k + n)
            others = []
            for later, other in enumerate(group[n + 1 :]):
                below = [spread(other[0], at + j) for j in range(PANEL)]
                ahead = [spread(other[0], at + PANEL + j) for j in range(PANEL)] if later == 0 else []
                others.append({"below": below, "cols": ahead, "blocks": other})
            pivots, inverses = eliminate(cols, blocks, others)
            rows.append(blocks[1] * lax.rsqrt(pivots))
            scaled.append(jnp.concatenate([block * inverses for block in blocks], axis=1))
            if others:
                cols = others[0]["cols"]
        if k + GROUP < len(matrix):
            update = outer_sum(
                jnp.concatenate([blocks[0] for blocks in group]), jnp.concatenate(scaled)
            )
            for m in range(k + GROUP, len(matrix)):
                matrix[m] = matrix[m] - update[PANEL * m : PANEL * (m + 1)]
    return jnp.concatenate(rows, axis=0)


def deep_left(value):
    high, middle, low = parts_of(value)
    return jnp.concatenate([high, high, high, middle, middle, low], axis=1).astype(jnp.bfloat16)


def deep_right(value, axis):
    high, middle, low = parts_of(value)
    return jnp.concatenate([high, middle, low, high, middle, high], axis=axis).astype(jnp.bfloat16)


def basis_kernel(total_ref, snap_ref, out_ref, *, rows_all):
    cols = total_ref.shape[1]
    row_id, col_id = ids((cols, cols))
    identity = jnp.where(row_id == col_id, jnp.float32(ridge), 0.0)
    gram_matrix = unfolded(total_ref[...]) / rows_all + identity

    gram_deep = deep_right(gram_matrix, 0)
    basis = gram_matrix[:RANK]
    for step in range(ITERS):
        if step > 0:
            basis = jnp.dot(deep_left(basis), gram_deep, preferred_element_type=jnp.float32)
        full = jnp.concatenate([basis, jnp.zeros((cols - RANK, cols), jnp.float32)], axis=0)
        inner = lax.dot_general(
            deep_left(basis),
            deep_right(full, 1),
            (((1,), (1,)), ((), ())),
            preferred_element_type=jnp.float32,
        )
        basis = orthonormal_rows(inner, basis)
    blocks = out_ref.shape[0] // RANK
    basis_deep = deep_left(basis)
    for block in range(0, blocks, 2):
        pair = [snap_ref[pl.ds(block + n, cols, stride=SLOT), :] for n in range(2)]
        modes = jnp.dot(
            basis_deep,
            deep_right(jnp.concatenate(pair, axis=1), 0),
            preferred_element_type=jnp.float32,
        )
        for n in range(2):
            out_ref[pl.ds(block + n, RANK, stride=blocks), :] = modes[:, LANES * n : LANES * (n + 1)]


def project(gram_total, snapshots, rows_all):
    return pl.pallas_call(
        functools.partial(basis_kernel, rows_all=rows_all),
        out_shape=jax.ShapeDtypeStruct((RANK * 12, LANES), jnp.float32),
        in_specs=[pl.BlockSpec(memory_space=pltpu.VMEM)] * 2,
        out_specs=pl.BlockSpec(memory_space=pltpu.VMEM),
        compiler_params=pltpu.CompilerParams(vmem_limit_bytes=16 * 2**20),
        name="basis",
    )(gram_total, snapshots)


def exact_dot(values, one_hot):
    high, middle, low = (part.astype(jnp.bfloat16) for part in parts_of(values))
    dot = functools.partial(jnp.dot, preferred_element_type=jnp.float32)
    return (dot(low, one_hot) + dot(middle, one_hot)) + dot(high, one_hot)


def sorting(size, to_sorted):
    cell = lax.broadcasted_iota(jnp.int32, (size, size), 0 if to_sorted else 1)
    spot = lax.broadcasted_iota(jnp.int32, (size, size), 1 if to_sorted else 0)
    place = (cell & 3) * (size // 4) + (cell >> 2)
    return jnp.where(place == spot, 1.0, 0.0).astype(jnp.bfloat16)


def edges_kernel(velocity_ref, coef_ref, low_ref, high_ref, arrived):
    layers, rows_z = low_ref.shape[2], coef_ref.shape[1]
    copies = []
    for n, (edge_ref, start) in enumerate(((low_ref, 0), (high_ref, rows_z - layers))):
        rows = pl.ds(start, layers)
        copies += [
            pltpu.make_async_copy(velocity_ref.at[:, :, rows], edge_ref.at[:3], arrived.at[2 * n]),
            pltpu.make_async_copy(coef_ref.at[:, rows], edge_ref.at[3], arrived.at[2 * n + 1]),
        ]
    for copy in copies:
        copy.start()
    for copy in copies:
        copy.wait()


def edges(velocity, smag_coef):
    rows_y, _, size_x = smag_coef.shape
    edge = jax.ShapeDtypeStruct((4, rows_y, 4, size_x), jnp.float32)
    return pl.pallas_call(
        edges_kernel,
        out_shape=(edge, edge),
        in_specs=[pl.BlockSpec(memory_space=pltpu.HBM)] * 2,
        out_specs=[pl.BlockSpec(memory_space=pltpu.VMEM)] * 2,
        scratch_shapes=[pltpu.SemaphoreType.DMA((4,))],
        compiler_params=pltpu.CompilerParams(vmem_limit_bytes=2 * 2**20),
        name="edges",
    )(*(pltpu.with_memory_space_constraint(a, pltpu.HBM) for a in (velocity, smag_coef)))


def pack_kernel(velocity_ref, coef_ref, block_ref, off_ref):
    odd = lax.axis_index("gy") % 2 == 1
    rows_y, rows_z, size_x = coef_ref.shape
    rows = [velocity_ref[c].reshape(-1, size_x) for c in range(3)] + [coef_ref[...].reshape(-1, size_x)]
    done = exact_dot(jnp.concatenate(rows), sorting(size_x, True))
    for c in range(4):
        for y in range(rows_y):
            start = (c * rows_y + y) * rows_z
            for o in range(4):
                plane = done[start : start + rows_z, LANES * o : LANES * (o + 1)]
                block_ref[c, y, o] = plane
                if c < 3:
                    off_ref[c * rows_y + y, o] = plane
                elif y < rows_y - 1:
                    above = done[start + rows_z : start + 2 * rows_z, LANES * o : LANES * (o + 1)]
                    off_ref[c * rows_y + y, o] = jnp.where(odd, above, plane)


def pack(velocity, smag_coef):
    rows_y, rows_z, _ = smag_coef.shape
    return pl.pallas_call(
        pack_kernel,
        out_shape=(
            jax.ShapeDtypeStruct((4, rows_y, 4, rows_z, LANES), jnp.float32),
            jax.ShapeDtypeStruct((4 * rows_y - 1, 4, rows_z, LANES), jnp.float32),
        ),
        in_specs=[pl.BlockSpec(memory_space=pltpu.VMEM)] * 2,
        out_specs=[pl.BlockSpec(memory_space=pltpu.VMEM)] * 2,
        compiler_params=pltpu.CompilerParams(vmem_limit_bytes=12 * 2**20),
        name="pack",
    )(velocity, smag_coef)


def sides_kernel(low_ref, high_ref, sides_ref, chip_ref, other_ref):
    odd = lax.axis_index("gy") % 2 == 1
    rows_y, layers, size_x = low_ref.shape[1:]
    rows = jnp.concatenate([high_ref[...], low_ref[...]], axis=2).reshape(-1, size_x)
    done = exact_dot(rows, sorting(size_x, True)).reshape(4, rows_y, 2 * layers, size_x)
    for c in range(4):
        for o in range(4):
            planes = [done[c, y, :, LANES * o : LANES * (o + 1)] for y in range(rows_y)]
            for y in range(rows_y):
                sides_ref[c, y, o] = planes[y]
            for away in range(rows_y - 1):
                upper, lower = planes[rows_y - 1 - away], planes[away]
                on_chip, off_chip = jnp.where(odd, lower, upper), jnp.where(odd, upper, lower)
                for ref, plane in ((chip_ref, on_chip), (other_ref, off_chip)):
                    if away == 0:
                        ref[c, 0, o] = plane
                    else:
                        for side, begin in enumerate((0, layers + 2)):
                            to = 4 * (away - 1) + 2 * side
                            ref[c, 1, o, to : to + 2] = plane[begin : begin + 2]


def sort_sides(low, high):
    _, rows_y, layers, _ = low.shape
    shape = lambda rows: jax.ShapeDtypeStruct((4, rows, 4, 2 * layers, LANES), jnp.float32)
    return pl.pallas_call(
        sides_kernel,
        out_shape=(shape(rows_y), shape(2), shape(2)),
        in_specs=[pl.BlockSpec(memory_space=pltpu.VMEM)] * 2,
        out_specs=[pl.BlockSpec(memory_space=pltpu.VMEM)] * 3,
        compiler_params=pltpu.CompilerParams(vmem_limit_bytes=12 * 2**20),
        cost_estimate=pl.CostEstimate(flops=2 * 10**10, bytes_accessed=10**6, transcendentals=0),
        name="sides",
    )(low, high)


def around_z(ref, index):
    return ref[(*index, slice(EDGE + 1, EDGE + 25))], ref[(*index, slice(EDGE - 1, EDGE + 23))]


def at(ref, *index):
    return ref[(*index, slice(EDGE, EDGE + 24))]


def put(ref, index, plane):
    ref[(*index, slice(EDGE, EDGE + 24))] = plane
    close(ref, index, plane)


def close(ref, index, plane):
    ref[(*index, slice(EDGE - 1, EDGE))] = plane[23:24]
    ref[(*index, slice(EDGE + 24, EDGE + 25))] = plane[:1]


def around_x(ref, index, o):
    ahead = at(ref, *index, o + 1) if o < 3 else pltpu.roll(at(ref, *index, 0), LANES - 1, 1)
    behind = at(ref, *index, o - 1) if o > 0 else pltpu.roll(at(ref, *index, 3), 1, 1)
    return ahead, behind


def half_viscosity(cells_ref, y, o, coefficient):
    jump = []
    for c in range(3):
        x_ahead, x_behind = around_x(cells_ref, (c, y), o)
        z_ahead, z_behind = around_z(cells_ref, (c, y, o))
        jump.append(
            (x_ahead - x_behind, at(cells_ref, c, y + 1, o) - at(cells_ref, c, y - 1, o), z_ahead - z_behind)
        )
    total = jump[0][0] ** 2 + jump[1][1] ** 2 + jump[2][2] ** 2
    total = total + total
    for c, d in ((0, 1), (0, 2), (1, 2)):
        total = total + (jump[c][d] + jump[d][c]) ** 2
    rate = coefficient * (0.5 * total * lax.rsqrt(jnp.maximum(total, 1e-37)))
    return (0.5 * nu_limit) * rate * recip(1.0 + rate)


def stepped(cells_ref, y, visc_ref, v, o):
    here = at(visc_ref, v, o)
    visc = [
        *around_x(visc_ref, (v,), o),
        at(visc_ref, v + 1, o),
        at(visc_ref, v - 1, o),
        *around_z(visc_ref, (v, o)),
    ]
    visc = [here + other for other in visc]
    result = []
    for c in range(3):
        centre = at(cells_ref, c, y, o)
        cells = [
            *around_x(cells_ref, (c, y), o),
            at(cells_ref, c, y + 1, o),
            at(cells_ref, c, y - 1, o),
            *around_z(cells_ref, (c, y, o)),
        ]
        change = visc[0] * (cells[0] - centre)
        for n in range(1, 6):
            change = change + visc[n] * (cells[n] - centre)
        result.append(centre + change)
    return result


def ids(shape):
    return lax.broadcasted_iota(jnp.int32, shape, 0), lax.broadcasted_iota(jnp.int32, shape, 1)


def folded(gram):
    half = gram.shape[0] // 2
    row, lane = ids((half, 2 * half))
    corner = pltpu.roll(gram[half:], half, 1)
    square = jnp.where(lane < row, corner, gram[:half])
    diagonal = jnp.sum(jnp.where(lane == row, corner, 0.0), axis=0, keepdims=True)
    return jnp.concatenate([square, jnp.broadcast_to(diagonal, (8, 2 * half))], axis=0)


def unfolded(parts):
    half = parts.shape[1] // 2
    row, lane = ids((half, 2 * half))
    square = parts[:half]
    upper = jnp.where(lane > row, square, 0.0)
    lower = pltpu.roll(jnp.where(lane < row, square, 0.0), half, 1)
    one_side = jnp.concatenate([upper, lower], axis=0)
    below = pltpu.roll(jnp.broadcast_to(parts[half : half + 1], square.shape), half, 1)
    diagonal = jnp.concatenate(
        [jnp.where(lane == row, square, 0.0), jnp.where(lane == row + half, below, 0.0)], axis=0
    )
    return one_side + one_side.T + diagonal


def steps_kernel(
    code_ref, block_ref, chip_ref, other_ref, sides_ref, side_chip_ref, side_other_ref,
    wide_ref, snap_ref, gram_ref,
    cells_ref, visc_ref, one_ref, two_ref, all_ref,
):
    _, rows_y, _, rows_z, _ = block_ref.shape
    cols = gram_ref.shape[1]
    place_y = lax.axis_index("gy")
    first, last, odd = place_y == 0, place_y == lax.axis_size("gy") - 1, place_y % 2 == 1

    def behind(chip, other):
        return jnp.where(first, 0.0, jnp.where(odd, chip, other))

    def ahead(chip, other):
        return jnp.where(last, 0.0, jnp.where(odd, other, chip))

    own_rows, layers = slice(EDGE, EDGE + rows_z), sides_ref.shape[3]
    side = slice(EDGE + rows_z, EDGE + rows_z + layers)
    for c in range(4):
        for y in range(rows_y):
            for o in range(4):
                own, below, above = (c, rows_y + y, o), (c, y, o), (c, 2 * rows_y + y, o)
                cells_ref[(*own, own_rows)] = block_ref[c, y, o]
                chip, plane = chip_ref[c, y, o], c * rows_y + y
                under, upper = (plane, plane) if c < 3 else (plane - min(y, 1), min(plane, 4 * rows_y - 2))
                cells_ref[(*below, own_rows)] = behind(chip, other_ref[under, o])
                cells_ref[(*above, own_rows)] = ahead(chip, other_ref[upper, o])
                cells_ref[(*own, side)] = sides_ref[c, y, o]
                for choose, place, away in ((behind, below, rows_y - 1 - y), (ahead, above, y)):
                    if away == 0:
                        halo = choose(side_chip_ref[c, 0, o], side_other_ref[c, 0, o])
                        cells_ref[(*place, side)] = halo
                    elif away <= rows_y - 2:
                        for n, begin in enumerate((rows_z, rows_z + layers - 2)):
                            part = (c, 1, o, slice(4 * (away - 1) + 2 * n, 4 * (away - 1) + 2 * n + 2))
                            halo = choose(side_chip_ref[part], side_other_ref[part])
                            cells_ref[(*place, slice(EDGE + begin, EDGE + begin + 2))] = halo
                if c < 3:
                    for place in (own, below, above):
                        close(cells_ref, place, at(cells_ref, *place))

    @pl.when(first)
    def _():
        for y in range(1, rows_y):
            cells_ref[3, y] = cells_ref[3, rows_y]

    @pl.when(last)
    def _():
        for y in range(rows_y - 1):
            cells_ref[3, 2 * rows_y + y] = cells_ref[3, 2 * rows_y - 1]

    def visc_one(y, carry):
        for o in range(4):
            put(visc_ref, (y, o), half_viscosity(cells_ref, y, o, at(cells_ref, 3, y, o)))
        return carry

    lax.fori_loop(1, 3 * rows_y - 1, visc_one, 0)

    def step_one(y, carry):
        outside = jnp.logical_or(
            jnp.logical_and(first, y < rows_y), jnp.logical_and(last, y >= 2 * rows_y)
        )
        for o in range(4):
            for c, cells in enumerate(stepped(cells_ref, y, visc_ref, y, o)):
                put(one_ref, (c, y, o), jnp.where(outside, 0.0, cells))
        return carry

    lax.fori_loop(2, 3 * rows_y - 2, step_one, 0)

    def visc_two(y, carry):
        for o in range(4):
            put(visc_ref, (y, o), half_viscosity(one_ref, y, o, at(cells_ref, 3, y, o)))
        return carry

    lax.fori_loop(rows_y - 1, 2 * rows_y + 1, visc_two, 0)

    for y in range(rows_y):
        for o in range(4):
            for c, cells in enumerate(stepped(one_ref, rows_y + y, visc_ref, rows_y + y, o)):
                two_ref[c, y, o] = cells[:rows_z]
                start = (c * rows_y + y) * rows_z
                wide_ref[start : start + rows_z, LANES * o : LANES * (o + 1)] = cells[:rows_z]
    states = ((block_ref, 0, 0), (one_ref, rows_y, EDGE), (two_ref, 0, 0))
    for state, (ref, shift, edge) in enumerate(states):
        for y in range(rows_y):
            for z in range(4):
                for o in range(4):
                    start = SLOT * (64 * state + 16 * y + 4 * z + o)
                    for c in range(3):
                        piece = ref[c, shift + y, o, pl.ds(edge + z, rows_z // 4, stride=4), :]
                        all_ref[start + 4 * c : start + 4 * c + 4, :] = piece

    def pick(column, carry):
        source = pl.multiple_of(code_ref[column] * SLOT, SLOT)
        target = pl.multiple_of(column * SLOT, SLOT)
        snap_ref[pl.ds(target, SLOT), :] = all_ref[pl.ds(source, SLOT), :]
        return carry

    lax.fori_loop(0, cols, pick, 0, unroll=16)
    even, odd = jnp.zeros((cols, cols), jnp.float32), jnp.zeros((cols, cols), jnp.float32)
    across = functools.partial(
        lax.dot_general,
        dimension_numbers=(((1,), (1,)), ((), ())),
        preferred_element_type=jnp.float32,
    )
    for block in range(0, 12, 2):
        part = jnp.concatenate(
            [snap_ref[pl.ds(block + i, cols, stride=SLOT), :] for i in range(2)], axis=1
        )
        high, middle, low = (p.astype(jnp.bfloat16) for p in parts_of(part))
        odd = odd + (across(high, low) + across(high, middle))
        even = even + (across(middle, middle) + across(high, high))
    gram_ref[...] = folded(even + (odd + odd.T))


def unsort_kernel(wide_ref, final_ref):
    final_ref[...] = exact_dot(wide_ref[...], sorting(wide_ref.shape[1], False)).reshape(final_ref.shape)


def unsort(wide, shape):
    return pl.pallas_call(
        unsort_kernel,
        out_shape=jax.ShapeDtypeStruct(shape, jnp.float32),
        in_specs=[pl.BlockSpec(memory_space=pltpu.VMEM)],
        out_specs=pl.BlockSpec(memory_space=pltpu.VMEM),
        compiler_params=pltpu.CompilerParams(vmem_limit_bytes=12 * 2**20),
        cost_estimate=pl.CostEstimate(flops=4 * 10**9, bytes_accessed=10**6, transcendentals=0),
        name="unsort",
    )(wide)


def both_steps(snap_code, block, *halo):
    _, rows_y, _, rows_z, _ = block.shape
    cols = snap_code.shape[0]
    f32 = lambda *shape: jax.ShapeDtypeStruct(shape, jnp.float32)
    scratch = lambda *shape: pltpu.VMEM(shape, jnp.float32)
    depth = EDGE + rows_z + 16
    return pl.pallas_call(
        steps_kernel,
        out_shape=(
            f32(3 * rows_y * rows_z, 4 * LANES),
            f32(SLOT * cols, LANES),
            f32(cols // 2 + 8, cols),
        ),
        in_specs=[pl.BlockSpec(memory_space=pltpu.SMEM)]
        + [pl.BlockSpec(memory_space=pltpu.VMEM)] * (1 + len(halo)),
        out_specs=[pl.BlockSpec(memory_space=pltpu.VMEM)] * 3,
        scratch_shapes=[
            scratch(4, 3 * rows_y, 4, depth, LANES),
            scratch(3 * rows_y, 4, depth, LANES),
            scratch(3, 3 * rows_y, 4, depth, LANES),
            scratch(3, rows_y, 4, rows_z, LANES),
            scratch(SLOT * 192, LANES),
        ],
        compiler_params=pltpu.CompilerParams(vmem_limit_bytes=32 * 2**20),
        name="steps",
    )(snap_code, block, *halo)


def device_sum(part):
    axes = ("gy", "gz")
    size_z, size_x = 8, lax.axis_size("gz")
    rounds = (
        [lambda x, y, z, core: (x, y, z, core ^ 1)],
        [lambda x, y, z, core, bits=bits: (x ^ bits, y, z, core) for bits in (1, 2, 3)],
        [lambda x, y, z, core, bits=bits: (x, y ^ bits, z, core) for bits in (1, 2, 3)],
        [lambda x, y, z, core, bits=bits: (x, y, z ^ bits, core) for bits in (1, 2, 3)],
        [lambda x, y, z, core: (x, y, size_z - 1 - z, core)],
    )

    def partner(move, device):
        row, x = divmod(device, size_x)
        x, y, z, core = move(x, row // (2 * size_z), row // 2 % size_z, row % 2)
        return ((y * size_z + z) * 2 + core) * size_x + x

    count = lax.axis_size("gy") * size_x
    for moves in rounds:
        others = [
            lax.ppermute(part, axes, [(device, partner(move, device)) for device in range(count)])
            for move in moves
        ]
        part = part + sum(others[1:], others[0])
    return part


def local(velocity, smag_coef, snap_code):
    count_y, count_z = lax.axis_size("gy"), lax.axis_size("gz")

    def along_z(part, step):
        return lax.ppermute(part, "gz", [(i, (i + step) % count_z) for i in range(count_z)])

    def on_chip(part):
        return lax.ppermute(part, "gy", [(i, i ^ 1) for i in range(count_y)])

    def off_chip(part):
        partners = [min(max(((i + 1) ^ 1) - 1, 0), count_y - 1) for i in range(count_y)]
        return lax.ppermute(part, "gy", list(enumerate(partners)))

    low, high = edges(velocity, smag_coef)
    velocity, smag_coef, low, high = lax.optimization_barrier((velocity, smag_coef, low, high))
    sides, side_chip, side_other = sort_sides(along_z(high, 1), along_z(low, -1))
    block, off = pack(velocity, smag_coef)
    wide, snapshots, gram = both_steps(
        snap_code, block, on_chip(block), off_chip(off), sides, on_chip(side_chip), off_chip(side_other)
    )
    rows_y, rows_z = velocity.shape[1], velocity.shape[2]
    rows_all = 12 * LANES * count_y * count_z
    pod_modes = project(device_sum(gram), snapshots, rows_all)
    return (unsort(wide, velocity.shape), pod_modes.reshape(RANK, 3, rows_y // 4, rows_z // 4, LANES))


def solution(mesh):
    placed = (P(None, "gy", "gz", None), P("gy", "gz", None), P())
    return jax.shard_map(
        local,
        mesh=mesh,
        in_specs=placed,
        out_specs=(P(None, "gy", "gz", None), P(None, None, "gy", "gz", None)),
        check_vma=False,
    )
```
